32 devices in a mesh: ctx: 8 (over z, x), head: 4 (over y, core).
Axes of the slice: x: 2, y: 2, z: 4, core: 2. Of those that a mesh axis runs over, the one named last changes fastest.
Arguments:
- states: bfloat16 [4096, 2048], P(('ctx', 'head')), may hold values from -6 to 6
- shared_kv: bfloat16 [4096, 2048], P(('ctx', 'head')), may hold values from -6 to 6
- norm_gain: float32 [2048], replicated, may hold values from 0.25 to 1.75
- kv_gain: float32 [2048], replicated, may hold values from 0.25 to 1.75
- ffn_gain: float32 [2048], replicated, may hold values from 0.25 to 1.75
- query_weight: bfloat16 [2048, 2048], P(('ctx', 'head')), may hold values from -0.125 to 0.125
- key_weight: bfloat16 [2048, 2048], P(('ctx', 'head')), may hold values from -0.125 to 0.125
- value_weight: bfloat16 [2048, 2048], P(('ctx', 'head')), may hold values from -0.125 to 0.125
- out_weight: bfloat16 [2048, 2048], P(('ctx', 'head')), may hold values from -2 to 2
- gate_weight: bfloat16 [2048, 5504], P(None, ('ctx', 'head')), may hold values from -0.125 to 0.125
- up_weight: bfloat16 [2048, 5504], P(None, ('ctx', 'head')), may hold values from -0.125 to 0.125
- down_weight: bfloat16 [5504, 2048], P(('ctx', 'head')), may hold values from -0.078125 to 0.078125
- span_order: int32 [16], replicated, may hold values from 0 to 15, each once
- grad_output: bfloat16 [4096, 2048], P(('ctx', 'head')), may hold values from -6 to 6
Outputs:
- output: bfloat16 [4096, 2048], P(('ctx', 'head'))
- grad_states: bfloat16 [4096, 2048], P(('ctx', 'head'))
- grad_shared: bfloat16 [4096, 2048], P(('ctx', 'head'))
- grad_norm_gain: float32 [2048], P(('ctx', 'head'))
- grad_kv_gain: float32 [2048], P(('ctx', 'head'))
- grad_ffn_gain: float32 [2048], P(('ctx', 'head'))
- grad_query: float32 [2048, 2048], P('ctx', 'head')
- grad_key: float32 [2048, 2048], P('ctx', 'head')
- grad_value: float32 [2048, 2048], P('ctx', 'head')
- grad_out: float32 [2048, 2048], P('head', 'ctx')
- grad_gate: float32 [2048, 5504], P(None, ('ctx', 'head'))
- grad_up: float32 [2048, 5504], P(None, ('ctx', 'head'))
- grad_down: float32 [5504, 2048], P(('ctx', 'head'))
The draws below stay inside these ranges and needn't reach their ends.
Inputs may be any that keep to these rules, and one draw needn't show every extreme that they name: A permutation: each number of 0 to 15 once; token rows r * 256 to r * 256 + 255 hold the positions from span_order[r] * 256 on.
All inputs are finite; a program needn't handle non-finite values.
Results may differ from the reference program's by a relative error of at most 0.02.
Values may be sent and summed in bfloat16 or wider, within the bound.
No kernel may reach another device: no remote copies, remote signals or barrier semaphores. Data moves between devices by JAX's collectives and lax.ppermute only.
A program may use at most 320 MiB of HBM per device.

```python
import math
import jax
import jax.numpy as jnp
from jax import lax

D = 2048
HEADS = 16
HD = 128
FF = 5504
TOKENS = 4096
SPANS = 16
SPAN = 256


def shard_levels(key, extent, split, smallest, largest):
    def one(axis_at, shards_of):
        steps = jax.random.uniform(jax.random.fold_in(jax.random.fold_in(key, 6), axis_at), (shards_of,), jnp.float32, smallest / len(split), largest / len(split))
        return jnp.repeat(jnp.exp(steps), extent[axis_at] // shards_of).reshape((-1,) + (1,) * (len(extent) - axis_at - 1))

    factor_of = one(*split[0])
    for cut in split[1:]:
        factor_of = factor_of * one(*cut)
    return factor_of


def normal_values(own_key, shape, spread, reach, pieces=(), held_as=jnp.bfloat16):
    values = spread * jax.random.normal(own_key, shape, jnp.float32)
    if pieces:
        values = values * shard_levels(own_key, shape, pieces, -0.22, 0.18)
    return jnp.clip(values, -reach, reach).astype(held_as)


def setup_inputs(seed: int = 0) -> dict:
    seeds = jax.random.split(jax.random.key(seed), 15)
    states = normal_values(seeds[0], (TOKENS, D), 1.0, 6.0, ((0, 32),))
    shared_kv = normal_values(seeds[1], (TOKENS, D), 1.0, 6.0, ((0, 32),))
    norm_gain = jnp.clip(1.0 + 0.15 * jax.random.normal(seeds[2], (D,), jnp.float32), 0.25, 1.75)
    kv_gain = jnp.clip(1.0 + 0.15 * jax.random.normal(seeds[3], (D,), jnp.float32), 0.25, 1.75)
    ffn_gain = jnp.clip(1.0 + 0.15 * jax.random.normal(seeds[4], (D,), jnp.float32), 0.25, 1.75)
    query_weight = normal_values(seeds[5], (D, D), D ** -0.5, 0.125, ((0, 32),))
    key_weight = normal_values(seeds[6], (D, D), D ** -0.5, 0.125, ((0, 32),))
    value_weight = normal_values(seeds[7], (D, D), D ** -0.5, 0.125, ((0, 32),))
    out_weight = normal_values(seeds[8], (D, D), (max(D // 256, 1)) ** -0.5, 2.0, ((0, 32),))
    gate_weight = normal_values(seeds[9], (D, FF), D ** -0.5, 0.125, ((1, 32),))
    up_weight = normal_values(seeds[10], (D, FF), D ** -0.5, 0.125, ((1, 32),))
    down_weight = normal_values(seeds[11], (FF, D), FF ** -0.5, 0.078125, ((0, 32),))
    span_order = jax.random.permutation(seeds[12], SPANS).astype(jnp.int32)
    grad_output = normal_values(seeds[13], (TOKENS, D), 1.0, 6.0, ((0, 32),))
    return dict(states=states, shared_kv=shared_kv, norm_gain=norm_gain, kv_gain=kv_gain, ffn_gain=ffn_gain, query_weight=query_weight, key_weight=key_weight, value_weight=value_weight, out_weight=out_weight, gate_weight=gate_weight, up_weight=up_weight, down_weight=down_weight, span_order=span_order, grad_output=grad_output)


EPSILON = 1e-06
MASKED = -1e+30

@jax.custom_vjp
def low(v):
    return lax.optimization_barrier(v.astype(jnp.bfloat16)).astype(jnp.float32)

@jax.custom_vjp
def low_back(v):
    return v

def low_keep(v):
    return (low(v), None)

def low_pass(kept, grad):
    return (grad,)

def back_keep(v):
    return (v, None)

def back_low(kept, grad):
    return (low(grad),)
low.defvjp(low_keep, low_pass)
low_back.defvjp(back_keep, back_low)

def matmul(left_side, right_side):
    return jnp.dot(left_side, right_side, preferred_element_type=jnp.float32, precision=lax.Precision.HIGHEST)

def rms_scale(values, gain_vec):
    factor = lax.rsqrt(lax.optimization_barrier(jnp.mean(values * values, axis=-1, keepdims=True)) + EPSILON)
    return values * factor * gain_vec

def attend(queries, keys, values, position):
    total_rows = queries.shape[0]
    block_rows = math.gcd(512, total_rows)
    score_scale = HD ** (-0.5)
    keys_split = keys.reshape(total_rows, HEADS, HD)
    values_split = values.reshape(total_rows, HEADS, HD)

    def one_block(inputs):
        query_rows, query_pos = inputs
        query_split = query_rows.reshape(block_rows, HEADS, HD)
        scores = jnp.einsum('qhd,khd->hqk', query_split, keys_split, precision=lax.Precision.HIGHEST) * score_scale
        scores = low_back(scores)
        visible = position[None, None, :] <= query_pos[None, :, None]
        scores = jnp.where(visible, scores, MASKED)
        weights = low(jax.nn.softmax(scores, axis=-1))
        mixed_heads = jnp.einsum('hqk,khd->qhd', weights, values_split, precision=lax.Precision.HIGHEST)
        return mixed_heads.reshape(block_rows, HEADS * HD)
    count_blocks = total_rows // block_rows
    blocks = lax.map(jax.checkpoint(one_block), (queries.reshape(count_blocks, block_rows, HEADS * HD), position.reshape(count_blocks, block_rows)))
    return blocks.reshape(total_rows, HEADS * HD)

def reference(states, shared_kv, norm_gain, kv_gain, ffn_gain, query_weight, key_weight, value_weight, out_weight, gate_weight, up_weight, down_weight, span_order, grad_output):
    row_ids = jnp.arange(TOKENS, dtype=jnp.int32)
    position = (span_order[row_ids // SPAN] * SPAN + row_ids % SPAN).astype(jnp.int32)

    def forward(state_rows, shared_rows, gain_attn, gain_shared, gain_ffn, weight_query, weight_key, weight_value, weight_out, weight_gate, weight_up, weight_down):
        normed = low(rms_scale(state_rows, gain_attn))
        shared_normed = low(rms_scale(shared_rows, gain_shared))
        queries = low_back(low(matmul(normed, weight_query)))
        keys = low_back(low(matmul(shared_normed, weight_key)))
        values = low_back(low(matmul(shared_normed, weight_value)))
        attended = low_back(low(attend(queries, keys, values, position)))
        residual = state_rows + low_back(matmul(attended, weight_out))
        normed_two = low(rms_scale(residual, gain_ffn))
        gate_act = low_back(matmul(normed_two, weight_gate))
        up_act = low_back(matmul(normed_two, weight_up))
        hidden = low(jax.nn.silu(gate_act) * up_act)
        return residual + low_back(matmul(hidden, weight_down))
    inputs = (states, shared_kv, norm_gain, kv_gain, ffn_gain, query_weight, key_weight, value_weight, out_weight, gate_weight, up_weight, down_weight)
    inputs = tuple((item.astype(jnp.float32) for item in inputs))
    result, pullback = jax.vjp(forward, *inputs)
    grads = pullback(grad_output.astype(jnp.float32))
    return (result.astype(jnp.bfloat16), grads[0].astype(jnp.bfloat16), grads[1].astype(jnp.bfloat16), grads[2], grads[3], grads[4], grads[5], grads[6], grads[7], grads[8], grads[9], grads[10], grads[11])
```

```python
import math

import jax
import jax.numpy as jnp
from jax import lax
from jax.experimental import pallas as pl
from jax.experimental.pallas import tpu as pltpu
from jax.sharding import Mesh, PartitionSpec as P

HD = 128
EPSILON = 1e-06
LOW = jnp.bfloat16
HIGH = jnp.float32
LOG2E = math.log2(math.e)
SCORE_SCALE = HD ** (-0.5)
ALL = ("z", "x", "y", "c")


def hop(values, axis, steps=1):
    size = lax.axis_size(axis)
    return lax.ppermute(values, axis, [(i, (i + steps) % size) for i in range(size)])


def gather_x_first(piece):
    pieces = []
    for step in range(lax.axis_size("x")):
        if step:
            piece = hop(piece, "x")
        pieces += [piece, hop(piece, "y")]
    return pieces


def gather_y_first(piece):
    other = hop(piece, "y")
    pieces = []
    for step in range(lax.axis_size("x")):
        if step:
            piece, other = hop(piece, "x"), hop(other, "x")
        pieces += [piece, other]
    return pieces


def add_low(first, second):
    return (first.astype(HIGH) + second.astype(HIGH)).astype(LOW)


def ring_sum(parts, axis):
    size = len(parts)
    total = parts[1 % size]
    for step in range(1, size):
        total = add_low(parts[(step + 1) % size], hop(total, axis))
    return total


def sum_y_first(parts):
    size = lax.axis_size("x")
    merged = [add_low(parts[2 * s], hop(parts[2 * s + 1], "y")) for s in range(size)]
    return ring_sum(merged, "x")


def sum_x_first(parts):
    size = lax.axis_size("x")
    near = ring_sum([parts[2 * s] for s in range(size)], "x")
    far = ring_sum([parts[2 * s + 1] for s in range(size)], "x")
    return add_low(near, hop(far, "y"))


def gather_rows(rows):
    blocks = []
    for step in range(lax.axis_size("z")):
        if step:
            rows = hop(rows, "z")
        blocks += [rows, hop(rows, "c")]
    return jnp.concatenate(blocks, axis=0)


def sum_rows(partial_of, rows_local):
    size = lax.axis_size("z")
    total = None
    for step in range(1, size + 1):
        block = partial_of(step % size)
        mine = block[:rows_local] + hop(block[rows_local:].astype(LOW), "c").astype(HIGH)
        if total is None:
            total = mine.astype(LOW)
        else:
            total = mine + hop(total, "z").astype(HIGH)
            if step < size:
                total = total.astype(LOW)
    return total


def normalize(values, gain_vec):
    factor = lax.rsqrt(jnp.mean(values * values, axis=-1, keepdims=True) + EPSILON)
    plain_rows = values * factor
    return (plain_rows, factor, plain_rows * gain_vec)


def norm_backward(grad_normed, plain_rows, factor, gain_vec):
    scaled = grad_normed * gain_vec
    gain_part = jnp.sum(grad_normed * plain_rows, axis=0)
    grad_input = factor * (
        scaled - plain_rows * jnp.mean(scaled * plain_rows, axis=-1, keepdims=True)
    )
    return (gain_part, grad_input)


def matmul(left_side, right_side):
    return jnp.dot(left_side, right_side, preferred_element_type=HIGH)


def matmul_right_t(left_side, right_side):
    return lax.dot_general(
        left_side, right_side, (((1,), (1,)), ((), ())), preferred_element_type=HIGH
    )


def matmul_left_t(left_side, right_side):
    return lax.dot_general(
        left_side, right_side, (((0,), (0,)), ((), ())), preferred_element_type=HIGH
    )


def pad_units(rows):
    extra = -rows.shape[0] % 16
    return jnp.pad(rows, ((0, extra), (0, 0)))


def split_units(count):
    return -(-count // 32) * 16


def diagonal_visible(core, span_rows, key_axis):
    half = span_rows // 2

    def place(axis):
        index = lax.broadcasted_iota(jnp.int32, (span_rows, span_rows), axis)
        flipped = jnp.where(index < half, index + half, index - half)
        return jnp.where(core == 0, index, flipped)

    return place(key_axis) <= place(1 - key_axis)


def forward_kernel(
    place_ref, rank_ref, core_ref, query_ref, key_ref, value_ref, mixed_ref, lse_ref, score_ref
):
    span_rows = query_ref.shape[0]
    heads = query_ref.shape[1] // HD
    rank = rank_ref[pl.program_id(1)]
    columns = [slice(h * HD, (h + 1) * HD) for h in range(heads)]

    def block_scores(step, h):
        start = pl.multiple_of(place_ref[step] * span_rows, span_rows)
        keys = key_ref[pl.ds(start, span_rows), columns[h]]
        return matmul_right_t(query_ref[:, columns[h]], keys) * (SCORE_SCALE * LOG2E)

    def fold(values, operation):
        folded = values[:, :HD]
        for at in range(HD, span_rows, HD):
            folded = operation(folded, values[:, at : at + HD])
        return folded

    def score_step(step, maxima):
        new = []
        for h in range(heads):
            scores = block_scores(step, h)
            score_ref[h, step] = scores
            new.append(jnp.maximum(maxima[h], fold(scores, jnp.maximum)))
        return tuple(new)

    start = tuple(jnp.full((span_rows, HD), -jnp.inf, HIGH) for _ in range(heads))
    maxima = lax.fori_loop(0, rank, score_step, start)
    visible = diagonal_visible(core_ref[0], span_rows, 1)
    tops = []
    for h in range(heads):
        scores = jnp.where(visible, block_scores(rank, h), -jnp.inf)
        score_ref[h, rank] = scores
        top = jnp.maximum(maxima[h], fold(scores, jnp.maximum))
        tops.append(jnp.max(top, axis=1, keepdims=True))

    def mix_step(step, running):
        new = []
        start = pl.multiple_of(place_ref[step] * span_rows, span_rows)
        for h in range(heads):
            total, mixed = running[h]
            weights = jnp.exp2(score_ref[h, step] - tops[h])
            values = value_ref[pl.ds(start, span_rows), columns[h]]
            new.append(
                (total + fold(weights, jnp.add), mixed + matmul(weights.astype(LOW), values))
            )
        return tuple(new)

    zero = jnp.zeros((span_rows, HD), HIGH)
    sums = lax.fori_loop(0, rank + 1, mix_step, tuple((zero, zero) for _ in range(heads)))
    for h in range(heads):
        total = jnp.sum(sums[h][0], axis=1, keepdims=True)
        mixed_ref[:, columns[h]] = (sums[h][1] / total).astype(LOW)
        lse = jnp.broadcast_to(tops[h] + jnp.log2(total), (span_rows, HD))
        lse_ref[h] = jnp.transpose(lse)[:8, :]


def backward_kernel(
    place_ref,
    rank_ref,
    core_ref,
    query_ref,
    grad_ref,
    mixed_ref,
    lse_ref,
    key_ref,
    value_ref,
    grad_query_ref,
    grad_key_ref,
    grad_value_ref,
    key_sum_ref,
    value_sum_ref,
):
    heads = query_ref.shape[1] // HD
    spans = query_ref.shape[0] // rank_ref.shape[0]
    span_rows = spans
    columns = [slice(h * HD, (h + 1) * HD) for h in range(heads)]
    key_sum_ref[...] = jnp.zeros_like(key_sum_ref)
    value_sum_ref[...] = jnp.zeros_like(value_sum_ref)

    def query_span(at, carry):
        first = pl.multiple_of(at * span_rows, span_rows)
        here = pl.ds(first, span_rows)
        rank = rank_ref[at]
        delta = []
        lse = []
        for h in range(heads):
            product = grad_ref[here, columns[h]].astype(HIGH) * mixed_ref[
                here, columns[h]
            ].astype(HIGH)
            delta.append(jnp.sum(jnp.transpose(product), axis=0, keepdims=True))
            lse.append(lse_ref[h, :1, here])

        def block(step, grad_query, visible):
            start = pl.multiple_of(place_ref[step] * span_rows, span_rows)
            there = pl.ds(start, span_rows)
            new = []
            for h in range(heads):
                query = query_ref[here, columns[h]]
                grad = grad_ref[here, columns[h]]
                keys = key_ref[there, columns[h]]
                values = value_ref[there, columns[h]]
                scores = matmul_right_t(keys, query) * (SCORE_SCALE * LOG2E)
                weights = jnp.exp2(scores - lse[h])
                if visible is not None:
                    weights = jnp.where(visible, weights, 0.0)
                grad_weights = matmul_right_t(values, grad)
                grad_scores = (weights * (grad_weights - delta[h])).astype(LOW)
                value_sum_ref[there, columns[h]] += matmul(weights.astype(LOW), grad)
                key_sum_ref[there, columns[h]] += matmul(grad_scores, query)
                new.append(grad_query[h] + matmul_left_t(grad_scores, keys))
            return tuple(new)

        start = tuple(jnp.zeros((span_rows, HD), HIGH) for _ in range(heads))
        grad_query = lax.fori_loop(0, rank, lambda s, g: block(s, g, None), start)
        visible = diagonal_visible(core_ref[0], span_rows, 0)
        grad_query = block(rank, grad_query, visible)
        for h in range(heads):
            grad_query_ref[here, columns[h]] = (grad_query[h] * SCORE_SCALE).astype(LOW)
        return carry

    lax.fori_loop(0, rank_ref.shape[0], query_span, 0)
    grad_key_ref[...] = (key_sum_ref[...] * SCORE_SCALE).astype(LOW)
    grad_value_ref[...] = value_sum_ref[...].astype(LOW)


def heads_at_once(key_rows, features):
    return features // HD if key_rows <= 4096 else 1


def attention_forward(scalars, queries, keys, values):
    rows, features = queries.shape
    key_rows = keys.shape[0]
    own_spans = scalars[1].shape[0]
    span_rows = rows // own_spans
    heads = heads_at_once(key_rows, features)
    width = heads * HD
    pairs = rows * key_rows * features
    return pl.pallas_call(
        forward_kernel,
        out_shape=(
            jax.ShapeDtypeStruct((rows, features), LOW),
            jax.ShapeDtypeStruct((features // HD, 8, rows), HIGH),
        ),
        grid_spec=pltpu.PrefetchScalarGridSpec(
            num_scalar_prefetch=3,
            grid=(features // width, own_spans),
            in_specs=[
                pl.BlockSpec((span_rows, width), lambda h, i, *_: (i, h)),
                pl.BlockSpec((key_rows, width), lambda h, i, *_: (0, h)),
                pl.BlockSpec((key_rows, width), lambda h, i, *_: (0, h)),
            ],
            out_specs=[
                pl.BlockSpec((span_rows, width), lambda h, i, *_: (i, h)),
                pl.BlockSpec((heads, 8, span_rows), lambda h, i, *_: (h, 0, i)),
            ],
            scratch_shapes=[
                pltpu.VMEM((heads, key_rows // span_rows, span_rows, span_rows), HIGH)
            ],
        ),
        compiler_params=pltpu.CompilerParams(vmem_limit_bytes=56 * 2**20),
        cost_estimate=pl.CostEstimate(
            flops=2 * pairs, bytes_accessed=4 * key_rows * features, transcendentals=pairs // 256
        ),
        name="attention_forward",
    )(*scalars, queries, keys, values)


def attention_backward(scalars, queries, grads, mixed, lse, keys, values):
    rows, features = queries.shape
    key_rows = keys.shape[0]
    heads = heads_at_once(key_rows, features)
    width = heads * HD
    pairs = rows * key_rows * features
    own = pl.BlockSpec((rows, width), lambda h, *_: (0, h))
    other = pl.BlockSpec((key_rows, width), lambda h, *_: (0, h))
    return pl.pallas_call(
        backward_kernel,
        out_shape=(
            jax.ShapeDtypeStruct((rows, features), LOW),
            jax.ShapeDtypeStruct((key_rows, features), LOW),
            jax.ShapeDtypeStruct((key_rows, features), LOW),
        ),
        grid_spec=pltpu.PrefetchScalarGridSpec(
            num_scalar_prefetch=3,
            grid=(features // width,),
            in_specs=[
                own,
                own,
                own,
                pl.BlockSpec((heads, 8, rows), lambda h, *_: (h, 0, 0)),
                other,
                other,
            ],
            out_specs=[own, other, other],
            scratch_shapes=[pltpu.VMEM((key_rows, width), HIGH)] * 2,
        ),
        compiler_params=pltpu.CompilerParams(vmem_limit_bytes=56 * 2**20),
        cost_estimate=pl.CostEstimate(
            flops=5 * pairs, bytes_accessed=8 * key_rows * features, transcendentals=pairs // 256
        ),
        name="attention_backward",
    )(*scalars, queries, grads, mixed, lse, keys, values)


def per_device(
    states,
    shared_kv,
    norm_gain,
    kv_gain,
    ffn_gain,
    query_weight,
    key_weight,
    value_weight,
    out_weight,
    gate_weight,
    up_weight,
    down_weight,
    span_order,
    grad_output,
):
    z, x, y, c = (lax.axis_index(name) for name in ALL)
    size_x = lax.axis_size("x")
    sides = 2 * size_x
    rows_local, width_model = states.shape
    weight_rows = query_weight.shape[0]
    units_local = gate_weight.shape[1]
    own_width = width_model // 8

    side = jnp.arange(sides, dtype=jnp.int32)
    side_owner = jnp.mod(x - side // 2, size_x) * 2 + jnp.bitwise_xor(y, side % 2)
    back = jnp.arange(4, dtype=jnp.int32)
    back_owner = jnp.mod(z - back, 4)

    def own_columns(weights):
        count = weights.shape[0]
        pair = 2 * own_width
        blocks = []
        for step in range(4):
            start = jnp.mod(z + step, 4) * pair
            block = lax.dynamic_slice_in_dim(weights, start, pair, 2)
            if step:
                block = hop(block, "z", step)
            keep = lax.dynamic_slice_in_dim(block, c * own_width, own_width, 2)
            give = lax.dynamic_slice_in_dim(block, (1 - c) * own_width, own_width, 2)
            blocks += [keep, hop(give, "c")]
        return [jnp.stack([b[i] for b in blocks]) for i in range(count)]

    spot = jnp.arange(8 * sides, dtype=jnp.int32)
    spot_z, spot_x, spot_y, spot_c = (
        spot // (4 * size_x),
        (spot // 4) % size_x,
        (spot // 2) % 2,
        spot % 2,
    )
    row_order = (
        (jnp.mod(x - spot_x, size_x) * 2 + jnp.bitwise_xor(y, spot_y)) * 4 + jnp.mod(z - spot_z, 4)
    ) * 2 + jnp.bitwise_xor(c, spot_c)

    def all_rows(pieces):
        stacked = jnp.concatenate(pieces, axis=0)
        return jnp.take(stacked, row_order, axis=0).reshape(width_model, own_width)

    state_rows = states.astype(HIGH)
    shared_rows = shared_kv.astype(HIGH)
    plain_kv, factor_kv, normed_kv = normalize(shared_rows, kv_gain)
    plain_one, factor_one, normed_one = normalize(state_rows, norm_gain)
    normed_low = normed_one.astype(LOW)
    shared_low = normed_kv.astype(LOW)

    key_slice, value_slice = own_columns(jnp.stack([key_weight, value_weight]))
    group_shared = gather_rows(shared_low)
    weight_key = all_rows(gather_x_first(key_slice))
    weight_value = all_rows(gather_y_first(value_slice))
    (query_slice,) = own_columns(query_weight[None])
    weight_query = all_rows(gather_x_first(query_slice))
    out_pieces = jnp.take(
        jnp.stack(gather_y_first(out_weight)), jnp.argsort(side_owner), axis=0
    ).reshape(2, size_x // 2, 2, weight_rows, width_model)
    out_keep = lax.dynamic_index_in_dim(out_pieces, c, 0, keepdims=False)
    out_got = hop(lax.dynamic_index_in_dim(out_pieces, 1 - c, 0, keepdims=False), "c")
    weight_out = jnp.where(
        c == 0, jnp.stack([out_keep, out_got], axis=2), jnp.stack([out_got, out_keep], axis=2)
    ).reshape(own_width, width_model)

    keys_own = matmul(group_shared, weight_key).astype(LOW)
    values_own = matmul(group_shared, weight_value).astype(LOW)
    keys_all = jnp.concatenate(gather_x_first(keys_own), axis=0)
    values_all = jnp.concatenate(gather_y_first(values_own), axis=0)
    group_normed = gather_rows(normed_low)
    queries = matmul(group_normed, weight_query).astype(LOW)

    span_of = (back_owner[None, :] * sides + side_owner[:, None]).reshape(-1)
    ranks = jnp.take(span_order, span_of)
    spans = span_order.shape[0]
    listed = jnp.arange(spans, dtype=jnp.int32)
    place = jnp.sum(jnp.where(ranks[None, :] == listed[:, None], listed[None, :], 0), axis=1)
    scalars = (place, ranks[:4], c.reshape(1).astype(jnp.int32))

    mixed, lse = attention_forward(scalars, queries, keys_all, values_all)

    gate_rows = pad_units(jnp.transpose(gate_weight))
    up_rows = pad_units(jnp.transpose(up_weight))
    down_rows = pad_units(down_weight)
    cut = split_units(gate_rows.shape[0])
    weight_gate = jnp.concatenate(gather_x_first(gate_rows), axis=0)
    weight_up = jnp.concatenate(gather_y_first(up_rows), axis=0)
    down_first = gather_x_first(down_rows[:cut])
    down_second = gather_y_first(down_rows[cut:])
    weight_down = jnp.concatenate(
        [part for pair in zip(down_first, down_second) for part in pair], axis=0
    )
    group_grad = gather_rows(grad_output)

    pair_rows = 2 * rows_local

    def rows_of(values, r):
        return values[r * pair_rows : (r + 1) * pair_rows]

    residual = state_rows + sum_rows(
        lambda r: matmul(rows_of(mixed, r), weight_out), rows_local
    )
    plain_two, factor_two, normed_two = normalize(residual, ffn_gain)
    group_in = gather_rows(normed_two.astype(LOW))

    gate_act = matmul_right_t(group_in, weight_gate)
    up_act = matmul_right_t(group_in, weight_up)
    grad_hidden = matmul_right_t(group_grad, weight_down)
    sigmoid = jax.nn.sigmoid(gate_act)
    silu_act = gate_act * sigmoid
    hidden = (silu_act * up_act).astype(LOW)
    grad_gate_act = (
        grad_hidden * up_act * sigmoid * (1.0 + gate_act * (1.0 - sigmoid))
    ).astype(LOW)
    grad_up_act = (grad_hidden * silu_act).astype(LOW)
    grad_ffn = sum_rows(
        lambda r: matmul(rows_of(grad_gate_act, r), weight_gate)
        + matmul(rows_of(grad_up_act, r), weight_up),
        rows_local,
    )
    branch = sum_rows(lambda r: matmul(rows_of(hidden, r), weight_down), rows_local)
    output = (residual + branch).astype(LOW)

    def unit_parts(values):
        step = values.shape[0] // sides
        return [values[s * step : (s + 1) * step] for s in range(sides)]

    gate_parts = unit_parts(matmul_left_t(grad_gate_act, group_in).astype(LOW))
    up_parts = unit_parts(matmul_left_t(grad_up_act, group_in).astype(LOW))
    down_parts = unit_parts(matmul_left_t(hidden, group_grad).astype(LOW))
    grad_gate = jnp.transpose(sum_y_first(gate_parts)[:units_local].astype(HIGH))
    grad_up = jnp.transpose(sum_x_first(up_parts)[:units_local].astype(HIGH))
    grad_down = jnp.concatenate(
        [sum_y_first([p[:cut] for p in down_parts]), sum_x_first([p[cut:] for p in down_parts])],
        axis=0,
    )[:units_local].astype(HIGH)

    gain_two, grad_norm_two = norm_backward(grad_ffn, plain_two, factor_two, ffn_gain)
    grad_residual = grad_output.astype(HIGH) + grad_norm_two
    group_branch = gather_rows(grad_residual.astype(LOW))
    grad_mixed = matmul_right_t(group_branch, weight_out).astype(LOW)

    grad_queries, key_terms, value_terms = attention_backward(
        scalars, queries, grad_mixed, mixed, lse, keys_all, values_all
    )
    grad_keys = sum_y_first(unit_parts(key_terms))
    grad_values = sum_x_first(unit_parts(value_terms))
    grad_normed = sum_rows(
        lambda r: matmul_right_t(rows_of(grad_queries, r), weight_query), rows_local
    )
    grad_shared_normed = sum_rows(
        lambda r: matmul_right_t(rows_of(grad_keys, r), weight_key)
        + matmul_right_t(rows_of(grad_values, r), weight_value),
        rows_local,
    )
    gain_one, grad_in_one = norm_backward(grad_normed, plain_one, factor_one, norm_gain)
    gain_kv, grad_in_kv = norm_backward(grad_shared_normed, plain_kv, factor_kv, kv_gain)
    grad_states = (grad_residual + grad_in_one).astype(LOW)
    grad_shared = grad_in_kv.astype(LOW)

    def side_parts(values):
        chunks = values.reshape(sides, -1, values.shape[1])
        return [
            lax.dynamic_index_in_dim(chunks, side_owner[s], 0, keepdims=False)
            for s in range(sides)
        ]

    to_layout = [
        [
            (
                ((za * size_x + xa) * 2 + ya) * 2 + ca,
                (4 * xa + 2 * ya + (ca ^ flip)) * 4 + za,
            )
            for za in range(4)
            for xa in range(size_x)
            for ya in range(2)
            for ca in range(2)
        ]
        for flip in range(2)
    ]

    def layout(summed):
        halves = summed.reshape(2, -1, summed.shape[1])
        got = []
        for flip in range(2):
            send = lax.dynamic_index_in_dim(
                halves, jnp.bitwise_xor(c, flip), 0, keepdims=False
            )
            got.append(lax.ppermute(send, ALL, to_layout[flip]))
        even = x % 2 == 0
        first = jnp.where(even, got[0], got[1])
        second = jnp.where(even, got[1], got[0])
        return jnp.concatenate([first, second], axis=1).astype(HIGH)

    grad_out = jnp.transpose(
        layout(sum_x_first(side_parts(matmul_left_t(group_branch, mixed).astype(LOW))))
    )
    grad_query = layout(
        sum_y_first(side_parts(matmul_left_t(group_normed, grad_queries).astype(LOW)))
    )
    grad_key = layout(
        sum_y_first(side_parts(matmul_left_t(group_shared, grad_keys).astype(LOW)))
    )
    grad_value = layout(
        sum_x_first(side_parts(matmul_left_t(group_shared, grad_values).astype(LOW)))
    )

    gain_stack = jnp.stack([gain_one, gain_kv, gain_two])
    gain_sums = lax.psum_scatter(gain_stack, ALL, scatter_dimension=1, tiled=True)
    return (
        output,
        grad_states,
        grad_shared,
        gain_sums[0],
        gain_sums[1],
        gain_sums[2],
        grad_query,
        grad_key,
        grad_value,
        grad_out,
        grad_gate,
        grad_up,
        grad_down,
    )


def solution(mesh):
    size_ctx, size_head = mesh.shape["ctx"], mesh.shape["head"]
    fine = Mesh(mesh.devices.reshape(4, size_ctx // 4, 2, size_head // 2), ALL)
    rows = P(ALL, None)
    ctx, head = ("z", "x"), ("y", "c")
    in_specs = (
        rows,
        rows,
        P(),
        P(),
        P(),
        rows,
        rows,
        rows,
        rows,
        P(None, ALL),
        P(None, ALL),
        rows,
        P(),
        rows,
    )
    out_specs = (
        rows,
        rows,
        rows,
        P(ALL),
        P(ALL),
        P(ALL),
        P(ctx, head),
        P(ctx, head),
        P(ctx, head),
        P(head, ctx),
        P(None, ALL),
        P(None, ALL),
        rows,
    )
    return jax.shard_map(
        per_device, mesh=fine, in_specs=in_specs, out_specs=out_specs, check_vma=False
    )
```

```python
import math

import jax
import jax.numpy as jnp
from jax import lax
from jax.experimental import pallas as pl
from jax.experimental.pallas import tpu as pltpu
from jax.sharding import Mesh, PartitionSpec as P

HD = 128
EPSILON = 1e-06
LOW = jnp.bfloat16
HIGH = jnp.float32
LOG2E = math.log2(math.e)
SCORE_SCALE = HD ** (-0.5)
ALL = ("z", "x", "y", "c")


def add_low(first, second):
    return (first.astype(HIGH) + second.astype(HIGH)).astype(LOW)


def after(values, *earlier):
    return lax.optimization_barrier((values, earlier))[0]


def hop(values, axis, steps=1):
    size = lax.axis_size(axis)
    return lax.ppermute(values, axis, [(i, (i + steps) % size) for i in range(size)])


def gather_task(first, second):
    size = lax.axis_size("x")
    firsts, seconds, first_over, second_over = [first], [second], [], []
    for stage in range(size):
        wanted = [("y", firsts[stage], first_over)]
        if stage == 0:
            wanted.append(("y", second, second_over))
        if stage < size - 1:
            wanted += [("x", firsts[stage], firsts), ("x", seconds[stage], seconds)]
        if stage:
            wanted.append(("x", second_over[stage - 1], second_over))
        yield wanted
    return (
        [piece for pair in zip(firsts, first_over) for piece in pair],
        [piece for pair in zip(seconds, second_over) for piece in pair],
    )


def sum_task(first, second):
    size = lax.axis_size("x")
    got, far, near = [], [], []
    over = [[] for _ in range(size)]
    far_total, near_total = second[3], second[2]
    for step in range(1, size):
        wanted = [("x", far_total, far), ("x", near_total, near)]
        if step == 1:
            wanted += [("y", first[2 * s + 1], over[s]) for s in range(1, size)]
            wanted.append(("y", first[1], over[0]))
        yield wanted
        at = 2 * ((step + 1) % size)
        far_total, near_total = add_low(second[at + 1], far[-1]), add_low(second[at], near[-1])
    merged = [add_low(first[2 * s], over[s][0]) for s in range(size)]
    total = merged[1]
    for step in range(1, size):
        wanted = [("x", total, got)]
        if step == 1:
            wanted.append(("y", far_total, far))
        yield wanted
        total = add_low(merged[(step + 1) % size], got[-1])
    return total, add_low(near_total, far[-1])


class Ticks:
    BYTES = 9 * 2**16

    def __init__(self):
        self.tasks = []
        self.over_z = ()
        self.sides = [(), ()]
        self.sent = None

    def add(self, task):
        entry = {"task": task, "wanted": None, "open": 0, "result": None}
        self.tasks.append(entry)
        self.advance(entry)
        return entry

    def advance(self, entry):
        try:
            entry["wanted"] = list(next(entry["task"]))
            entry["open"] = len(entry["wanted"])
        except StopIteration as stop:
            entry["result"] = stop.value
            self.tasks.remove(entry)

    def tick(self, *moves, room=1):
        got = []
        for values, steps in moves:
            self.sent = after(values, self.over_z, self.sides[-2])
            got.append(hop(self.sent, "z", steps))
        left = {"x": room * self.BYTES, "y": room * self.BYTES}
        arrived = []
        finished = []
        for entry in self.tasks:
            later = []
            for axis, values, into in entry["wanted"]:
                if left[axis] >= min(values.nbytes, self.BYTES):
                    left[axis] -= values.nbytes
                    into.append(hop(after(values, self.sides[-1]), axis))
                    arrived.append(into[-1])
                    entry["open"] -= 1
                else:
                    later.append((axis, values, into))
            entry["wanted"] = later
            if not entry["open"]:
                finished.append(entry)
        self.over_z = tuple(got) or self.over_z
        self.sides = self.sides[-1:] + [tuple(arrived)]
        for entry in finished:
            self.advance(entry)
        return got

    def finish(self, *entries):
        while any(entry["result"] is None for entry in entries):
            self.tick()
        return [entry["result"] for entry in entries]

    def gather_rows(self, rows):
        blocks = [rows]
        for _ in range(1, lax.axis_size("z")):
            blocks += self.tick((blocks[-1], 1))
        return self.both_cores(blocks)

    def both_cores(self, blocks):
        blocks = blocks[1:] + blocks[:1]
        return jnp.concatenate(blocks + [hop(block, "c") for block in blocks], axis=0)


class RowSum:
    def __init__(self, ticks, terms_of, inputs, rows_local):
        self.ticks = ticks
        self.rows = rows_local
        self.half = inputs[0].shape[0] // 2
        self.terms_of = terms_of
        self.inputs = inputs
        self.count = 0
        self.total = self.terms(inputs, 0, 1)[0].astype(LOW)

    def terms(self, inputs, start, stop):
        start, stop = start * self.rows, stop * self.rows
        far = self.terms_of(*(v[self.half + start : self.half + stop] for v in inputs))
        near = self.terms_of(*(v[start:stop] for v in inputs))
        got = hop(far.astype(LOW), "c").astype(HIGH)
        return [
            near[at : at + self.rows] + got[at : at + self.rows]
            for at in range(0, stop - start, self.rows)
        ]

    def step(self):
        (got,) = self.ticks.tick((self.total, 1))
        self.sent = self.ticks.sent
        if not self.count:
            inputs = after(tuple(self.inputs), self.sent)
            self.rest = self.terms(inputs, 1, lax.axis_size("z"))
        self.total = self.rest[self.count] + got.astype(HIGH)
        self.count += 1
        if self.count < len(self.rest):
            self.total = self.total.astype(LOW)
        return got

    def finish(self):
        while self.count < 3:
            self.step()
        return self.total


def place_blocks(pieces, places, widths):
    count, rows, width = pieces[0].shape
    total = len(pieces) * count

    def kernel(place_ref, *refs):
        ins, outs = refs[: len(pieces)], refs[len(pieces) :]
        for at in range(total):
            start = 0
            for out, size in zip(outs, widths):
                out[place_ref[at]] = ins[at // count][at % count, :, start : start + size]
                start += size

    shapes = [(total, rows, size) for size in widths]
    placed = pl.pallas_call(
        kernel,
        out_shape=[jax.ShapeDtypeStruct(shape, pieces[0].dtype) for shape in shapes],
        grid_spec=pltpu.PrefetchScalarGridSpec(
            num_scalar_prefetch=1,
            grid=(1,),
            in_specs=[pl.BlockSpec((count, rows, width), lambda i, *_: (0, 0, 0))] * len(pieces),
            out_specs=[pl.BlockSpec(shape, lambda i, *_: (0, 0, 0)) for shape in shapes],
        ),
        compiler_params=pltpu.CompilerParams(vmem_limit_bytes=48 * 2**20),
        cost_estimate=pl.CostEstimate(
            flops=0, bytes_accessed=4 * total * rows * width, transcendentals=0
        ),
        name="place_blocks",
    )(places, *pieces)
    return [out.reshape(total * rows, -1) for out in placed]


def normalize(values, gain_vec):
    factor = lax.rsqrt(jnp.mean(values * values, axis=-1, keepdims=True) + EPSILON)
    plain_rows = values * factor
    return (plain_rows, factor, plain_rows * gain_vec)


def norm_backward(grad_normed, plain_rows, factor, gain_vec):
    scaled = grad_normed * gain_vec
    gain_part = jnp.sum(grad_normed * plain_rows, axis=0)
    grad_input = factor * (
        scaled - plain_rows * jnp.mean(scaled * plain_rows, axis=-1, keepdims=True)
    )
    return (gain_part, grad_input)


def matmul(left_side, right_side):
    return jnp.dot(left_side, right_side, preferred_element_type=HIGH)


def matmul_right_t(left_side, right_side):
    return lax.dot_general(
        left_side, right_side, (((1,), (1,)), ((), ())), preferred_element_type=HIGH
    )


def matmul_left_t(left_side, right_side):
    return lax.dot_general(
        left_side, right_side, (((0,), (0,)), ((), ())), preferred_element_type=HIGH
    )


def pad_units(rows):
    extra = -rows.shape[0] % 16
    return jnp.pad(rows, ((0, extra), (0, 0)))


def quarters(count):
    tiles = count // 16
    return [16 * (tiles * i // 4) for i in range(5)]


def diagonal_visible(core, span_rows, key_axis):
    half = span_rows // 2

    def place(axis):
        index = lax.broadcasted_iota(jnp.int32, (span_rows, span_rows), axis)
        flipped = jnp.where(index < half, index + half, index - half)
        return jnp.where(core == 0, index, flipped)

    return place(key_axis) <= place(1 - key_axis)


def forward_kernel(
    place_ref, rank_ref, core_ref, query_ref, key_ref, value_ref, mixed_ref, lse_ref, score_ref
):
    half_rows = query_ref.shape[1]
    span_rows = 2 * half_rows
    heads = query_ref.shape[2] // HD
    rank = rank_ref[pl.program_id(1)]
    columns = [slice(h * HD, (h + 1) * HD) for h in range(heads)]

    def span(ref, step, h):
        side = place_ref[step] // 4
        start = pl.multiple_of((place_ref[step] % 4) * half_rows, half_rows)
        return ref[side, :, pl.ds(start, half_rows), columns[h]].reshape(span_rows, HD)

    def block_scores(step, h):
        query = query_ref[:, :, columns[h]].reshape(span_rows, HD)
        return matmul_right_t(query, span(key_ref, step, h)) * (SCORE_SCALE * LOG2E)

    def fold(values, operation):
        folded = values[:, :HD]
        for at in range(HD, span_rows, HD):
            folded = operation(folded, values[:, at : at + HD])
        return folded

    def score_step(step, maxima, count):
        new = []
        for h in range(heads):
            top = maxima[h]
            for at in range(count):
                scores = block_scores(step + at, h)
                score_ref[h, step + at] = scores
                top = jnp.maximum(top, fold(scores, jnp.maximum))
            new.append(top)
        return tuple(new)

    maxima = tuple(jnp.full((span_rows, HD), -jnp.inf, HIGH) for _ in range(heads))
    maxima = lax.fori_loop(0, rank // 2, lambda p, m: score_step(2 * p, m, 2), maxima)
    maxima = lax.fori_loop(rank // 2 * 2, rank, lambda p, m: score_step(p, m, 1), maxima)
    visible = diagonal_visible(core_ref[0], span_rows, 1)
    tops = []
    for h in range(heads):
        scores = jnp.where(visible, block_scores(rank, h), -jnp.inf)
        score_ref[h, rank] = scores
        top = jnp.maximum(maxima[h], fold(scores, jnp.maximum))
        tops.append(jnp.max(top, axis=1, keepdims=True))

    def mix_step(step, running, count):
        new = []
        for h in range(heads):
            total, mixed = running[h]
            for at in range(count):
                weights = jnp.exp2(score_ref[h, step + at] - tops[h])
                total = total + fold(weights, jnp.add)
                mixed = mixed + matmul(weights.astype(LOW), span(value_ref, step + at, h))
            new.append((total, mixed))
        return tuple(new)

    zero = jnp.zeros((span_rows, HD), HIGH)
    sums = tuple((zero, zero) for _ in range(heads))
    blocks = rank + 1
    sums = lax.fori_loop(0, blocks // 2, lambda p, r: mix_step(2 * p, r, 2), sums)
    sums = lax.fori_loop(blocks // 2 * 2, blocks, lambda p, r: mix_step(p, r, 1), sums)
    for h in range(heads):
        total = jnp.sum(sums[h][0], axis=1, keepdims=True)
        mixed = (sums[h][1] / total).astype(LOW)
        mixed_ref[:, :, columns[h]] = mixed.reshape(2, half_rows, HD)
        lse = jnp.broadcast_to(tops[h] + jnp.log2(total), (span_rows, HD))
        lse_ref[h] = jnp.transpose(lse)[:8, :]


def backward_kernel(
    place_ref,
    rank_ref,
    core_ref,
    query_ref,
    grad_ref,
    mixed_ref,
    lse_ref,
    key_ref,
    value_ref,
    grad_query_ref,
    grad_key_ref,
    grad_value_ref,
    key_sum_ref,
    value_sum_ref,
):
    heads = query_ref.shape[2] // HD
    half_rows = query_ref.shape[1] // rank_ref.shape[0]
    span_rows = 2 * half_rows
    columns = [slice(h * HD, (h + 1) * HD) for h in range(heads)]
    key_sum_ref[...] = jnp.zeros_like(key_sum_ref)
    value_sum_ref[...] = jnp.zeros_like(value_sum_ref)

    def query_span(at, carry):
        here = pl.ds(pl.multiple_of(at * half_rows, half_rows), half_rows)
        lanes = pl.ds(pl.multiple_of(at * span_rows, span_rows), span_rows)
        rank = rank_ref[at]

        def own(ref, h):
            return ref[:, here, columns[h]].reshape(span_rows, HD)

        delta = []
        lse = []
        for h in range(heads):
            product = own(grad_ref, h).astype(HIGH) * own(mixed_ref, h).astype(HIGH)
            delta.append(jnp.sum(jnp.transpose(product), axis=0, keepdims=True))
            lse.append(lse_ref[h, :1, lanes])

        def block(step, grad_query, visible):
            side = place_ref[step] // 4
            start = pl.multiple_of((place_ref[step] % 4) * half_rows, half_rows)
            there = pl.ds(start, half_rows)
            new = []
            for h in range(heads):
                query = own(query_ref, h)
                grad = own(grad_ref, h)
                keys = key_ref[side, :, there, columns[h]].reshape(span_rows, HD)
                values = value_ref[side, :, there, columns[h]].reshape(span_rows, HD)
                scores = matmul_right_t(keys, query) * (SCORE_SCALE * LOG2E)
                weights = jnp.exp2(scores - lse[h])
                if visible is not None:
                    weights = jnp.where(visible, weights, 0.0)
                grad_weights = matmul_right_t(values, grad)
                grad_scores = (weights * (grad_weights - delta[h])).astype(LOW)
                value_term = matmul(weights.astype(LOW), grad)
                key_term = matmul(grad_scores, query)
                value_sum_ref[side, :, there, columns[h]] += value_term.reshape(2, half_rows, HD)
                key_sum_ref[side, :, there, columns[h]] += key_term.reshape(2, half_rows, HD)
                new.append(grad_query[h] + matmul_left_t(grad_scores, keys))
            return tuple(new)

        start = tuple(jnp.zeros((span_rows, HD), HIGH) for _ in range(heads))
        grad_query = lax.fori_loop(
            0, rank // 2, lambda p, g: block(2 * p + 1, block(2 * p, g, None), None), start
        )
        grad_query = lax.fori_loop(
            rank // 2 * 2, rank, lambda p, g: block(p, g, None), grad_query
        )
        visible = diagonal_visible(core_ref[0], span_rows, 0)
        grad_query = block(rank, grad_query, visible)
        for h in range(heads):
            result = (grad_query[h] * SCORE_SCALE).astype(LOW)
            grad_query_ref[:, here, columns[h]] = result.reshape(2, half_rows, HD)
        return carry

    lax.fori_loop(0, rank_ref.shape[0], query_span, 0)
    grad_key_ref[...] = (key_sum_ref[...] * SCORE_SCALE).astype(LOW)
    grad_value_ref[...] = value_sum_ref[...].astype(LOW)


def heads_at_once(key_rows, features):
    return features // HD if key_rows <= 4096 else 1


def attention_forward(scalars, queries, keys, values):
    rows, features = queries.shape
    key_rows = keys.shape[0]
    own_spans = scalars[1].shape[0]
    half_rows = rows // own_spans // 2
    span_rows = 2 * half_rows
    heads = heads_at_once(key_rows, features)
    width = heads * HD
    pairs = rows * key_rows * features
    sides = key_rows // rows
    own = pl.BlockSpec((2, half_rows, width), lambda h, i, *_: (0, i, h))
    other = pl.BlockSpec((sides, 2, rows // 2, width), lambda h, i, *_: (0, 0, 0, h))
    mixed, lse = pl.pallas_call(
        forward_kernel,
        out_shape=(
            jax.ShapeDtypeStruct((2, rows // 2, features), LOW),
            jax.ShapeDtypeStruct((features // HD, 8, rows), HIGH),
        ),
        grid_spec=pltpu.PrefetchScalarGridSpec(
            num_scalar_prefetch=3,
            grid=(features // width, own_spans),
            in_specs=[own, other, other],
            out_specs=[own, pl.BlockSpec((heads, 8, span_rows), lambda h, i, *_: (h, 0, i))],
            scratch_shapes=[
                pltpu.VMEM((heads, key_rows // span_rows, span_rows, span_rows), HIGH)
            ],
        ),
        compiler_params=pltpu.CompilerParams(vmem_limit_bytes=56 * 2**20),
        cost_estimate=pl.CostEstimate(
            flops=2 * pairs, bytes_accessed=4 * key_rows * features, transcendentals=pairs // 256
        ),
        name="attention_forward",
    )(
        *scalars,
        queries.reshape(2, rows // 2, features),
        keys.reshape(sides, 2, rows // 2, features),
        values.reshape(sides, 2, rows // 2, features),
    )
    return mixed.reshape(rows, features), lse


def attention_backward(scalars, head, queries, grads, mixed, lse, keys, values):
    rows, features = queries.shape
    key_rows = keys.shape[0]
    pairs = rows * key_rows * HD
    sides = key_rows // rows
    own_shape = (2, rows // 2, features)
    key_shape = (sides, 2, rows // 2, features)
    own_part, key_part = own_shape[:2] + (HD,), key_shape[:3] + (HD,)
    own = pl.BlockSpec(own_part, lambda i, *_: (0, 0, head))
    other = pl.BlockSpec(key_part, lambda i, *_: (0, 0, 0, head))
    own_out = pl.BlockSpec(own_part, lambda i, *_: (0, 0, 0))
    other_out = pl.BlockSpec(key_part, lambda i, *_: (0, 0, 0, 0))
    grad_queries, grad_keys, grad_values = pl.pallas_call(
        backward_kernel,
        out_shape=(
            jax.ShapeDtypeStruct(own_part, LOW),
            jax.ShapeDtypeStruct(key_part, LOW),
            jax.ShapeDtypeStruct(key_part, LOW),
        ),
        grid_spec=pltpu.PrefetchScalarGridSpec(
            num_scalar_prefetch=3,
            grid=(1,),
            in_specs=[
                own,
                own,
                own,
                pl.BlockSpec((1, 8, rows), lambda i, *_: (head, 0, 0)),
                other,
                other,
            ],
            out_specs=[own_out, other_out, other_out],
            scratch_shapes=[pltpu.VMEM(key_part, HIGH)] * 2,
        ),
        compiler_params=pltpu.CompilerParams(vmem_limit_bytes=56 * 2**20),
        cost_estimate=pl.CostEstimate(
            flops=5 * pairs, bytes_accessed=8 * key_rows * HD, transcendentals=pairs // 256
        ),
        name="attention_backward",
    )(
        *scalars,
        queries.reshape(own_shape),
        grads.reshape(own_shape),
        mixed.reshape(own_shape),
        lse,
        keys.reshape(key_shape),
        values.reshape(key_shape),
    )
    return (
        grad_queries.reshape(rows, HD),
        grad_keys.reshape(key_rows, HD),
        grad_values.reshape(key_rows, HD),
    )


def per_device(
    states,
    shared_kv,
    norm_gain,
    kv_gain,
    ffn_gain,
    query_weight,
    key_weight,
    value_weight,
    out_weight,
    gate_weight,
    up_weight,
    down_weight,
    span_order,
    grad_output,
):
    z, x, y, c = (lax.axis_index(name) for name in ALL)
    size_x = lax.axis_size("x")
    sides = 2 * size_x
    rows_local, width_model = states.shape
    weight_rows = query_weight.shape[0]
    units_local = gate_weight.shape[1]
    own_width = width_model // 8

    side = jnp.arange(sides, dtype=jnp.int32)
    side_owner = jnp.mod(x - side // 2, size_x) * 2 + jnp.bitwise_xor(y, side % 2)
    back = jnp.mod(jnp.arange(4, dtype=jnp.int32) + 1, 4)
    back_owner = jnp.mod(z - back, 4)

    ticks = Ticks()

    block = jnp.arange(8 * sides, dtype=jnp.int32)
    block_half, block_side = block // (4 * sides), block // 4 % sides
    block_back = 2 * block_half + block // 2 % 2
    block_place = (
        (jnp.mod(z - block_back, 4) * size_x + jnp.mod(x - block_side // 2, size_x)) * 2
        + jnp.bitwise_xor(y, block_side % 2)
    ) * 2 + jnp.bitwise_xor(c, block % 2)

    state_rows = states.astype(HIGH)
    shared_rows = shared_kv.astype(HIGH)
    plain_kv, factor_kv, normed_kv = normalize(shared_rows, kv_gain)
    plain_one, factor_one, normed_one = normalize(state_rows, norm_gain)
    shared_low = normed_kv.astype(LOW)
    normed_low = normed_one.astype(LOW)

    with jax.named_scope("weight_columns"):
        pair = 2 * own_width
        stacked = jnp.stack([key_weight, value_weight, query_weight], axis=1)
        cut = [
            lax.dynamic_slice_in_dim(stacked, jnp.mod(z + step, 4) * pair, pair, 2)
            for step in range(4)
        ]
        shared_next, *over = ticks.tick((shared_low, 1), (cut[1], 1), (cut[2], 2), (cut[3], 3))
        columns = []
        for part in [cut[0]] + over:
            keep = lax.dynamic_slice_in_dim(part, c * own_width, own_width, 2)
            give = lax.dynamic_slice_in_dim(part, (1 - c) * own_width, own_width, 2)
            columns += [keep, hop(give, "c")]
        columns = jnp.stack(columns).reshape(8, weight_rows, 3 * own_width)
    with jax.named_scope("shared_rows"):
        weight_task = ticks.add(gather_task(columns[:4], columns[4:]))
        shared_blocks = [shared_low, shared_next]
        for _ in range(2):
            shared_blocks += ticks.tick((shared_blocks[-1], 1))
        group_shared = ticks.both_cores(shared_blocks)
    with jax.named_scope("weight_columns"):
        first, second = ticks.finish(weight_task)[0]
        weight_kv, weight_query = place_blocks(
            first + second, block_place, (2 * own_width, own_width)
        )
    with jax.named_scope("keys_values"):
        keys_own = matmul(group_shared, weight_kv[:, :own_width]).astype(LOW)
        values_own = matmul(group_shared, weight_kv[:, own_width:]).astype(LOW)
        keys_task = ticks.add(gather_task(keys_own, values_own))
    with jax.named_scope("out_weight"):
        out_task = ticks.add(
            gather_task(out_weight[: weight_rows // 2], out_weight[weight_rows // 2 :])
        )
    with jax.named_scope("normed_rows"):
        group_normed = ticks.gather_rows(normed_low)
        queries = matmul(group_normed, weight_query).astype(LOW)
    with jax.named_scope("grad_output_rows"):
        grad_back, grad_ahead = ticks.tick((grad_output, 1), (grad_output, -1))
    with jax.named_scope("keys_values"):
        ((keys_all, values_all),) = ticks.finish(keys_task)
        keys_all, values_all = jnp.concatenate(keys_all), jnp.concatenate(values_all)

    span_of = (back_owner[None, :] * sides + side_owner[:, None]).reshape(-1)
    ranks = jnp.take(span_order, span_of)
    spans = span_order.shape[0]
    listed = jnp.arange(spans, dtype=jnp.int32)
    place = jnp.sum(jnp.where(ranks[None, :] == listed[:, None], listed[None, :], 0), axis=1)
    scalars = (place, ranks[:4], c.reshape(1).astype(jnp.int32))

    with jax.named_scope("unit_weights"):
        late = (keys_all, values_all)
        unit_rows = jnp.concatenate(
            [
                pad_units(jnp.transpose(after(gate_weight, *late))),
                pad_units(jnp.transpose(after(up_weight, *late))),
                pad_units(after(down_weight, *late)),
            ],
            axis=0,
        )
        cuts = quarters(unit_rows.shape[0])
        chunks = [unit_rows[cuts[i] : cuts[i + 1]] for i in range(4)]
        unit_tasks = [ticks.add(gather_task(chunks[i], chunks[i + 1])) for i in (0, 2)]
    with jax.named_scope("grad_output_rows"):
        (grad_far,) = ticks.tick((grad_back, 1), room=2)
        group_grad = ticks.both_cores([grad_output, grad_back, grad_far, grad_ahead])
    mixed, lse = attention_forward(scalars, queries, keys_all, values_all)

    with jax.named_scope("out_weight"):
        whole = jnp.arange(sides, dtype=jnp.int32)
        whole_side = jnp.mod(x - whole // 2, size_x) * 2 + jnp.bitwise_xor(y, whole % 2)
        out_pieces = [
            part for pair in zip(*ticks.finish(out_task)[0]) for part in pair
        ]
        out_pieces = jnp.stack(out_pieces).reshape(sides, weight_rows, width_model)
        out_pieces = jnp.take(out_pieces, whole_side, axis=0).reshape(
            2, size_x // 2, 2, weight_rows, width_model
        )
        out_keep = lax.dynamic_index_in_dim(out_pieces, c, 0, keepdims=False)
        out_give = lax.dynamic_index_in_dim(out_pieces, 1 - c, 0, keepdims=False)
        out_got = hop(out_give, "c")
        weight_out = jnp.where(
            c == 0, jnp.stack([out_keep, out_got], axis=2), jnp.stack([out_got, out_keep], axis=2)
        ).reshape(own_width, width_model)

    with jax.named_scope("attention_sum"):
        attention_sum = RowSum(ticks, lambda v: matmul(v, weight_out), [mixed], rows_local)
        residual = state_rows + attention_sum.finish()
    plain_two, factor_two, normed_two = normalize(residual, ffn_gain)
    with jax.named_scope("normed_two_rows"):
        group_in = ticks.gather_rows(normed_two.astype(LOW))
    with jax.named_scope("unit_weights"):
        gathered = [pieces for result in ticks.finish(*unit_tasks) for pieces in result]
        units_padded = unit_rows.shape[0] // 3

        def units_of(which):
            low, high = which * units_padded, (which + 1) * units_padded
            rows = []
            for s in range(sides):
                for i in range(4):
                    start, stop = max(low, cuts[i]), min(high, cuts[i + 1])
                    if start < stop:
                        rows.append(gathered[i][s][start - cuts[i] : stop - cuts[i]])
            return jnp.concatenate(rows, axis=0)

        weight_gate, weight_up, weight_down = (units_of(which) for which in range(3))

    gate_act = matmul_right_t(group_in, weight_gate)
    up_act = matmul_right_t(group_in, weight_up)
    grad_hidden = matmul_right_t(group_grad, weight_down)
    sigmoid = jax.nn.sigmoid(gate_act)
    silu_act = gate_act * sigmoid
    hidden = (silu_act * up_act).astype(LOW)
    grad_gate_act = (
        grad_hidden * up_act * sigmoid * (1.0 + gate_act * (1.0 - sigmoid))
    ).astype(LOW)
    grad_up_act = (grad_hidden * silu_act).astype(LOW)
    with jax.named_scope("ffn_grad_sum"):
        ffn_grad_sum = RowSum(
            ticks,
            lambda g, u: matmul(g, weight_gate) + matmul(u, weight_up),
            [grad_gate_act, grad_up_act],
            rows_local,
        )
        ffn_grad_sum.step()
        ffn_grad_sum.step()
        sent = ffn_grad_sum.sent

    def unit_parts(values):
        step = values.shape[0] // sides
        return [values[s * step : (s + 1) * step] for s in range(sides)]

    with jax.named_scope("unit_weight_sums"):
        unit_terms = [
            unit_parts(matmul_left_t(after(left, sent), right).astype(LOW))
            for left, right in (
                (grad_gate_act, group_in),
                (grad_up_act, group_in),
                (hidden, group_grad),
            )
        ]

        def chunk_parts(i):
            parts = []
            for s in range(sides):
                rows = []
                for which in range(3):
                    low = which * units_padded
                    start, stop = max(low, cuts[i]), min(low + units_padded, cuts[i + 1])
                    if start < stop:
                        rows.append(unit_terms[which][s][start - low : stop - low])
                parts.append(jnp.concatenate(rows, axis=0))
            return parts

        unit_sum_tasks = [
            ticks.add(sum_task(chunk_parts(i), chunk_parts(i + 1))) for i in (0, 2)
        ]

    with jax.named_scope("ffn_grad_sum"):
        grad_ffn = ffn_grad_sum.finish()
    gain_two, grad_norm_two = norm_backward(grad_ffn, plain_two, factor_two, ffn_gain)
    grad_residual = grad_output.astype(HIGH) + grad_norm_two
    with jax.named_scope("branch_rows"):
        group_branch = ticks.gather_rows(grad_residual.astype(LOW))
    grad_mixed = matmul_right_t(group_branch, weight_out).astype(LOW)
    with jax.named_scope("ffn_sum"):
        ffn_sum = RowSum(
            ticks,
            lambda v: matmul(v, weight_down),
            [after(hidden, grad_residual)],
            rows_local,
        )
    head_terms = []
    key_tasks = []
    backward_inputs = (queries, grad_mixed, mixed)
    for head in range(own_width // HD):
        if ffn_sum.count < 2:
            with jax.named_scope("ffn_sum"):
                backward_inputs = after(backward_inputs, ticks.over_z)
                ffn_sum.step()
        terms = attention_backward(
            scalars, head, *after(backward_inputs, ffn_sum.sent), lse, keys_all, values_all
        )
        head_terms.append(terms[0])
        with jax.named_scope("grad_keys_values"):
            key_tasks.append(ticks.add(sum_task(unit_parts(terms[1]), unit_parts(terms[2]))))
    grad_queries = jnp.concatenate(head_terms, axis=1)

    def side_parts(values, k):
        chunks = values.reshape(2 * sides, -1, values.shape[1])
        return [
            lax.dynamic_index_in_dim(
                chunks,
                2 * jnp.bitwise_xor(jnp.bitwise_xor(side_owner[s], z), 2 * k) + k,
                0,
                keepdims=False,
            )
            for s in range(sides)
        ]

    def chunk_sums(values):
        return sum_task(side_parts(values, 0), side_parts(values, 1))

    to_layout = [
        [
            (
                ((za * size_x + xa) * 2 + ya) * 2 + ca,
                (2 * ((2 * xa + ya) ^ za ^ (2 * (ca ^ flip))) + (ca ^ flip)) * 4 + za,
            )
            for za in range(4)
            for xa in range(size_x)
            for ya in range(2)
            for ca in range(2)
        ]
        for flip in range(2)
    ]

    def layout(summed):
        sent = jnp.where(c == 0, summed[0], summed[1]), jnp.where(c == 0, summed[1], summed[0])
        got = [lax.ppermute(sent[flip], ALL, to_layout[flip]) for flip in range(2)]
        even = x % 2 == 0
        first = jnp.where(even, got[0], got[1]).astype(HIGH)
        second = jnp.where(even, got[1], got[0]).astype(HIGH)
        return [
            jnp.concatenate([part[:, at : at + own_width] for part in (first, second)], axis=1)
            for at in range(0, first.shape[1], own_width)
        ]

    with jax.named_scope("normed_sum"):
        normed_sum = RowSum(
            ticks, lambda v: matmul_right_t(v, weight_query), [grad_queries], rows_local
        )
        normed_sum.step()
        sent = normed_sum.sent
    with jax.named_scope("query_weight_sum"):
        query_terms = matmul_left_t(after(group_normed, sent), grad_queries).astype(LOW)
    with jax.named_scope("out_weight_sum"):
        out_terms = matmul_left_t(after(group_branch, sent), mixed).astype(LOW)
    with jax.named_scope("normed_sum"):
        grad_normed = normed_sum.finish()
    with jax.named_scope("ffn_sum"):
        output = (residual + ffn_sum.finish()).astype(LOW)
    with jax.named_scope("grad_keys_values"):
        parts = ticks.finish(*key_tasks)
        grad_kv = jnp.concatenate(
            [part[0] for part in parts] + [part[1] for part in parts], axis=1
        )
    with jax.named_scope("query_out_weight_sum"):
        query_out_task = ticks.add(
            chunk_sums(jnp.concatenate([query_terms, out_terms], axis=1))
        )
    with jax.named_scope("shared_sum"):
        shared_sum = RowSum(
            ticks, lambda v: matmul_right_t(v, weight_kv), [grad_kv], rows_local
        )
        shared_sum.step()
        sent = shared_sum.sent
    with jax.named_scope("key_value_weight_sum"):
        kv_terms = matmul_left_t(after(group_shared, sent), grad_kv).astype(LOW)
        kv_task = ticks.add(chunk_sums(kv_terms))
    with jax.named_scope("shared_sum"):
        grad_shared_normed = shared_sum.finish()
    with jax.named_scope("weight_layout"):
        query_out_sum, kv_sum = ticks.finish(query_out_task, kv_task)
        grad_query, grad_out = layout(query_out_sum)
        grad_key, grad_value = layout(kv_sum)
        grad_out = jnp.transpose(grad_out)
    with jax.named_scope("unit_weight_sums"):
        sums = [part for result in ticks.finish(*unit_sum_tasks) for part in result]
        whole = jnp.concatenate(sums, axis=0).astype(HIGH)
        grad_gate, grad_up, grad_down = (
            whole[w * units_padded : w * units_padded + units_local] for w in range(3)
        )
        grad_gate, grad_up = jnp.transpose(grad_gate), jnp.transpose(grad_up)

    gain_one, grad_in_one = norm_backward(grad_normed, plain_one, factor_one, norm_gain)
    gain_kv, grad_in_kv = norm_backward(grad_shared_normed, plain_kv, factor_kv, kv_gain)
    grad_states = (grad_residual + grad_in_one).astype(LOW)
    grad_shared = grad_in_kv.astype(LOW)

    devices = 8 * sides
    gain_terms = jnp.stack([g.reshape(devices, -1) for g in (gain_one, gain_kv, gain_two)], axis=1)
    gain_terms = lax.all_to_all(
        gain_terms.reshape(devices, -1), ALL, split_axis=0, concat_axis=0, tiled=True
    )
    gain_sums = jnp.sum(gain_terms, axis=0).reshape(3, -1)
    return (
        output,
        grad_states,
        grad_shared,
        gain_sums[0],
        gain_sums[1],
        gain_sums[2],
        grad_query,
        grad_key,
        grad_value,
        grad_out,
        grad_gate,
        grad_up,
        grad_down,
    )


def solution(mesh):
    size_ctx, size_head = mesh.shape["ctx"], mesh.shape["head"]
    fine = Mesh(mesh.devices.reshape(4, size_ctx // 4, 2, size_head // 2), ALL)
    rows = P(ALL, None)
    ctx, head = ("z", "x"), ("y", "c")
    in_specs = (
        rows,
        rows,
        P(),
        P(),
        P(),
        rows,
        rows,
        rows,
        rows,
        P(None, ALL),
        P(None, ALL),
        rows,
        P(),
        rows,
    )
    out_specs = (
        rows,
        rows,
        rows,
        P(ALL),
        P(ALL),
        P(ALL),
        P(ctx, head),
        P(ctx, head),
        P(ctx, head),
        P(head, ctx),
        P(None, ALL),
        P(None, ALL),
        rows,
    )
    return jax.shard_map(
        per_device, mesh=fine, in_specs=in_specs, out_specs=out_specs, check_vma=False
    )
```

```python
import math

import jax
import jax.numpy as jnp
from jax import lax
from jax.experimental import pallas as pl
from jax.experimental.pallas import tpu as pltpu
from jax.sharding import Mesh, PartitionSpec as P

HD = 128
EPSILON = 1e-06
LOW = jnp.bfloat16
HIGH = jnp.float32
LOG2E = math.log2(math.e)
SCORE_SCALE = HD ** (-0.5)
ALL = ("z", "x", "y", "c")


def add_low(first, second):
    return (first.astype(HIGH) + second.astype(HIGH)).astype(LOW)


def after(values, *earlier):
    return lax.optimization_barrier((values, earlier))[0]


def hop(values, axis, steps=1):
    size = lax.axis_size(axis)
    return lax.ppermute(values, axis, [(i, (i + steps) % size) for i in range(size)])


def both_cores(blocks):
    blocks = blocks[1:] + blocks[:1]
    return blocks + [hop(block, "c") for block in blocks]


def gather_task(first, second):
    size = lax.axis_size("x")
    firsts, seconds, first_over, second_over = [first], [second], [], []
    for stage in range(size):
        wanted = [("y", firsts[stage], first_over)]
        if stage == 0:
            wanted.append(("y", second, second_over))
        if stage < size - 1:
            wanted += [("x", firsts[stage], firsts), ("x", seconds[stage], seconds)]
        if stage:
            wanted.append(("x", second_over[stage - 1], second_over))
        yield wanted
    return (
        [piece for pair in zip(firsts, first_over) for piece in pair],
        [piece for pair in zip(seconds, second_over) for piece in pair],
    )


def sum_task(first, second):
    size = lax.axis_size("x")
    got, far, near = [], [], []
    over = [[] for _ in range(size)]
    far_total, near_total = second[3], second[2]
    for step in range(1, size):
        wanted = [("x", far_total, far), ("x", near_total, near)]
        if step == 1:
            wanted += [("y", first[2 * s + 1], over[s]) for s in range(1, size)]
            wanted.append(("y", first[1], over[0]))
        yield wanted
        at = 2 * ((step + 1) % size)
        far_total, near_total = add_low(second[at + 1], far[-1]), add_low(second[at], near[-1])
    merged = [add_low(first[2 * s], over[s][0]) for s in range(size)]
    total = merged[1]
    for step in range(1, size):
        wanted = [("x", total, got)]
        if step == 1:
            wanted.append(("y", far_total, far))
        yield wanted
        total = add_low(merged[(step + 1) % size], got[-1])
    return total, add_low(near_total, far[-1])


class Ticks:
    BYTES = 9 * 2**16

    def __init__(self):
        self.tasks = []
        self.over_z = ()
        self.sides = [(), ()]
        self.sent = None

    def add(self, task, urgent=False):
        entry = {"task": task, "wanted": None, "open": 0, "result": None}
        self.tasks.insert(0 if urgent else len(self.tasks), entry)
        self.advance(entry)
        return entry

    def advance(self, entry):
        try:
            entry["wanted"] = list(next(entry["task"]))
            entry["open"] = len(entry["wanted"])
        except StopIteration as stop:
            entry["result"] = stop.value
            self.tasks.remove(entry)

    def tick(self, *moves, room=1, lock=True, hold=False):
        got = []
        for values, steps in moves:
            self.sent = after(values, self.over_z, self.sides[-2])
            got.append(hop(self.sent, "z", steps))
        left = {"x": room * self.BYTES, "y": room * self.BYTES}
        before = self.over_z if lock else ()
        places = []
        arrived = []
        finished = []
        for entry in self.tasks:
            later = []
            for axis, values, into in entry["wanted"]:
                if left[axis] >= min(values.nbytes, self.BYTES):
                    left[axis] -= values.nbytes
                    into.append(hop(after(values, self.sides[-1], before), axis))
                    places.append((into, len(into) - 1))
                    arrived.append(into[-1])
                    entry["open"] -= 1
                else:
                    later.append((axis, values, into))
            entry["wanted"] = later
            if not entry["open"]:
                finished.append(entry)
        self.over_z = tuple(got) or self.over_z
        self.sides = self.sides[-1:] + [tuple(arrived)]
        self.held = (places, finished)
        if not hold:
            self.release()
        return got

    def release(self, *earlier):
        places, finished = self.held
        if earlier:
            for into, at in places:
                into[at] = after(into[at], earlier)
        for entry in finished:
            self.tasks.remove(entry)
            self.tasks.append(entry)
            self.advance(entry)

    def finish(self, *entries):
        while any(entry["result"] is None for entry in entries):
            self.tick()
        return [entry["result"] for entry in entries]

    def gather_rows(self, rows):
        blocks = [rows]
        for _ in range(1, lax.axis_size("z")):
            blocks += self.tick((blocks[-1], 1))
        return self.join_cores(blocks)

    def join_cores(self, blocks):
        return jnp.concatenate(both_cores(blocks), axis=0)


class RowSum:
    def __init__(self, ticks, terms_of, inputs, rows_local):
        self.ticks = ticks
        self.rows = rows_local
        self.half = inputs[0].shape[0] // 2
        self.terms_of = terms_of
        self.inputs = tuple(inputs)
        self.count = 0
        self.total = self.terms(self.inputs, 0).astype(LOW)

    def terms(self, inputs, block):
        near, far = block * self.rows, self.half + block * self.rows
        far_terms = self.terms_of(*(v[far : far + self.rows] for v in inputs))
        got = hop(far_terms.astype(LOW), "c")
        return self.terms_of(*(v[near : near + self.rows] for v in inputs)) + got.astype(HIGH)

    def step(self):
        (got,) = self.ticks.tick((self.total, 1))
        self.sent = self.ticks.sent
        self.count += 1
        self.total = self.terms(after(self.inputs, self.sent), self.count) + got.astype(HIGH)
        if self.count < 3:
            self.total = self.total.astype(LOW)

    def finish(self):
        while self.count < 3:
            self.step()
        return self.total


def place_blocks(pieces, places, widths):
    count, rows, width = pieces[0].shape
    total = len(pieces) * count

    def kernel(place_ref, *refs):
        ins, outs = refs[: len(pieces)], refs[len(pieces) :]
        for at in range(total):
            start = 0
            for out, size in zip(outs, widths):
                out[place_ref[at]] = ins[at // count][at % count, :, start : start + size]
                start += size

    shapes = [(total, rows, size) for size in widths]
    placed = pl.pallas_call(
        kernel,
        out_shape=[jax.ShapeDtypeStruct(shape, pieces[0].dtype) for shape in shapes],
        grid_spec=pltpu.PrefetchScalarGridSpec(
            num_scalar_prefetch=1,
            grid=(1,),
            in_specs=[pl.BlockSpec((count, rows, width), lambda i, *_: (0, 0, 0))] * len(pieces),
            out_specs=[pl.BlockSpec(shape, lambda i, *_: (0, 0, 0)) for shape in shapes],
        ),
        compiler_params=pltpu.CompilerParams(vmem_limit_bytes=48 * 2**20),
        cost_estimate=pl.CostEstimate(
            flops=0, bytes_accessed=4 * total * rows * width, transcendentals=0
        ),
        name="place_blocks",
    )(places, *pieces)
    return [out.reshape(total * rows, -1) for out in placed]


def normalize(values, gain_vec):
    factor = lax.rsqrt(jnp.mean(values * values, axis=-1, keepdims=True) + EPSILON)
    plain_rows = values * factor
    return (plain_rows, factor, plain_rows * gain_vec)


def norm_backward(grad_normed, plain_rows, factor, gain_vec):
    scaled = grad_normed * gain_vec
    gain_part = jnp.sum(grad_normed * plain_rows, axis=0)
    grad_input = factor * (
        scaled - plain_rows * jnp.mean(scaled * plain_rows, axis=-1, keepdims=True)
    )
    return (gain_part, grad_input)


def matmul(left_side, right_side):
    return jnp.dot(left_side, right_side, preferred_element_type=HIGH)


def matmul_right_t(left_side, right_side):
    return lax.dot_general(
        left_side, right_side, (((1,), (1,)), ((), ())), preferred_element_type=HIGH
    )


def matmul_left_t(left_side, right_side):
    return lax.dot_general(
        left_side, right_side, (((0,), (0,)), ((), ())), preferred_element_type=HIGH
    )


def pad_units(rows):
    extra = -rows.shape[0] % 16
    return jnp.pad(rows, ((0, extra), (0, 0)))


def quarters(count):
    tiles = count // 16
    return [16 * (tiles * i // 4) for i in range(5)]


def diagonal_visible(core, span_rows, key_axis):
    half = span_rows // 2

    def place(axis):
        index = lax.broadcasted_iota(jnp.int32, (span_rows, span_rows), axis)
        flipped = jnp.where(index < half, index + half, index - half)
        return jnp.where(core == 0, index, flipped)

    return place(key_axis) <= place(1 - key_axis)


def forward_kernel(
    place_ref, rank_ref, core_ref, query_ref, key_ref, value_ref, mixed_ref, lse_ref, score_ref
):
    half_rows = query_ref.shape[1]
    span_rows = 2 * half_rows
    heads = query_ref.shape[2] // HD
    rank = rank_ref[pl.program_id(1)]
    columns = [slice(h * HD, (h + 1) * HD) for h in range(heads)]

    def span(ref, step, h):
        side = place_ref[step] // 4
        start = pl.multiple_of((place_ref[step] % 4) * half_rows, half_rows)
        return ref[side, :, pl.ds(start, half_rows), columns[h]].reshape(span_rows, HD)

    def block_scores(step, h):
        query = query_ref[:, :, columns[h]].reshape(span_rows, HD)
        return matmul_right_t(query, span(key_ref, step, h)) * (SCORE_SCALE * LOG2E)

    def fold(values, operation):
        folded = values[:, :HD]
        for at in range(HD, span_rows, HD):
            folded = operation(folded, values[:, at : at + HD])
        return folded

    def score_step(step, maxima, count):
        new = []
        for h in range(heads):
            top = maxima[h]
            for at in range(count):
                scores = block_scores(step + at, h)
                score_ref[h, step + at] = scores
                top = jnp.maximum(top, fold(scores, jnp.maximum))
            new.append(top)
        return tuple(new)

    maxima = tuple(jnp.full((span_rows, HD), -jnp.inf, HIGH) for _ in range(heads))
    maxima = lax.fori_loop(0, rank // 2, lambda p, m: score_step(2 * p, m, 2), maxima)
    maxima = lax.fori_loop(rank // 2 * 2, rank, lambda p, m: score_step(p, m, 1), maxima)
    visible = diagonal_visible(core_ref[0], span_rows, 1)
    tops = []
    for h in range(heads):
        scores = jnp.where(visible, block_scores(rank, h), -jnp.inf)
        score_ref[h, rank] = scores
        top = jnp.maximum(maxima[h], fold(scores, jnp.maximum))
        tops.append(jnp.max(top, axis=1, keepdims=True))

    def mix_step(step, running, count):
        new = []
        for h in range(heads):
            total, mixed = running[h]
            for at in range(count):
                weights = jnp.exp2(score_ref[h, step + at] - tops[h])
                total = total + fold(weights, jnp.add)
                mixed = mixed + matmul(weights.astype(LOW), span(value_ref, step + at, h))
            new.append((total, mixed))
        return tuple(new)

    zero = jnp.zeros((span_rows, HD), HIGH)
    sums = tuple((zero, zero) for _ in range(heads))
    blocks = rank + 1
    sums = lax.fori_loop(0, blocks // 2, lambda p, r: mix_step(2 * p, r, 2), sums)
    sums = lax.fori_loop(blocks // 2 * 2, blocks, lambda p, r: mix_step(p, r, 1), sums)
    for h in range(heads):
        total = jnp.sum(sums[h][0], axis=1, keepdims=True)
        mixed = (sums[h][1] / total).astype(LOW)
        mixed_ref[:, :, columns[h]] = mixed.reshape(2, half_rows, HD)
        lse = jnp.broadcast_to(tops[h] + jnp.log2(total), (span_rows, HD))
        lse_ref[h] = jnp.transpose(lse)[:8, :]


def backward_kernel(
    place_ref,
    rank_ref,
    core_ref,
    query_ref,
    mixed_ref,
    lse_ref,
    key_ref,
    value_ref,
    weight_ref,
    *refs,
):
    *branch_refs, grad_query_ref, grad_key_ref, grad_value_ref = refs[:-3]
    grad_ref, key_sum_ref, value_sum_ref = refs[-3:]
    heads = query_ref.shape[2] // HD
    half_rows = query_ref.shape[1] // rank_ref.shape[0]
    span_rows = 2 * half_rows
    columns = [slice(h * HD, (h + 1) * HD) for h in range(heads)]
    for at, ref in enumerate(branch_refs):
        rows = slice(at % 4 * half_rows, (at % 4 + 1) * half_rows)
        grad_ref[at // 4, rows, :] = matmul_right_t(ref[...], weight_ref[...]).astype(LOW)
    key_sum_ref[...] = jnp.zeros_like(key_sum_ref)
    value_sum_ref[...] = jnp.zeros_like(value_sum_ref)

    def query_span(at, carry):
        here = pl.ds(pl.multiple_of(at * half_rows, half_rows), half_rows)
        lanes = pl.ds(pl.multiple_of(at * span_rows, span_rows), span_rows)
        rank = rank_ref[at]

        def own(ref, h):
            return ref[:, here, columns[h]].reshape(span_rows, HD)

        delta = []
        lse = []
        for h in range(heads):
            product = own(grad_ref, h).astype(HIGH) * own(mixed_ref, h).astype(HIGH)
            delta.append(jnp.sum(jnp.transpose(product), axis=0, keepdims=True))
            lse.append(lse_ref[h, :1, lanes])

        def block(step, grad_query, visible):
            side = place_ref[step] // 4
            start = pl.multiple_of((place_ref[step] % 4) * half_rows, half_rows)
            there = pl.ds(start, half_rows)
            new = []
            for h in range(heads):
                query = own(query_ref, h)
                grad = own(grad_ref, h)
                keys = key_ref[side, :, there, columns[h]].reshape(span_rows, HD)
                values = value_ref[side, :, there, columns[h]].reshape(span_rows, HD)
                scores = matmul_right_t(keys, query) * (SCORE_SCALE * LOG2E)
                weights = jnp.exp2(scores - lse[h])
                if visible is not None:
                    weights = jnp.where(visible, weights, 0.0)
                grad_weights = matmul_right_t(values, grad)
                grad_scores = (weights * (grad_weights - delta[h])).astype(LOW)
                value_term = matmul(weights.astype(LOW), grad)
                key_term = matmul(grad_scores, query)
                value_sum_ref[side, :, there, columns[h]] += value_term.reshape(2, half_rows, HD)
                key_sum_ref[side, :, there, columns[h]] += key_term.reshape(2, half_rows, HD)
                new.append(grad_query[h] + matmul_left_t(grad_scores, keys))
            return tuple(new)

        start = tuple(jnp.zeros((span_rows, HD), HIGH) for _ in range(heads))
        grad_query = lax.fori_loop(
            0, rank // 2, lambda p, g: block(2 * p + 1, block(2 * p, g, None), None), start
        )
        grad_query = lax.fori_loop(
            rank // 2 * 2, rank, lambda p, g: block(p, g, None), grad_query
        )
        visible = diagonal_visible(core_ref[0], span_rows, 0)
        grad_query = block(rank, grad_query, visible)
        for h in range(heads):
            result = (grad_query[h] * SCORE_SCALE).astype(LOW)
            grad_query_ref[:, here, columns[h]] = result.reshape(2, half_rows, HD)
        return carry

    lax.fori_loop(0, rank_ref.shape[0], query_span, 0)
    grad_key_ref[...] = (key_sum_ref[...] * SCORE_SCALE).astype(LOW)
    grad_value_ref[...] = value_sum_ref[...].astype(LOW)


def heads_at_once(key_rows, features):
    return features // HD if key_rows <= 4096 else 1


def attention_forward(scalars, queries, keys, values):
    rows, features = queries.shape
    key_rows = keys.shape[0]
    own_spans = scalars[1].shape[0]
    half_rows = rows // own_spans // 2
    span_rows = 2 * half_rows
    heads = heads_at_once(key_rows, features)
    width = heads * HD
    pairs = rows * key_rows * features
    sides = key_rows // rows
    own = pl.BlockSpec((2, half_rows, width), lambda h, i, *_: (0, i, h))
    other = pl.BlockSpec((sides, 2, rows // 2, width), lambda h, i, *_: (0, 0, 0, h))
    mixed, lse = pl.pallas_call(
        forward_kernel,
        out_shape=(
            jax.ShapeDtypeStruct((2, rows // 2, features), LOW),
            jax.ShapeDtypeStruct((features // HD, 8, rows), HIGH),
        ),
        grid_spec=pltpu.PrefetchScalarGridSpec(
            num_scalar_prefetch=3,
            grid=(features // width, own_spans),
            in_specs=[own, other, other],
            out_specs=[own, pl.BlockSpec((heads, 8, span_rows), lambda h, i, *_: (h, 0, i))],
            scratch_shapes=[
                pltpu.VMEM((heads, key_rows // span_rows, span_rows, span_rows), HIGH)
            ],
        ),
        compiler_params=pltpu.CompilerParams(vmem_limit_bytes=56 * 2**20),
        cost_estimate=pl.CostEstimate(
            flops=20 * pairs, bytes_accessed=4 * key_rows * features, transcendentals=pairs // 256
        ),
        name="attention_forward",
    )(
        *scalars,
        queries.reshape(2, rows // 2, features),
        keys.reshape(sides, 2, rows // 2, features),
        values.reshape(sides, 2, rows // 2, features),
    )
    return mixed.reshape(rows, features), lse


def attention_backward(scalars, queries, mixed, lse, keys, values, weight_out, branch_blocks):
    rows, features = queries.shape
    key_rows = keys.shape[0]
    heads = heads_at_once(key_rows, features)
    width = heads * HD
    pairs = rows * key_rows * features
    sides = key_rows // rows
    own_shape = (2, rows // 2, features)
    key_shape = (sides, 2, rows // 2, features)
    once = pl.Buffered(1)
    own_part, key_part = own_shape[:2] + (width,), key_shape[:3] + (width,)
    own = pl.BlockSpec(own_part, lambda h, *_: (0, 0, h))
    other = pl.BlockSpec(key_part, lambda h, *_: (0, 0, 0, h))
    other_in = pl.BlockSpec(key_part, lambda h, *_: (0, 0, 0, h), pipeline_mode=once)
    block = pl.BlockSpec(branch_blocks[0].shape, lambda h, *_: (0, 0), pipeline_mode=once)
    grad_queries, grad_keys, grad_values = pl.pallas_call(
        backward_kernel,
        out_shape=(
            jax.ShapeDtypeStruct(own_shape, LOW),
            jax.ShapeDtypeStruct(key_shape, LOW),
            jax.ShapeDtypeStruct(key_shape, LOW),
        ),
        grid_spec=pltpu.PrefetchScalarGridSpec(
            num_scalar_prefetch=3,
            grid=(features // width,),
            in_specs=[
                own,
                own,
                pl.BlockSpec((heads, 8, rows), lambda h, *_: (h, 0, 0)),
                other_in,
                other_in,
                pl.BlockSpec((width, weight_out.shape[1]), lambda h, *_: (h, 0)),
            ]
            + [block] * len(branch_blocks),
            out_specs=[own, other, other],
            scratch_shapes=[pltpu.VMEM(own_part, LOW)] + [pltpu.VMEM(key_part, HIGH)] * 2,
        ),
        compiler_params=pltpu.CompilerParams(vmem_limit_bytes=56 * 2**20),
        cost_estimate=pl.CostEstimate(
            flops=120 * pairs, bytes_accessed=8 * key_rows * features, transcendentals=pairs // 256
        ),
        name="attention_backward",
    )(
        *scalars,
        queries.reshape(own_shape),
        mixed.reshape(own_shape),
        lse,
        keys.reshape(key_shape),
        values.reshape(key_shape),
        weight_out,
        *branch_blocks,
    )
    return (
        grad_queries.reshape(rows, features),
        grad_keys.reshape(key_rows, features),
        grad_values.reshape(key_rows, features),
    )


def per_device(
    states,
    shared_kv,
    norm_gain,
    kv_gain,
    ffn_gain,
    query_weight,
    key_weight,
    value_weight,
    out_weight,
    gate_weight,
    up_weight,
    down_weight,
    span_order,
    grad_output,
):
    z, x, y, c = (lax.axis_index(name) for name in ALL)
    size_x = lax.axis_size("x")
    sides = 2 * size_x
    rows_local, width_model = states.shape
    weight_rows = query_weight.shape[0]
    units_local = gate_weight.shape[1]
    own_width = width_model // 8

    side = jnp.arange(sides, dtype=jnp.int32)
    side_owner = jnp.mod(x - side // 2, size_x) * 2 + jnp.bitwise_xor(y, side % 2)
    back = jnp.mod(jnp.arange(4, dtype=jnp.int32) + 1, 4)
    back_owner = jnp.mod(z - back, 4)

    ticks = Ticks()

    block = jnp.arange(8 * sides, dtype=jnp.int32)
    block_half, block_side = block // (4 * sides), block // 4 % sides
    block_back = 2 * block_half + block // 2 % 2
    block_place = (
        (jnp.mod(z - block_back, 4) * size_x + jnp.mod(x - block_side // 2, size_x)) * 2
        + jnp.bitwise_xor(y, block_side % 2)
    ) * 2 + jnp.bitwise_xor(c, block % 2)

    state_rows = states.astype(HIGH)
    shared_rows = shared_kv.astype(HIGH)
    plain_kv, factor_kv, normed_kv = normalize(shared_rows, kv_gain)
    plain_one, factor_one, normed_one = normalize(state_rows, norm_gain)
    shared_low = normed_kv.astype(LOW)
    normed_low = normed_one.astype(LOW)

    with jax.named_scope("out_weight"):
        out_task = ticks.add(
            gather_task(out_weight[: weight_rows // 2], out_weight[weight_rows // 2 :])
        )
    with jax.named_scope("weight_columns"):
        pair = 2 * own_width
        projections = (key_weight, value_weight, query_weight)

        def cut(start, size, arrays):
            return jnp.concatenate(
                [lax.dynamic_slice_in_dim(v, start, size, 1) for v in arrays], axis=1
            )

        parts = [cut(jnp.mod(z + step, 4) * pair, pair, projections) for step in range(4)]
        over = ticks.tick((parts[1], 1), (parts[2], 2), (parts[3], 3), lock=False)
        columns = []
        for part in [parts[0]] + over:
            arrays = [part[:, i * pair : (i + 1) * pair] for i in range(3)]
            columns.append(cut(c * own_width, own_width, arrays))
            columns.append(hop(cut((1 - c) * own_width, own_width, arrays), "c"))
        columns = jnp.stack(columns)
    with jax.named_scope("shared_rows"):
        weight_task = ticks.add(gather_task(columns[:4], columns[4:]))
        shared_blocks = [shared_low]
        for _ in range(3):
            shared_blocks += ticks.tick((shared_blocks[-1], 1), lock=False)
        group_shared = ticks.join_cores(shared_blocks)
    with jax.named_scope("weight_columns"):
        first, second = ticks.finish(weight_task)[0]
        weight_kv, weight_query = place_blocks(
            first + second, block_place, (2 * own_width, own_width)
        )
    with jax.named_scope("out_weight"):
        whole = jnp.arange(sides, dtype=jnp.int32)
        whole_side = jnp.mod(x - whole // 2, size_x) * 2 + jnp.bitwise_xor(y, whole % 2)
        out_pieces = ticks.finish(out_task)[0]
        out_pieces = jnp.stack([part for pair in zip(*out_pieces) for part in pair])
        out_pieces = jnp.take(
            out_pieces.reshape(sides, weight_rows, width_model), whole_side, axis=0
        ).reshape(2, size_x // 2, 2, weight_rows, width_model)
        out_keep = lax.dynamic_index_in_dim(out_pieces, c, 0, keepdims=False)
        out_give = lax.dynamic_index_in_dim(out_pieces, 1 - c, 0, keepdims=False)
        out_got = hop(out_give, "c")
        weight_out = jnp.where(
            c == 0, jnp.stack([out_keep, out_got], axis=2), jnp.stack([out_got, out_keep], axis=2)
        ).reshape(own_width, width_model)

    with jax.named_scope("keys_values"):
        group_shared = after(group_shared, weight_out)
        keys_own = matmul(group_shared, weight_kv[:, :own_width]).astype(LOW)
        values_own = matmul(group_shared, weight_kv[:, own_width:]).astype(LOW)
        keys_task = ticks.add(gather_task(keys_own, values_own))
    with jax.named_scope("normed_rows"):
        normed_blocks = [normed_low]
        for _ in range(3):
            normed_blocks += ticks.tick((normed_blocks[-1], 1), lock=False)
    with jax.named_scope("normed_rows"):
        group_normed = ticks.join_cores(normed_blocks)
        queries = matmul(group_normed, weight_query).astype(LOW)
    with jax.named_scope("grad_output_rows"):
        grad_blocks = [grad_output] + ticks.tick((grad_output, 1))
    with jax.named_scope("keys_values"):
        keys_all, values_all = after(ticks.finish(keys_task)[0], queries)
        keys_all, values_all = jnp.concatenate(keys_all), jnp.concatenate(values_all)

    span_of = (back_owner[None, :] * sides + side_owner[:, None]).reshape(-1)
    ranks = jnp.take(span_order, span_of)
    spans = span_order.shape[0]
    listed = jnp.arange(spans, dtype=jnp.int32)
    place = jnp.sum(jnp.where(ranks[None, :] == listed[:, None], listed[None, :], 0), axis=1)
    scalars = (place, ranks[:4], c.reshape(1).astype(jnp.int32))

    with jax.named_scope("unit_weights"):
        late = (keys_all, values_all)
        unit_rows = jnp.concatenate(
            [
                pad_units(jnp.transpose(after(gate_weight, *late))),
                pad_units(jnp.transpose(after(up_weight, *late))),
                pad_units(after(down_weight, *late)),
            ],
            axis=0,
        )
        cuts = quarters(unit_rows.shape[0])
        chunks = [unit_rows[cuts[i] : cuts[i + 1]] for i in range(4)]
        unit_tasks = [ticks.add(gather_task(chunks[i], chunks[i + 1])) for i in (0, 2)]
    with jax.named_scope("grad_output_rows"):
        grad_blocks += ticks.tick((grad_blocks[-1], 1), (grad_output, -1))
    mixed, lse = attention_forward(scalars, queries, keys_all, values_all)
    with jax.named_scope("grad_output_rows"):
        group_grad = ticks.join_cores(grad_blocks)
    with jax.named_scope("attention_sum"):
        attention_sum = RowSum(ticks, lambda v: matmul(v, weight_out), [mixed], rows_local)
        residual = state_rows + attention_sum.finish()
    plain_two, factor_two, normed_two = normalize(residual, ffn_gain)
    with jax.named_scope("normed_two_rows"):
        group_in = ticks.gather_rows(normed_two.astype(LOW))
    with jax.named_scope("unit_weights"):
        gathered = [pieces for result in ticks.finish(*unit_tasks) for pieces in result]
        units_padded = unit_rows.shape[0] // 3

        def units_of(which):
            low, high = which * units_padded, (which + 1) * units_padded
            rows = []
            for s in range(sides):
                for i in range(4):
                    start, stop = max(low, cuts[i]), min(high, cuts[i + 1])
                    if start < stop:
                        rows.append(gathered[i][s][start - cuts[i] : stop - cuts[i]])
            return jnp.concatenate(rows, axis=0)

        weight_gate, weight_up, weight_down = (units_of(which) for which in range(3))

    gate_act = matmul_right_t(group_in, weight_gate)
    up_act = matmul_right_t(group_in, weight_up)
    grad_hidden = matmul_right_t(group_grad, weight_down)
    sigmoid = jax.nn.sigmoid(gate_act)
    silu_act = gate_act * sigmoid
    hidden = (silu_act * up_act).astype(LOW)
    grad_gate_act = (
        grad_hidden * up_act * sigmoid * (1.0 + gate_act * (1.0 - sigmoid))
    ).astype(LOW)
    grad_up_act = (grad_hidden * silu_act).astype(LOW)
    def unit_parts(values):
        step = values.shape[0] // sides
        return [values[s * step : (s + 1) * step] for s in range(sides)]

    with jax.named_scope("ffn_grad_sum"):
        ffn_grad_sum = RowSum(
            ticks,
            lambda g, u: matmul(g, weight_gate) + matmul(u, weight_up),
            [grad_gate_act, grad_up_act],
            rows_local,
        )
        unit_terms = []

        def unit_window(left, right):
            ffn_grad_sum.step()
            terms = matmul_left_t(after(left, ffn_grad_sum.sent), right).astype(LOW)
            unit_terms.append(unit_parts(terms))

        def chunk_parts(i):
            parts = []
            for s in range(sides):
                rows = []
                for which in range(3):
                    low = which * units_padded
                    start, stop = max(low, cuts[i]), min(low + units_padded, cuts[i + 1])
                    if start < stop:
                        rows.append(unit_terms[which][s][start - low : stop - low])
                parts.append(jnp.concatenate(rows, axis=0) if rows[1:] else rows[0])
            return parts

        unit_window(grad_gate_act, group_in)
        unit_window(grad_up_act, group_in)
        unit_sum_tasks = [ticks.add(sum_task(chunk_parts(0), chunk_parts(1)))]
        unit_window(hidden, group_grad)
        unit_sum_tasks.append(ticks.add(sum_task(chunk_parts(2), chunk_parts(3))))
        grad_ffn = ffn_grad_sum.finish()

    gain_two, grad_norm_two = norm_backward(grad_ffn, plain_two, factor_two, ffn_gain)
    grad_residual = grad_output.astype(HIGH) + grad_norm_two
    with jax.named_scope("branch_rows"):
        branch_blocks = [grad_residual.astype(LOW)]
        branch_blocks += ticks.tick((branch_blocks[-1], 1))
        lined = jnp.arange(8, dtype=jnp.int32)
        order = jnp.bitwise_xor(c, lined % 2) * 4 + jnp.mod(z - lined // 2 - 1, 4)
        late_hidden = after(hidden, ticks.sent).reshape(8, rows_local, -1)
        late_hidden = jnp.take(late_hidden, order, axis=0).reshape(8 * rows_local, -1)
        branch_blocks += ticks.tick((branch_blocks[-1], 1))
        terms = matmul(after(late_hidden, ticks.sent), weight_down).astype(LOW)
        branch_blocks += ticks.tick((branch_blocks[-1], 1))
        branch_both = both_cores(branch_blocks)
    with jax.named_scope("ffn_sum"):
        branch = lax.psum_scatter(
            after(terms, branch_blocks[-1]), ("z", "c"), scatter_dimension=0, tiled=True
        )
        output = (residual + branch.astype(HIGH)).astype(LOW)
    with jax.named_scope("unit_weight_sums"):
        ticks.tick(room=2, lock=False, hold=True)
    grad_queries, key_terms, value_terms = attention_backward(
        scalars, queries, mixed, lse, keys_all, values_all, weight_out, branch_both
    )

    with jax.named_scope("unit_weight_sums"):
        ticks.release(grad_queries)

    def side_parts(values, k):
        count = values.shape[0] // (2 * sides)
        return [
            lax.dynamic_slice_in_dim(
                values,
                (2 * jnp.bitwise_xor(jnp.bitwise_xor(side_owner[s], z), 2 * k) + k) * count,
                count,
                0,
            )
            for s in range(sides)
        ]

    def chunk_sums(values):
        return sum_task(side_parts(values, 0), side_parts(values, 1))

    to_layout = [
        [
            (
                ((za * size_x + xa) * 2 + ya) * 2 + ca,
                (2 * ((2 * xa + ya) ^ za ^ (2 * (ca ^ flip))) + (ca ^ flip)) * 4 + za,
            )
            for za in range(4)
            for xa in range(size_x)
            for ya in range(2)
            for ca in range(2)
        ]
        for flip in range(2)
    ]

    def layout(summed):
        sent = jnp.where(c == 0, summed[0], summed[1]), jnp.where(c == 0, summed[1], summed[0])
        got = [lax.ppermute(sent[flip], ALL, to_layout[flip]) for flip in range(2)]
        even = x % 2 == 0
        first = jnp.where(even, got[0], got[1]).astype(HIGH)
        second = jnp.where(even, got[1], got[0]).astype(HIGH)
        return [
            jnp.concatenate([part[:, at : at + own_width] for part in (first, second)], axis=1)
            for at in range(0, first.shape[1], own_width)
        ]

    with jax.named_scope("grad_keys_values"):
        keys_task = ticks.add(
            sum_task(unit_parts(key_terms), unit_parts(value_terms)), urgent=True
        )
    with jax.named_scope("normed_sum"):
        normed_sum = RowSum(
            ticks, lambda v: matmul_right_t(v, weight_query), [grad_queries], rows_local
        )
        normed_sum.step()
        sent = normed_sum.sent
    with jax.named_scope("query_weight_sum"):
        query_terms = matmul_left_t(after(group_normed, sent), grad_queries).astype(LOW)
    with jax.named_scope("out_weight_sum"):
        group_branch = jnp.concatenate(after(branch_both, sent), axis=0)
        out_terms = matmul_left_t(group_branch, mixed).astype(LOW)
    with jax.named_scope("normed_sum"):
        grad_normed = normed_sum.finish()
    with jax.named_scope("grad_keys_values"):
        grad_kv = jnp.concatenate(ticks.finish(keys_task)[0], axis=1)
    with jax.named_scope("query_out_weight_sum"):
        query_out_task = ticks.add(
            chunk_sums(jnp.concatenate([query_terms, out_terms], axis=1))
        )
    with jax.named_scope("shared_sum"):
        shared_sum = RowSum(
            ticks, lambda v: matmul_right_t(v, weight_kv), [grad_kv], rows_local
        )
        shared_sum.total = after(shared_sum.total, branch)
        shared_sum.step()
        sent = shared_sum.sent
    with jax.named_scope("key_value_weight_sum"):
        kv_terms = matmul_left_t(after(group_shared, sent), grad_kv).astype(LOW)
        kv_task = ticks.add(chunk_sums(kv_terms))
    with jax.named_scope("shared_sum"):
        grad_shared_normed = shared_sum.finish()
    with jax.named_scope("weight_layout"):
        query_out_sum, kv_sum = ticks.finish(query_out_task, kv_task)
        grad_query, grad_out = layout(query_out_sum)
        grad_key, grad_value = layout(kv_sum)
        grad_out = jnp.transpose(grad_out)
    with jax.named_scope("unit_weight_sums"):
        sums = [part for result in ticks.finish(*unit_sum_tasks) for part in result]
        whole = jnp.concatenate(sums, axis=0).astype(HIGH)
        grad_gate, grad_up, grad_down = (
            whole[w * units_padded : w * units_padded + units_local] for w in range(3)
        )
        grad_gate, grad_up = jnp.transpose(grad_gate), jnp.transpose(grad_up)

    gain_one, grad_in_one = norm_backward(grad_normed, plain_one, factor_one, norm_gain)
    gain_kv, grad_in_kv = norm_backward(grad_shared_normed, plain_kv, factor_kv, kv_gain)
    grad_states = (grad_residual + grad_in_one).astype(LOW)
    grad_shared = grad_in_kv.astype(LOW)

    devices = 8 * sides
    gain_terms = jnp.stack([g.reshape(devices, -1) for g in (gain_one, gain_kv, gain_two)], axis=1)
    gain_terms = lax.all_to_all(
        gain_terms.reshape(devices, -1), ALL, split_axis=0, concat_axis=0, tiled=True
    )
    gain_sums = jnp.sum(gain_terms, axis=0).reshape(3, -1)
    return (
        output,
        grad_states,
        grad_shared,
        gain_sums[0],
        gain_sums[1],
        gain_sums[2],
        grad_query,
        grad_key,
        grad_value,
        grad_out,
        grad_gate,
        grad_up,
        grad_down,
    )


def solution(mesh):
    size_ctx, size_head = mesh.shape["ctx"], mesh.shape["head"]
    fine = Mesh(mesh.devices.reshape(4, size_ctx // 4, 2, size_head // 2), ALL)
    rows = P(ALL, None)
    ctx, head = ("z", "x"), ("y", "c")
    in_specs = (
        rows,
        rows,
        P(),
        P(),
        P(),
        rows,
        rows,
        rows,
        rows,
        P(None, ALL),
        P(None, ALL),
        rows,
        P(),
        rows,
    )
    out_specs = (
        rows,
        rows,
        rows,
        P(ALL),
        P(ALL),
        P(ALL),
        P(ctx, head),
        P(ctx, head),
        P(ctx, head),
        P(head, ctx),
        P(None, ALL),
        P(None, ALL),
        rows,
    )
    return jax.shard_map(
        per_device, mesh=fine, in_specs=in_specs, out_specs=out_specs, check_vma=False
    )
```

```python
import math

import jax
import jax.numpy as jnp
from jax import lax
from jax.experimental import pallas as pl
from jax.experimental.pallas import tpu as pltpu
from jax.sharding import Mesh, PartitionSpec as P

HD = 128
EPSILON = 1e-06
LOW = jnp.bfloat16
HIGH = jnp.float32
LOG2E = math.log2(math.e)
SCORE_SCALE = HD ** (-0.5)
ALL = ("z", "x", "y", "c")


def add_low(first, second):
    return (first.astype(HIGH) + second.astype(HIGH)).astype(LOW)


def after(values, *earlier):
    return lax.optimization_barrier((values, earlier))[0]


def hop(values, axis, steps=1):
    size = lax.axis_size(axis)
    return lax.ppermute(values, axis, [(i, (i + steps) % size) for i in range(size)])


def both_cores(blocks):
    blocks = blocks[1:] + blocks[:1]
    return blocks + [hop(block, "c") for block in blocks]


def gather_task(first, second):
    size = lax.axis_size("x")
    firsts, seconds, first_over, second_over = [first], [second], [], []
    for stage in range(size):
        wanted = [("y", firsts[stage], first_over)]
        if stage == 0:
            wanted.append(("y", second, second_over))
        if stage < size - 1:
            wanted += [("x", firsts[stage], firsts), ("x", seconds[stage], seconds)]
        if stage:
            wanted.append(("x", second_over[stage - 1], second_over))
        yield wanted
    return (
        [piece for pair in zip(firsts, first_over) for piece in pair],
        [piece for pair in zip(seconds, second_over) for piece in pair],
    )


def sum_task(first, second):
    size = lax.axis_size("x")
    got, far, near = [], [], []
    over = [[] for _ in range(size)]
    far_total, near_total = second[3], second[2]
    for step in range(1, size):
        wanted = [("x", far_total, far), ("x", near_total, near)]
        if step == 1:
            wanted += [("y", first[2 * s + 1], over[s]) for s in range(1, size)]
            wanted.append(("y", first[1], over[0]))
        yield wanted
        at = 2 * ((step + 1) % size)
        far_total, near_total = add_low(second[at + 1], far[-1]), add_low(second[at], near[-1])
    merged = [add_low(first[2 * s], over[s][0]) for s in range(size)]
    total = merged[1]
    for step in range(1, size):
        wanted = [("x", total, got)]
        if step == 1:
            wanted.append(("y", far_total, far))
        yield wanted
        total = add_low(merged[(step + 1) % size], got[-1])
    return total, add_low(near_total, far[-1])


class Ticks:
    BYTES = 9 * 2**16

    def __init__(self):
        self.tasks = []
        self.over_z = ()
        self.sides = [(), ()]
        self.sent = None
        self.held = []
        self.places = []

    def add(self, task, urgent=False):
        entry = {"task": task, "wanted": None, "open": 0, "result": None, "urgent": urgent}
        self.tasks.insert(0 if urgent else len(self.tasks), entry)
        self.advance(entry)
        return entry

    def advance(self, entry):
        try:
            entry["wanted"] = list(next(entry["task"]))
            entry["open"] = len(entry["wanted"])
        except StopIteration as stop:
            entry["result"] = stop.value
            self.tasks.remove(entry)

    def tick(self, *moves, room=1, lock=True):
        got = []
        for values, steps in moves:
            self.sent = after(values, self.over_z, self.sides[-2])
            got.append(hop(self.sent, "z", steps))
        self.release(*([self.sent] if moves else []))
        left = {"x": room * self.BYTES, "y": room * self.BYTES}
        before = self.over_z if lock else ()
        arrived = []
        finished = []
        for entry in self.tasks:
            later = []
            for axis, values, into in entry["wanted"]:
                if left[axis] >= min(values.nbytes, self.BYTES):
                    left[axis] -= values.nbytes
                    into.append(hop(after(values, self.sides[-1], before), axis))
                    if not entry["urgent"]:
                        self.places.append((into, len(into) - 1))
                    arrived.append(into[-1])
                    entry["open"] -= 1
                else:
                    later.append((axis, values, into))
            entry["wanted"] = later
            if not entry["open"]:
                finished.append(entry)
        self.over_z = tuple(got) or self.over_z
        self.sides = self.sides[-1:] + [tuple(arrived)]
        for entry in finished:
            if entry["urgent"]:
                self.advance(entry)
            else:
                self.held.append(entry)
        return got

    def release(self, *earlier):
        if earlier:
            for into, at in self.places:
                into[at] = after(into[at], earlier)
        held, self.held, self.places = self.held, [], []
        for entry in held:
            self.tasks.remove(entry)
            self.tasks.append(entry)
            self.advance(entry)

    def finish(self, *entries):
        self.release()
        while any(entry["result"] is None for entry in entries):
            self.tick()
            self.release()
        return [entry["result"] for entry in entries]

    def gather_parts(self, rows):
        blocks = [rows]
        for _ in range(1, lax.axis_size("z")):
            blocks += self.tick((blocks[-1], 1))
            yield self.sent
        yield both_cores(blocks)

    def gather_rows(self, rows):
        *_, blocks = self.gather_parts(rows)
        return jnp.concatenate(blocks, axis=0)

    def join_cores(self, blocks):
        return jnp.concatenate(both_cores(blocks), axis=0)


class RowSum:
    def __init__(self, ticks, terms_of, inputs, rows_local):
        self.ticks = ticks
        self.rows = rows_local
        self.half = inputs[0].shape[0] // 2
        self.terms_of = terms_of
        self.inputs = tuple(inputs)
        self.count = 0
        self.total = self.terms(self.inputs, 0).astype(LOW)

    def terms(self, inputs, block):
        near, far = block * self.rows, self.half + block * self.rows
        far_terms = self.terms_of(*(v[far : far + self.rows] for v in inputs))
        got = hop(far_terms.astype(LOW), "c")
        return self.terms_of(*(v[near : near + self.rows] for v in inputs)) + got.astype(HIGH)

    def step(self, room=1):
        (got,) = self.ticks.tick((self.total, 1), room=room)
        self.sent = self.ticks.sent
        self.count += 1
        terms = lax.optimization_barrier(self.terms(after(self.inputs, self.sent), self.count))
        self.total = terms + got.astype(HIGH)
        if self.count < 3:
            self.total = self.total.astype(LOW)

    def finish(self, room=1):
        while self.count < 3:
            self.step(room)
        return self.total


def place_blocks(pieces, places, widths):
    count, rows, width = pieces[0].shape
    total = len(pieces) * count

    def kernel(place_ref, *refs):
        ins, outs = refs[: len(pieces)], refs[len(pieces) :]
        for at in range(total):
            start = 0
            for out, size in zip(outs, widths):
                out[place_ref[at]] = ins[at // count][at % count, :, start : start + size]
                start += size

    shapes = [(total, rows, size) for size in widths]
    placed = pl.pallas_call(
        kernel,
        out_shape=[jax.ShapeDtypeStruct(shape, pieces[0].dtype) for shape in shapes],
        grid_spec=pltpu.PrefetchScalarGridSpec(
            num_scalar_prefetch=1,
            grid=(1,),
            in_specs=[pl.BlockSpec((count, rows, width), lambda i, *_: (0, 0, 0))] * len(pieces),
            out_specs=[pl.BlockSpec(shape, lambda i, *_: (0, 0, 0)) for shape in shapes],
        ),
        compiler_params=pltpu.CompilerParams(vmem_limit_bytes=48 * 2**20),
        cost_estimate=pl.CostEstimate(
            flops=0, bytes_accessed=4 * total * rows * width, transcendentals=0
        ),
        name="place_blocks",
    )(places, *pieces)
    return [out.reshape(total * rows, -1) for out in placed]


def normalize(values, gain_vec):
    factor = lax.rsqrt(jnp.mean(values * values, axis=-1, keepdims=True) + EPSILON)
    plain_rows = values * factor
    return (plain_rows, factor, plain_rows * gain_vec)


def norm_backward(grad_normed, plain_rows, factor, gain_vec):
    scaled = grad_normed * gain_vec
    gain_part = jnp.sum(grad_normed * plain_rows, axis=0)
    grad_input = factor * (
        scaled - plain_rows * jnp.mean(scaled * plain_rows, axis=-1, keepdims=True)
    )
    return (gain_part, grad_input)


def matmul(left_side, right_side):
    return jnp.dot(left_side, right_side, preferred_element_type=HIGH)


def matmul_right_t(left_side, right_side):
    return lax.dot_general(
        left_side, right_side, (((1,), (1,)), ((), ())), preferred_element_type=HIGH
    )


def matmul_left_t(left_side, right_side):
    return lax.dot_general(
        left_side, right_side, (((0,), (0,)), ((), ())), preferred_element_type=HIGH
    )


def pad_units(rows):
    extra = -rows.shape[0] % 16
    return jnp.pad(rows, ((0, extra), (0, 0)))


def quarters(count):
    tiles = count // 16
    return [16 * (tiles * i // 4) for i in range(5)]


def diagonal_visible(core, span_rows, key_axis):
    half = span_rows // 2

    def place(axis):
        index = lax.broadcasted_iota(jnp.int32, (span_rows, span_rows), axis)
        flipped = jnp.where(index < half, index + half, index - half)
        return jnp.where(core == 0, index, flipped)

    return place(key_axis) <= place(1 - key_axis)


def forward_kernel(
    place_ref, rank_ref, core_ref, query_ref, key_ref, value_ref, mixed_ref, lse_ref, score_ref
):
    half_rows = query_ref.shape[1]
    span_rows = 2 * half_rows
    heads = query_ref.shape[2] // HD
    rank = rank_ref[pl.program_id(1)]
    columns = [slice(h * HD, (h + 1) * HD) for h in range(heads)]

    def span(ref, step, h):
        side = place_ref[step] // 4
        start = pl.multiple_of((place_ref[step] % 4) * half_rows, half_rows)
        return ref[side, :, pl.ds(start, half_rows), columns[h]].reshape(span_rows, HD)

    def block_scores(step, h):
        query = query_ref[:, :, columns[h]].reshape(span_rows, HD)
        return matmul_right_t(query, span(key_ref, step, h)) * (SCORE_SCALE * LOG2E)

    def fold(values, operation):
        folded = values[:, :HD]
        for at in range(HD, span_rows, HD):
            folded = operation(folded, values[:, at : at + HD])
        return folded

    def score_step(step, maxima, count):
        new = []
        for h in range(heads):
            top = maxima[h]
            for at in range(count):
                scores = block_scores(step + at, h)
                score_ref[h, step + at] = scores
                top = jnp.maximum(top, fold(scores, jnp.maximum))
            new.append(top)
        return tuple(new)

    maxima = tuple(jnp.full((span_rows, HD), -jnp.inf, HIGH) for _ in range(heads))
    maxima = lax.fori_loop(0, rank // 2, lambda p, m: score_step(2 * p, m, 2), maxima)
    maxima = lax.fori_loop(rank // 2 * 2, rank, lambda p, m: score_step(p, m, 1), maxima)
    visible = diagonal_visible(core_ref[0], span_rows, 1)
    tops = []
    for h in range(heads):
        scores = jnp.where(visible, block_scores(rank, h), -jnp.inf)
        score_ref[h, rank] = scores
        top = jnp.maximum(maxima[h], fold(scores, jnp.maximum))
        tops.append(jnp.max(top, axis=1, keepdims=True))

    def mix_step(step, running, count):
        new = []
        for h in range(heads):
            total, mixed = running[h]
            for at in range(count):
                weights = jnp.exp2(score_ref[h, step + at] - tops[h])
                total = total + fold(weights, jnp.add)
                mixed = mixed + matmul(weights.astype(LOW), span(value_ref, step + at, h))
            new.append((total, mixed))
        return tuple(new)

    zero = jnp.zeros((span_rows, HD), HIGH)
    sums = tuple((zero, zero) for _ in range(heads))
    blocks = rank + 1
    sums = lax.fori_loop(0, blocks // 2, lambda p, r: mix_step(2 * p, r, 2), sums)
    sums = lax.fori_loop(blocks // 2 * 2, blocks, lambda p, r: mix_step(p, r, 1), sums)
    for h in range(heads):
        total = jnp.sum(sums[h][0], axis=1, keepdims=True)
        mixed = (sums[h][1] / total).astype(LOW)
        mixed_ref[:, :, columns[h]] = mixed.reshape(2, half_rows, HD)
        lse = jnp.broadcast_to(tops[h] + jnp.log2(total), (span_rows, HD))
        lse_ref[h] = jnp.transpose(lse)[:8, :]


def backward_kernel(
    place_ref,
    rank_ref,
    core_ref,
    query_ref,
    mixed_ref,
    lse_ref,
    key_ref,
    value_ref,
    weight_ref,
    *refs,
):
    *branch_refs, grad_query_ref, grad_key_ref, grad_value_ref = refs[:-4]
    grad_ref, turned_ref, key_sum_ref, value_sum_ref = refs[-4:]
    heads = query_ref.shape[2] // HD
    half_rows = query_ref.shape[1] // rank_ref.shape[0]
    span_rows = 2 * half_rows
    columns = [slice(h * HD, (h + 1) * HD) for h in range(heads)]
    count = len(branch_refs) // 2
    for core in range(2):
        rows = [ref[...] for ref in branch_refs[core * count : (core + 1) * count]]
        rows = jnp.concatenate(rows, axis=0)
        grad_ref[core] = matmul_right_t(rows, weight_ref[...]).astype(LOW)
    for h in range(heads):
        for at in range(turned_ref.shape[1]):
            rows = slice(at % 4 * half_rows, (at % 4 + 1) * half_rows)
            keys = key_ref[at // 4, :, rows, columns[h]].reshape(span_rows, HD)
            turned_ref[h, at] = jnp.transpose(keys)
    key_sum_ref[...] = jnp.zeros_like(key_sum_ref)
    value_sum_ref[...] = jnp.zeros_like(value_sum_ref)

    def query_span(at, carry):
        here = pl.ds(pl.multiple_of(at * half_rows, half_rows), half_rows)
        lanes = pl.ds(pl.multiple_of(at * span_rows, span_rows), span_rows)
        rank = rank_ref[at]

        def own(ref, h):
            return ref[:, here, columns[h]].reshape(span_rows, HD)

        delta = []
        lse = []
        for h in range(heads):
            product = own(grad_ref, h).astype(HIGH) * own(mixed_ref, h).astype(HIGH)
            delta.append(jnp.sum(jnp.transpose(product), axis=0, keepdims=True))
            lse.append(lse_ref[h, :1, lanes])

        def block(step, grad_query, visible):
            side = place_ref[step] // 4
            start = pl.multiple_of((place_ref[step] % 4) * half_rows, half_rows)
            there = pl.ds(start, half_rows)
            new = []
            for h in range(heads):
                query = own(query_ref, h)
                grad = own(grad_ref, h)
                keys = key_ref[side, :, there, columns[h]].reshape(span_rows, HD)
                values = value_ref[side, :, there, columns[h]].reshape(span_rows, HD)
                scores = matmul_right_t(keys, query) * (SCORE_SCALE * LOG2E)
                weights = jnp.exp2(scores - lse[h])
                if visible is not None:
                    weights = jnp.where(visible, weights, 0.0)
                grad_weights = matmul_right_t(values, grad)
                grad_scores = (weights * (grad_weights - delta[h])).astype(LOW)
                value_term = matmul(weights.astype(LOW), grad)
                key_term = matmul(grad_scores, query)
                value_sum_ref[side, :, there, columns[h]] += value_term.reshape(2, half_rows, HD)
                key_sum_ref[side, :, there, columns[h]] += key_term.reshape(2, half_rows, HD)
                new.append(grad_query[h] + matmul(turned_ref[h, place_ref[step]], grad_scores))
            return tuple(new)

        start = tuple(jnp.zeros((HD, span_rows), HIGH) for _ in range(heads))
        grad_query = lax.fori_loop(
            0, rank // 2, lambda p, g: block(2 * p + 1, block(2 * p, g, None), None), start
        )
        grad_query = lax.fori_loop(
            rank // 2 * 2, rank, lambda p, g: block(p, g, None), grad_query
        )
        visible = diagonal_visible(core_ref[0], span_rows, 0)
        grad_query = block(rank, grad_query, visible)
        for h in range(heads):
            result = (jnp.transpose(grad_query[h]) * SCORE_SCALE).astype(LOW)
            grad_query_ref[:, here, columns[h]] = result.reshape(2, half_rows, HD)
        return carry

    lax.fori_loop(0, rank_ref.shape[0], query_span, 0)
    grad_key_ref[...] = (key_sum_ref[...] * SCORE_SCALE).astype(LOW)
    grad_value_ref[...] = value_sum_ref[...].astype(LOW)


def heads_at_once(key_rows, features):
    return features // HD if key_rows <= 4096 else 1


def attention_forward(scalars, queries, keys, values):
    rows, features = queries.shape
    key_rows = keys.shape[0]
    own_spans = scalars[1].shape[0]
    half_rows = rows // own_spans // 2
    span_rows = 2 * half_rows
    heads = heads_at_once(key_rows, features)
    width = heads * HD
    pairs = rows * key_rows * features
    sides = key_rows // rows
    own = pl.BlockSpec((2, half_rows, width), lambda h, i, *_: (0, i, h))
    other = pl.BlockSpec((sides, 2, rows // 2, width), lambda h, i, *_: (0, 0, 0, h))
    mixed, lse = pl.pallas_call(
        forward_kernel,
        out_shape=(
            jax.ShapeDtypeStruct((2, rows // 2, features), LOW),
            jax.ShapeDtypeStruct((features // HD, 8, rows), HIGH),
        ),
        grid_spec=pltpu.PrefetchScalarGridSpec(
            num_scalar_prefetch=3,
            grid=(features // width, own_spans),
            in_specs=[own, other, other],
            out_specs=[own, pl.BlockSpec((heads, 8, span_rows), lambda h, i, *_: (h, 0, i))],
            scratch_shapes=[
                pltpu.VMEM((heads, key_rows // span_rows, span_rows, span_rows), HIGH)
            ],
        ),
        compiler_params=pltpu.CompilerParams(vmem_limit_bytes=56 * 2**20),
        cost_estimate=pl.CostEstimate(
            flops=20 * pairs, bytes_accessed=4 * key_rows * features, transcendentals=pairs // 256
        ),
        name="attention_forward",
    )(
        *scalars,
        queries.reshape(2, rows // 2, features),
        keys.reshape(sides, 2, rows // 2, features),
        values.reshape(sides, 2, rows // 2, features),
    )
    return mixed.reshape(rows, features), lse


def attention_backward(scalars, queries, mixed, lse, keys, values, weight_out, branch_blocks):
    rows, features = queries.shape
    key_rows = keys.shape[0]
    heads = heads_at_once(key_rows, features)
    width = heads * HD
    pairs = rows * key_rows * features
    sides = key_rows // rows
    own_shape = (2, rows // 2, features)
    key_shape = (sides, 2, rows // 2, features)
    once = pl.Buffered(1)
    own_part, key_part = own_shape[:2] + (width,), key_shape[:3] + (width,)
    own = pl.BlockSpec(own_part, lambda h, *_: (0, 0, h))
    other = pl.BlockSpec(key_part, lambda h, *_: (0, 0, 0, h))
    other_in = pl.BlockSpec(key_part, lambda h, *_: (0, 0, 0, h), pipeline_mode=once)
    block = pl.BlockSpec(branch_blocks[0].shape, lambda h, *_: (0, 0), pipeline_mode=once)
    grad_queries, grad_keys, grad_values = pl.pallas_call(
        backward_kernel,
        out_shape=(
            jax.ShapeDtypeStruct(own_shape, LOW),
            jax.ShapeDtypeStruct(key_shape, LOW),
            jax.ShapeDtypeStruct(key_shape, LOW),
        ),
        grid_spec=pltpu.PrefetchScalarGridSpec(
            num_scalar_prefetch=3,
            grid=(features // width,),
            in_specs=[
                own,
                own,
                pl.BlockSpec((heads, 8, rows), lambda h, *_: (h, 0, 0)),
                other_in,
                other_in,
                pl.BlockSpec((width, weight_out.shape[1]), lambda h, *_: (h, 0)),
            ]
            + [block] * len(branch_blocks),
            out_specs=[own, other, other],
            scratch_shapes=[
                pltpu.VMEM(own_part, LOW),
                pltpu.VMEM((heads, 4 * sides, HD, key_rows // (4 * sides)), LOW),
            ]
            + [pltpu.VMEM(key_part, HIGH)] * 2,
        ),
        compiler_params=pltpu.CompilerParams(vmem_limit_bytes=56 * 2**20),
        cost_estimate=pl.CostEstimate(
            flops=120 * pairs, bytes_accessed=8 * key_rows * features, transcendentals=pairs // 256
        ),
        name="attention_backward",
    )(
        *scalars,
        queries.reshape(own_shape),
        mixed.reshape(own_shape),
        lse,
        keys.reshape(key_shape),
        values.reshape(key_shape),
        weight_out,
        *branch_blocks,
    )
    return (
        grad_queries.reshape(rows, features),
        grad_keys.reshape(key_rows, features),
        grad_values.reshape(key_rows, features),
    )


def per_device(
    states,
    shared_kv,
    norm_gain,
    kv_gain,
    ffn_gain,
    query_weight,
    key_weight,
    value_weight,
    out_weight,
    gate_weight,
    up_weight,
    down_weight,
    span_order,
    grad_output,
):
    z, x, y, c = (lax.axis_index(name) for name in ALL)
    size_x = lax.axis_size("x")
    sides = 2 * size_x
    rows_local, width_model = states.shape
    weight_rows = query_weight.shape[0]
    units_local = gate_weight.shape[1]
    own_width = width_model // 8

    side = jnp.arange(sides, dtype=jnp.int32)
    side_owner = jnp.mod(x - side // 2, size_x) * 2 + jnp.bitwise_xor(y, side % 2)
    back = jnp.mod(jnp.arange(4, dtype=jnp.int32) + 1, 4)
    back_owner = jnp.mod(z - back, 4)

    ticks = Ticks()

    block = jnp.arange(8 * sides, dtype=jnp.int32)
    block_half, block_side = block // (4 * sides), block // 4 % sides
    block_back = 2 * block_half + block // 2 % 2
    block_place = (
        (jnp.mod(z - block_back, 4) * size_x + jnp.mod(x - block_side // 2, size_x)) * 2
        + jnp.bitwise_xor(y, block_side % 2)
    ) * 2 + jnp.bitwise_xor(c, block % 2)

    state_rows = states.astype(HIGH)
    shared_rows = shared_kv.astype(HIGH)
    plain_kv, factor_kv, normed_kv = normalize(shared_rows, kv_gain)
    plain_one, factor_one, normed_one = normalize(state_rows, norm_gain)
    shared_low = normed_kv.astype(LOW)
    normed_low = normed_one.astype(LOW)

    with jax.named_scope("weight_columns"):
        pair = 2 * own_width
        projections = (key_weight, value_weight, query_weight)

        def cut(start, size, arrays):
            return jnp.concatenate(
                [lax.dynamic_slice_in_dim(v, start, size, 1) for v in arrays], axis=1
            )

        parts = [cut(jnp.mod(z + step, 4) * pair, pair, projections) for step in range(4)]
        over = ticks.tick((parts[1], 1), (parts[2], 2), (parts[3], 3), lock=False)
        columns = []
        for part in [parts[0]] + over:
            arrays = [part[:, i * pair : (i + 1) * pair] for i in range(3)]
            columns.append(cut(c * own_width, own_width, arrays))
            columns.append(hop(cut((1 - c) * own_width, own_width, arrays), "c"))
        columns = jnp.stack(columns)
    with jax.named_scope("shared_rows"):
        out_weight = after(out_weight, over)
        out_task = ticks.add(
            gather_task(out_weight[: weight_rows // 2], out_weight[weight_rows // 2 :]),
            urgent=True,
        )
        weight_task = ticks.add(gather_task(columns[:4], columns[4:]), urgent=True)
        shared_blocks = [shared_low]
        for _ in range(3):
            shared_blocks += ticks.tick((shared_blocks[-1], 1), room=1.2, lock=False)
        group_shared = ticks.join_cores(shared_blocks)
    with jax.named_scope("weight_columns"):
        first, second = ticks.finish(weight_task)[0]
        weight_kv, weight_query = place_blocks(
            first + second, block_place, (2 * own_width, own_width)
        )
    with jax.named_scope("out_weight"):
        whole = jnp.arange(sides, dtype=jnp.int32)
        whole_side = jnp.mod(x - whole // 2, size_x) * 2 + jnp.bitwise_xor(y, whole % 2)
        out_pieces = ticks.finish(out_task)[0]
        out_pieces = jnp.stack([part for pair in zip(*out_pieces) for part in pair])
        out_pieces = jnp.take(
            out_pieces.reshape(sides, weight_rows, width_model), whole_side, axis=0
        ).reshape(2, size_x // 2, 2, weight_rows, width_model)
        out_keep = lax.dynamic_index_in_dim(out_pieces, c, 0, keepdims=False)
        out_give = lax.dynamic_index_in_dim(out_pieces, 1 - c, 0, keepdims=False)
        out_got = hop(out_give, "c")
        weight_out = jnp.where(
            c == 0, jnp.stack([out_keep, out_got], axis=2), jnp.stack([out_got, out_keep], axis=2)
        ).reshape(own_width, width_model)

    with jax.named_scope("keys_values"):
        group_shared = after(group_shared, weight_out)
        keys_own = matmul(group_shared, weight_kv[:, :own_width]).astype(LOW)
        values_own = matmul(group_shared, weight_kv[:, own_width:]).astype(LOW)
        keys_task = ticks.add(gather_task(keys_own, values_own), urgent=True)
    with jax.named_scope("normed_rows"):
        normed_blocks = [normed_low]
        for _ in range(3):
            normed_blocks += ticks.tick((normed_blocks[-1], 1), lock=False)
    with jax.named_scope("normed_rows"):
        group_normed = ticks.join_cores(normed_blocks)
    with jax.named_scope("grad_output_rows"):
        grad_blocks = [grad_output] + ticks.tick((grad_output, 1))
    with jax.named_scope("keys_values"):
        key_pieces, value_pieces = ticks.finish(keys_task)[0]
        keys_all, values_all = jnp.concatenate(key_pieces), jnp.concatenate(value_pieces)
    with jax.named_scope("queries"):
        late_normed = after(group_normed, key_pieces[-1], value_pieces[-1])
        queries = matmul(late_normed, weight_query).astype(LOW)

    span_of = (back_owner[None, :] * sides + side_owner[:, None]).reshape(-1)
    ranks = jnp.take(span_order, span_of)
    spans = span_order.shape[0]
    listed = jnp.arange(spans, dtype=jnp.int32)
    place = jnp.sum(jnp.where(ranks[None, :] == listed[:, None], listed[None, :], 0), axis=1)
    scalars = (place, ranks[:4], c.reshape(1).astype(jnp.int32))

    with jax.named_scope("unit_weights"):
        late = (keys_all, values_all)
        unit_rows = jnp.concatenate(
            [
                pad_units(jnp.transpose(after(gate_weight, *late))),
                pad_units(jnp.transpose(after(up_weight, *late))),
                pad_units(after(down_weight, *late)),
            ],
            axis=0,
        )
        cuts = quarters(unit_rows.shape[0])
        chunks = [unit_rows[cuts[i] : cuts[i + 1]] for i in range(4)]
        unit_tasks = [ticks.add(gather_task(chunks[i], chunks[i + 1])) for i in (0, 2)]
    with jax.named_scope("grad_output_rows"):
        grad_blocks += ticks.tick((grad_blocks[-1], 1), (grad_output, -1))
    mixed, lse = attention_forward(scalars, queries, keys_all, values_all)
    with jax.named_scope("grad_output_rows"):
        group_grad = ticks.join_cores(grad_blocks)
    with jax.named_scope("attention_sum"):
        attention_sum = RowSum(ticks, lambda v: matmul(v, weight_out), [mixed], rows_local)
        residual = state_rows + attention_sum.finish()
    plain_two, factor_two, normed_two = normalize(residual, ffn_gain)
    with jax.named_scope("normed_two_rows"):
        group_in = ticks.gather_rows(normed_two.astype(LOW))
    with jax.named_scope("unit_weights"):
        gathered = [pieces for result in ticks.finish(*unit_tasks) for pieces in result]
        units_padded = unit_rows.shape[0] // 3

        def units_of(which):
            low, high = which * units_padded, (which + 1) * units_padded
            rows = []
            for s in range(sides):
                for i in range(4):
                    start, stop = max(low, cuts[i]), min(high, cuts[i + 1])
                    if start < stop:
                        rows.append(gathered[i][s][start - cuts[i] : stop - cuts[i]])
            return jnp.concatenate(rows, axis=0)

        weight_gate, weight_up, weight_down = (units_of(which) for which in range(3))

    gate_act = matmul_right_t(group_in, weight_gate)
    up_act = matmul_right_t(group_in, weight_up)
    grad_hidden = matmul_right_t(group_grad, weight_down)
    sigmoid = jax.nn.sigmoid(gate_act)
    silu_act = gate_act * sigmoid
    hidden = (silu_act * up_act).astype(LOW)
    grad_gate_act = (
        grad_hidden * up_act * sigmoid * (1.0 + gate_act * (1.0 - sigmoid))
    ).astype(LOW)
    grad_up_act = (grad_hidden * silu_act).astype(LOW)

    def unit_parts(values):
        step = values.shape[0] // sides
        return [values[s * step : (s + 1) * step] for s in range(sides)]

    with jax.named_scope("ffn_grad_sum"):
        ffn_grad_sum = RowSum(
            ticks,
            lambda g, u: matmul(g, weight_gate) + matmul(u, weight_up),
            [grad_gate_act, grad_up_act],
            rows_local,
        )
        unit_terms = []

        def unit_window(left, right, room=1):
            ffn_grad_sum.step(room)
            terms = matmul_left_t(after(left, ffn_grad_sum.sent), right).astype(LOW)
            unit_terms.append(unit_parts(terms))

        def chunk_parts(i):
            parts = []
            for s in range(sides):
                rows = []
                for which in range(3):
                    low = which * units_padded
                    start, stop = max(low, cuts[i]), min(low + units_padded, cuts[i + 1])
                    if start < stop:
                        rows.append(unit_terms[which][s][start - low : stop - low])
                parts.append(jnp.concatenate(rows, axis=0) if rows[1:] else rows[0])
            return parts

        unit_window(grad_gate_act, group_in)
        unit_window(grad_up_act, group_in)
        unit_sum_tasks = [ticks.add(sum_task(chunk_parts(0), chunk_parts(1)))]
        unit_window(hidden, group_grad, room=2)
        unit_sum_tasks.append(ticks.add(sum_task(chunk_parts(2), chunk_parts(3))))
        grad_ffn = ffn_grad_sum.finish()

    gain_two, grad_norm_two = norm_backward(grad_ffn, plain_two, factor_two, ffn_gain)
    grad_residual = grad_output.astype(HIGH) + grad_norm_two
    with jax.named_scope("branch_rows"):
        branch_moves = ticks.gather_parts(grad_residual.astype(LOW))
        sent = next(branch_moves)
        lined = jnp.arange(8, dtype=jnp.int32)
        order = jnp.bitwise_xor(c, lined % 2) * 4 + jnp.mod(z - lined // 2 - 1, 4)
        late_hidden = after(hidden, sent).reshape(8, rows_local, -1)
        late_hidden = jnp.take(late_hidden, order, axis=0).reshape(8 * rows_local, -1)
        terms = matmul(after(late_hidden, next(branch_moves)), weight_down).astype(LOW)
        next(branch_moves)
        branch_both = next(branch_moves)
    with jax.named_scope("ffn_sum"):
        branch = lax.psum_scatter(
            after(terms, ticks.over_z), ("z", "c"), scatter_dimension=0, tiled=True
        )
        output = (residual + branch.astype(HIGH)).astype(LOW)
    with jax.named_scope("unit_weight_sums"):
        ticks.tick(room=2, lock=False)
    grad_queries, key_terms, value_terms = attention_backward(
        scalars, queries, mixed, lse, keys_all, values_all, weight_out, branch_both
    )

    def side_parts(values, k):
        count = values.shape[0] // (2 * sides)
        return [
            lax.dynamic_slice_in_dim(
                values,
                (2 * jnp.bitwise_xor(jnp.bitwise_xor(side_owner[s], z), 2 * k) + k) * count,
                count,
                0,
            )
            for s in range(sides)
        ]

    def chunk_sums(values):
        return sum_task(side_parts(values, 0), side_parts(values, 1))

    to_layout = [
        [
            (
                ((za * size_x + xa) * 2 + ya) * 2 + ca,
                (2 * ((2 * xa + ya) ^ za ^ (2 * (ca ^ flip))) + (ca ^ flip)) * 4 + za,
            )
            for za in range(4)
            for xa in range(size_x)
            for ya in range(2)
            for ca in range(2)
        ]
        for flip in range(2)
    ]

    def layout(summed):
        sent = jnp.where(c == 0, summed[0], summed[1]), jnp.where(c == 0, summed[1], summed[0])
        got = [lax.ppermute(sent[flip], ALL, to_layout[flip]) for flip in range(2)]
        even = x % 2 == 0
        first = jnp.where(even, got[0], got[1]).astype(HIGH)
        second = jnp.where(even, got[1], got[0]).astype(HIGH)
        return [
            jnp.concatenate([part[:, at : at + own_width] for part in (first, second)], axis=1)
            for at in range(0, first.shape[1], own_width)
        ]

    with jax.named_scope("grad_keys_values"):
        keys_task = ticks.add(
            sum_task(unit_parts(key_terms), unit_parts(value_terms)), urgent=True
        )
    with jax.named_scope("normed_sum"):
        normed_sum = RowSum(
            ticks, lambda v: matmul_right_t(v, weight_query), [grad_queries], rows_local
        )
        normed_sum.step()
        sent = normed_sum.sent
    with jax.named_scope("query_weight_sum"):
        query_terms = matmul_left_t(after(group_normed, sent), grad_queries).astype(LOW)
    with jax.named_scope("out_weight_sum"):
        group_branch = jnp.concatenate(after(branch_both, sent), axis=0)
        out_terms = matmul_left_t(group_branch, mixed).astype(LOW)
    with jax.named_scope("normed_sum"):
        grad_normed = normed_sum.finish()
    with jax.named_scope("grad_keys_values"):
        grad_keys, grad_values = ticks.finish(keys_task)[0]
    with jax.named_scope("query_out_weight_sum"):
        query_out_task = ticks.add(
            chunk_sums(jnp.concatenate([query_terms, out_terms], axis=1))
        )
    with jax.named_scope("shared_sum"):
        weight_key, weight_value = weight_kv[:, :own_width], weight_kv[:, own_width:]
        shared_sum = RowSum(
            ticks,
            lambda k, v: matmul_right_t(k, weight_key) + matmul_right_t(v, weight_value),
            [grad_keys, grad_values],
            rows_local,
        )
        shared_sum.total = after(shared_sum.total, branch)
        shared_sum.step()
        sent = shared_sum.sent
    with jax.named_scope("key_value_weight_sum"):
        grad_kv = jnp.concatenate(after((grad_keys, grad_values), sent), axis=1)
        kv_terms = matmul_left_t(group_shared, grad_kv).astype(LOW)
        kv_task = ticks.add(chunk_sums(kv_terms))
    with jax.named_scope("shared_sum"):
        grad_shared_normed = shared_sum.finish()
    with jax.named_scope("weight_layout"):
        (query_out_sum,) = ticks.finish(query_out_task)
        grad_query, grad_out = layout(after(query_out_sum, grad_shared_normed))
        (kv_sum,) = ticks.finish(kv_task)
        grad_key, grad_value = layout(kv_sum)
        grad_out = jnp.transpose(grad_out)
    with jax.named_scope("unit_weight_sums"):
        sums = [part for result in ticks.finish(*unit_sum_tasks) for part in result]
        whole = jnp.concatenate(sums, axis=0).astype(HIGH)
        grad_gate, grad_up, grad_down = (
            whole[w * units_padded : w * units_padded + units_local] for w in range(3)
        )
        grad_gate, grad_up = jnp.transpose(grad_gate), jnp.transpose(grad_up)

    grad_normed = after(grad_normed, sent)
    gain_one, grad_in_one = norm_backward(grad_normed, plain_one, factor_one, norm_gain)
    gain_kv, grad_in_kv = norm_backward(grad_shared_normed, plain_kv, factor_kv, kv_gain)
    grad_states = (grad_residual + grad_in_one).astype(LOW)
    grad_shared = grad_in_kv.astype(LOW)

    devices = 8 * sides
    gain_terms = jnp.stack([g.reshape(devices, -1) for g in (gain_one, gain_kv, gain_two)], axis=1)
    gain_terms = lax.all_to_all(
        gain_terms.reshape(devices, -1), ALL, split_axis=0, concat_axis=0, tiled=True
    )
    gain_sums = jnp.sum(gain_terms, axis=0).reshape(3, -1)
    return (
        output,
        grad_states,
        grad_shared,
        gain_sums[0],
        gain_sums[1],
        gain_sums[2],
        grad_query,
        grad_key,
        grad_value,
        grad_out,
        grad_gate,
        grad_up,
        grad_down,
    )


def solution(mesh):
    size_ctx, size_head = mesh.shape["ctx"], mesh.shape["head"]
    fine = Mesh(mesh.devices.reshape(4, size_ctx // 4, 2, size_head // 2), ALL)
    rows = P(ALL, None)
    ctx, head = ("z", "x"), ("y", "c")
    in_specs = (
        rows,
        rows,
        P(),
        P(),
        P(),
        rows,
        rows,
        rows,
        rows,
        P(None, ALL),
        P(None, ALL),
        rows,
        P(),
        rows,
    )
    out_specs = (
        rows,
        rows,
        rows,
        P(ALL),
        P(ALL),
        P(ALL),
        P(ctx, head),
        P(ctx, head),
        P(ctx, head),
        P(head, ctx),
        P(None, ALL),
        P(None, ALL),
        rows,
    )
    return jax.shard_map(
        per_device, mesh=fine, in_specs=in_specs, out_specs=out_specs, check_vma=False
    )
```

```python
import math

import jax
import jax.numpy as jnp
from jax import lax
from jax.experimental import pallas as pl
from jax.experimental.pallas import tpu as pltpu
from jax.sharding import Mesh, PartitionSpec as P

HD = 128
EPSILON = 1e-06
LOW = jnp.bfloat16
HIGH = jnp.float32
LOG2E = math.log2(math.e)
SCORE_SCALE = HD ** (-0.5)
ALL = ("z", "x", "y", "c")
RUNS = (8, 4, 2, 1)


def add_low(first, second):
    return (first.astype(HIGH) + second.astype(HIGH)).astype(LOW)


def after(values, *earlier):
    return lax.optimization_barrier((values, earlier))[0]


def hop(values, axis, steps=1):
    size = lax.axis_size(axis)
    return lax.ppermute(values, axis, [(i, (i + steps) % size) for i in range(size)])


def both_cores(blocks):
    blocks = blocks[1:] + blocks[:1]
    return blocks + [hop(block, "c") for block in blocks]


def gather_task(first, second):
    size = lax.axis_size("x")
    firsts, seconds, first_over, second_over = [first], [second], [], []
    for stage in range(size):
        wanted = [("y", firsts[stage], first_over)]
        if stage == 0:
            wanted.append(("y", second, second_over))
        if stage < size - 1:
            wanted += [("x", firsts[stage], firsts), ("x", seconds[stage], seconds)]
        if stage:
            wanted.append(("x", second_over[stage - 1], second_over))
        yield wanted
    return (
        [piece for pair in zip(firsts, first_over) for piece in pair],
        [piece for pair in zip(seconds, second_over) for piece in pair],
    )


def sum_task(first, second):
    size = lax.axis_size("x")
    got, far, near = [], [], []
    over = [[] for _ in range(size)]
    far_total, near_total = second[3], second[2]
    for step in range(1, size):
        wanted = [("x", far_total, far), ("x", near_total, near)]
        if step == 1:
            wanted += [("y", first[2 * s + 1], over[s]) for s in range(1, size)]
            wanted.append(("y", first[1], over[0]))
        yield wanted
        at = 2 * ((step + 1) % size)
        far_total, near_total = add_low(second[at + 1], far[-1]), add_low(second[at], near[-1])
    merged = [add_low(first[2 * s], over[s][0]) for s in range(size)]
    total = merged[1]
    for step in range(1, size):
        wanted = [("x", total, got)]
        if step == 1:
            wanted.append(("y", far_total, far))
        yield wanted
        total = add_low(merged[(step + 1) % size], got[-1])
    return total, add_low(near_total, far[-1])


class Ticks:
    BYTES = 9 * 2**16

    def __init__(self):
        self.tasks = []
        self.over_z = ()
        self.sides = [(), ()]
        self.sent = None
        self.held = []
        self.places = []

    def add(self, task, urgent=False):
        entry = {"task": task, "wanted": None, "open": 0, "result": None, "urgent": urgent}
        self.tasks.insert(0 if urgent else len(self.tasks), entry)
        self.advance(entry)
        return entry

    def advance(self, entry):
        try:
            entry["wanted"] = list(next(entry["task"]))
            entry["open"] = len(entry["wanted"])
        except StopIteration as stop:
            entry["result"] = stop.value
            self.tasks.remove(entry)

    def tick(self, *moves, room=1, lock=True):
        got = []
        for values, steps in moves:
            self.sent = after(values, self.over_z, self.sides[-2])
            got.append(hop(self.sent, "z", steps))
        self.release(*([self.sent] if moves else []))
        left = {"x": room * self.BYTES, "y": room * self.BYTES}
        before = self.over_z if lock else ()
        arrived = []
        finished = []
        for entry in self.tasks:
            later = []
            for axis, values, into in entry["wanted"]:
                if left[axis] >= min(values.nbytes, self.BYTES):
                    left[axis] -= values.nbytes
                    into.append(hop(after(values, self.sides[-1], before), axis))
                    if not entry["urgent"]:
                        self.places.append((into, len(into) - 1))
                    arrived.append(into[-1])
                    entry["open"] -= 1
                else:
                    later.append((axis, values, into))
            entry["wanted"] = later
            if not entry["open"]:
                finished.append(entry)
        self.over_z = tuple(got) or self.over_z
        self.sides = self.sides[-1:] + [tuple(arrived)]
        for entry in finished:
            if entry["urgent"]:
                self.advance(entry)
            else:
                self.held.append(entry)
        return got

    def release(self, *earlier):
        if earlier:
            for into, at in self.places:
                into[at] = after(into[at], earlier)
        held, self.held, self.places = self.held, [], []
        for entry in held:
            self.tasks.remove(entry)
            self.tasks.append(entry)
            self.advance(entry)

    def finish(self, *entries):
        self.release()
        while any(entry["result"] is None for entry in entries):
            self.tick()
            self.release()
        return [entry["result"] for entry in entries]

    def gather_parts(self, rows):
        blocks = [rows]
        for _ in range(1, lax.axis_size("z")):
            blocks += self.tick((blocks[-1], 1))
            yield self.sent
        yield both_cores(blocks)

    def gather_rows(self, rows):
        *_, blocks = self.gather_parts(rows)
        return jnp.concatenate(blocks, axis=0)

    def join_cores(self, blocks):
        return jnp.concatenate(both_cores(blocks), axis=0)


class RowSum:
    def __init__(self, ticks, terms_of, inputs, rows_local):
        self.ticks = ticks
        self.rows = rows_local
        self.half = inputs[0].shape[0] // 2
        self.terms_of = terms_of
        self.inputs = tuple(inputs)
        self.count = 0
        self.total = self.terms(self.inputs, 0).astype(LOW)

    def terms(self, inputs, block):
        near, far = block * self.rows, self.half + block * self.rows
        far_terms = self.terms_of(*(v[far : far + self.rows] for v in inputs))
        got = hop(far_terms.astype(LOW), "c")
        return self.terms_of(*(v[near : near + self.rows] for v in inputs)) + got.astype(HIGH)

    def step(self, room=1):
        (got,) = self.ticks.tick((self.total, 1), room=room)
        self.sent = self.ticks.sent
        self.count += 1
        terms = lax.optimization_barrier(self.terms(after(self.inputs, self.sent), self.count))
        self.total = terms + got.astype(HIGH)
        if self.count < 3:
            self.total = self.total.astype(LOW)

    def finish(self, room=1):
        while self.count < 3:
            self.step(room)
        return self.total


def place_blocks(pieces, places, widths):
    count, rows, width = pieces[0].shape
    total = len(pieces) * count

    def kernel(place_ref, *refs):
        ins, outs = refs[: len(pieces)], refs[len(pieces) :]
        for at in range(total):
            start = 0
            for out, size in zip(outs, widths):
                out[place_ref[at]] = ins[at // count][at % count, :, start : start + size]
                start += size

    shapes = [(total, rows, size) for size in widths]
    placed = pl.pallas_call(
        kernel,
        out_shape=[jax.ShapeDtypeStruct(shape, pieces[0].dtype) for shape in shapes],
        grid_spec=pltpu.PrefetchScalarGridSpec(
            num_scalar_prefetch=1,
            grid=(1,),
            in_specs=[pl.BlockSpec((count, rows, width), lambda i, *_: (0, 0, 0))] * len(pieces),
            out_specs=[pl.BlockSpec(shape, lambda i, *_: (0, 0, 0)) for shape in shapes],
        ),
        compiler_params=pltpu.CompilerParams(vmem_limit_bytes=48 * 2**20),
        cost_estimate=pl.CostEstimate(
            flops=0, bytes_accessed=4 * total * rows * width, transcendentals=0
        ),
        name="place_blocks",
    )(places, *pieces)
    return [out.reshape(total * rows, -1) for out in placed]


def normalize(values, gain_vec):
    factor = lax.rsqrt(jnp.mean(values * values, axis=-1, keepdims=True) + EPSILON)
    plain_rows = values * factor
    return (plain_rows, factor, plain_rows * gain_vec)


def norm_backward(grad_normed, plain_rows, factor, gain_vec):
    scaled = grad_normed * gain_vec
    gain_part = jnp.sum(grad_normed * plain_rows, axis=0)
    grad_input = factor * (
        scaled - plain_rows * jnp.mean(scaled * plain_rows, axis=-1, keepdims=True)
    )
    return (gain_part, grad_input)


def matmul(left_side, right_side):
    return jnp.dot(left_side, right_side, preferred_element_type=HIGH)


def matmul_right_t(left_side, right_side):
    return lax.dot_general(
        left_side, right_side, (((1,), (1,)), ((), ())), preferred_element_type=HIGH
    )


def matmul_left_t(left_side, right_side):
    return lax.dot_general(
        left_side, right_side, (((0,), (0,)), ((), ())), preferred_element_type=HIGH
    )


def pad_units(rows):
    extra = -rows.shape[0] % 16
    return jnp.pad(rows, ((0, extra), (0, 0)))


def quarters(count):
    tiles = count // 16
    return [16 * (tiles * i // 4) for i in range(5)]


def diagonal_visible(core, span_rows, key_axis):
    half = span_rows // 2

    def place(axis):
        index = lax.broadcasted_iota(jnp.int32, (span_rows, span_rows), axis)
        flipped = jnp.where(index < half, index + half, index - half)
        return jnp.where(core == 0, index, flipped)

    return place(key_axis) <= place(1 - key_axis)


def in_runs(count, step, carry):
    done = 0
    for run in RUNS:
        stop = count // run * run
        first = done

        def body(at, carry, run=run, first=first):
            return step(first + run * at, carry, run)

        carry = lax.fori_loop(0, (stop - done) // run, body, carry)
        done = stop
    return carry


def forward_kernel(
    place_ref, rank_ref, core_ref, query_ref, key_ref, value_ref, mixed_ref, lse_ref, score_ref
):
    half_rows = query_ref.shape[1]
    span_rows = 2 * half_rows
    heads = query_ref.shape[2] // HD
    rank = rank_ref[pl.program_id(1)]
    columns = [slice(h * HD, (h + 1) * HD) for h in range(heads)]

    def span(ref, step, h):
        side = place_ref[step] // 4
        start = pl.multiple_of((place_ref[step] % 4) * half_rows, half_rows)
        return ref[side, :, pl.ds(start, half_rows), columns[h]].reshape(span_rows, HD)

    def block_scores(step, h):
        query = query_ref[:, :, columns[h]].reshape(span_rows, HD)
        return matmul_right_t(query, span(key_ref, step, h)) * (SCORE_SCALE * LOG2E)

    def fold(values, operation):
        folded = values[:, :HD]
        for at in range(HD, span_rows, HD):
            folded = operation(folded, values[:, at : at + HD])
        return folded

    def score_step(step, maxima, count):
        new = []
        for h in range(heads):
            top = maxima[h]
            for at in range(count):
                scores = block_scores(step + at, h)
                score_ref[h, step + at] = scores
                top = jnp.maximum(top, fold(scores, jnp.maximum))
            new.append(top)
        return tuple(new)

    maxima = tuple(jnp.full((span_rows, HD), -jnp.inf, HIGH) for _ in range(heads))
    maxima = in_runs(rank, score_step, maxima)
    visible = diagonal_visible(core_ref[0], span_rows, 1)
    tops = []
    for h in range(heads):
        scores = jnp.where(visible, block_scores(rank, h), -jnp.inf)
        score_ref[h, rank] = scores
        top = jnp.maximum(maxima[h], fold(scores, jnp.maximum))
        tops.append(jnp.max(top, axis=1, keepdims=True))

    def mix_step(step, running, count):
        new = []
        for h in range(heads):
            total, mixed = running[h]
            for at in range(count):
                weights = jnp.exp2(score_ref[h, step + at] - tops[h])
                total = total + fold(weights, jnp.add)
                mixed = mixed + matmul(weights.astype(LOW), span(value_ref, step + at, h))
            new.append((total, mixed))
        return tuple(new)

    zero = jnp.zeros((span_rows, HD), HIGH)
    sums = tuple((zero, zero) for _ in range(heads))
    blocks = rank + 1
    sums = in_runs(blocks, mix_step, sums)
    for h in range(heads):
        total = jnp.sum(sums[h][0], axis=1, keepdims=True)
        mixed = (sums[h][1] / total).astype(LOW)
        mixed_ref[:, :, columns[h]] = mixed.reshape(2, half_rows, HD)
        lse = jnp.broadcast_to(tops[h] + jnp.log2(total), (span_rows, HD))
        lse_ref[h] = jnp.transpose(lse)[:8, :]


def backward_kernel(
    place_ref,
    rank_ref,
    core_ref,
    query_ref,
    mixed_ref,
    lse_ref,
    key_ref,
    value_ref,
    weight_ref,
    *refs,
):
    *branch_refs, grad_query_ref, grad_key_ref, grad_value_ref = refs[:-4]
    grad_ref, turned_ref, key_sum_ref, value_sum_ref = refs[-4:]
    heads = query_ref.shape[2] // HD
    half_rows = query_ref.shape[1] // rank_ref.shape[0]
    span_rows = 2 * half_rows
    columns = [slice(h * HD, (h + 1) * HD) for h in range(heads)]
    count = len(branch_refs) // 2
    for core in range(2):
        rows = [ref[...] for ref in branch_refs[core * count : (core + 1) * count]]
        rows = jnp.concatenate(rows, axis=0)
        grad_ref[core] = matmul_right_t(rows, weight_ref[...]).astype(LOW)
    for h in range(heads):
        for at in range(turned_ref.shape[1]):
            rows = slice(at % 4 * half_rows, (at % 4 + 1) * half_rows)
            keys = key_ref[at // 4, :, rows, columns[h]].reshape(span_rows, HD)
            turned_ref[h, at] = jnp.transpose(keys)
    key_sum_ref[...] = jnp.zeros_like(key_sum_ref)
    value_sum_ref[...] = jnp.zeros_like(value_sum_ref)

    def query_span(at, carry):
        here = pl.ds(pl.multiple_of(at * half_rows, half_rows), half_rows)
        lanes = pl.ds(pl.multiple_of(at * span_rows, span_rows), span_rows)
        rank = rank_ref[at]

        def own(ref, h):
            return ref[:, here, columns[h]].reshape(span_rows, HD)

        delta = []
        lse = []
        for h in range(heads):
            product = own(grad_ref, h).astype(HIGH) * own(mixed_ref, h).astype(HIGH)
            delta.append(jnp.sum(jnp.transpose(product), axis=0, keepdims=True))
            lse.append(lse_ref[h, :1, lanes])

        def block(step, grad_query, visible):
            side = place_ref[step] // 4
            start = pl.multiple_of((place_ref[step] % 4) * half_rows, half_rows)
            there = pl.ds(start, half_rows)
            new = []
            for h in range(heads):
                query = own(query_ref, h)
                grad = own(grad_ref, h)
                keys = key_ref[side, :, there, columns[h]].reshape(span_rows, HD)
                values = value_ref[side, :, there, columns[h]].reshape(span_rows, HD)
                scores = matmul_right_t(keys, query) * (SCORE_SCALE * LOG2E)
                weights = jnp.exp2(scores - lse[h])
                if visible is not None:
                    weights = jnp.where(visible, weights, 0.0)
                grad_weights = matmul_right_t(values, grad)
                grad_scores = (weights * (grad_weights - delta[h])).astype(LOW)
                value_term = matmul(weights.astype(LOW), grad)
                key_term = matmul(grad_scores, query)
                value_sum_ref[side, :, there, columns[h]] += value_term.reshape(2, half_rows, HD)
                key_sum_ref[side, :, there, columns[h]] += key_term.reshape(2, half_rows, HD)
                new.append(grad_query[h] + matmul(turned_ref[h, place_ref[step]], grad_scores))
            return tuple(new)

        start = tuple(jnp.zeros((HD, span_rows), HIGH) for _ in range(heads))
        def blocks(first, grad_query, count):
            for more in range(count):
                grad_query = block(first + more, grad_query, None)
            return grad_query

        grad_query = in_runs(rank, blocks, start)
        visible = diagonal_visible(core_ref[0], span_rows, 0)
        grad_query = block(rank, grad_query, visible)
        for h in range(heads):
            result = (jnp.transpose(grad_query[h]) * SCORE_SCALE).astype(LOW)
            grad_query_ref[:, here, columns[h]] = result.reshape(2, half_rows, HD)
        return carry

    lax.fori_loop(0, rank_ref.shape[0], query_span, 0)
    grad_key_ref[...] = (key_sum_ref[...] * SCORE_SCALE).astype(LOW)
    grad_value_ref[...] = value_sum_ref[...].astype(LOW)


def heads_at_once(key_rows, features):
    return features // HD if key_rows <= 4096 else 1


def attention_forward(scalars, queries, keys, values):
    rows, features = queries.shape
    key_rows = keys.shape[0]
    own_spans = scalars[1].shape[0]
    half_rows = rows // own_spans // 2
    span_rows = 2 * half_rows
    heads = heads_at_once(key_rows, features)
    width = heads * HD
    pairs = rows * key_rows * features
    sides = key_rows // rows
    own = pl.BlockSpec((2, half_rows, width), lambda h, i, *_: (0, i, h))
    other = pl.BlockSpec((sides, 2, rows // 2, width), lambda h, i, *_: (0, 0, 0, h))
    mixed, lse = pl.pallas_call(
        forward_kernel,
        out_shape=(
            jax.ShapeDtypeStruct((2, rows // 2, features), LOW),
            jax.ShapeDtypeStruct((features // HD, 8, rows), HIGH),
        ),
        grid_spec=pltpu.PrefetchScalarGridSpec(
            num_scalar_prefetch=3,
            grid=(features // width, own_spans),
            in_specs=[own, other, other],
            out_specs=[own, pl.BlockSpec((heads, 8, span_rows), lambda h, i, *_: (h, 0, i))],
            scratch_shapes=[
                pltpu.VMEM((heads, key_rows // span_rows, span_rows, span_rows), HIGH)
            ],
        ),
        compiler_params=pltpu.CompilerParams(vmem_limit_bytes=56 * 2**20),
        cost_estimate=pl.CostEstimate(
            flops=20 * pairs, bytes_accessed=4 * key_rows * features, transcendentals=pairs // 256
        ),
        name="attention_forward",
    )(
        *scalars,
        queries.reshape(2, rows // 2, features),
        keys.reshape(sides, 2, rows // 2, features),
        values.reshape(sides, 2, rows // 2, features),
    )
    return mixed.reshape(rows, features), lse


def attention_backward(scalars, queries, mixed, lse, keys, values, weight_out, branch_blocks):
    rows, features = queries.shape
    key_rows = keys.shape[0]
    heads = heads_at_once(key_rows, features)
    width = heads * HD
    pairs = rows * key_rows * features
    sides = key_rows // rows
    own_shape = (2, rows // 2, features)
    key_shape = (sides, 2, rows // 2, features)
    once = pl.Buffered(1)
    own_part, key_part = own_shape[:2] + (width,), key_shape[:3] + (width,)
    own = pl.BlockSpec(own_part, lambda h, *_: (0, 0, h))
    other = pl.BlockSpec(key_part, lambda h, *_: (0, 0, 0, h))
    other_in = pl.BlockSpec(key_part, lambda h, *_: (0, 0, 0, h), pipeline_mode=once)
    block = pl.BlockSpec(branch_blocks[0].shape, lambda h, *_: (0, 0), pipeline_mode=once)
    grad_queries, grad_keys, grad_values = pl.pallas_call(
        backward_kernel,
        out_shape=(
            jax.ShapeDtypeStruct(own_shape, LOW),
            jax.ShapeDtypeStruct(key_shape, LOW),
            jax.ShapeDtypeStruct(key_shape, LOW),
        ),
        grid_spec=pltpu.PrefetchScalarGridSpec(
            num_scalar_prefetch=3,
            grid=(features // width,),
            in_specs=[
                own,
                own,
                pl.BlockSpec((heads, 8, rows), lambda h, *_: (h, 0, 0)),
                other_in,
                other_in,
                pl.BlockSpec((width, weight_out.shape[1]), lambda h, *_: (h, 0)),
            ]
            + [block] * len(branch_blocks),
            out_specs=[own, other, other],
            scratch_shapes=[
                pltpu.VMEM(own_part, LOW),
                pltpu.VMEM((heads, 4 * sides, HD, key_rows // (4 * sides)), LOW),
            ]
            + [pltpu.VMEM(key_part, HIGH)] * 2,
        ),
        compiler_params=pltpu.CompilerParams(vmem_limit_bytes=56 * 2**20),
        cost_estimate=pl.CostEstimate(
            flops=120 * pairs, bytes_accessed=8 * key_rows * features, transcendentals=pairs // 256
        ),
        name="attention_backward",
    )(
        *scalars,
        queries.reshape(own_shape),
        mixed.reshape(own_shape),
        lse,
        keys.reshape(key_shape),
        values.reshape(key_shape),
        weight_out,
        *branch_blocks,
    )
    return (
        grad_queries.reshape(rows, features),
        grad_keys.reshape(key_rows, features),
        grad_values.reshape(key_rows, features),
    )


def per_device(
    states,
    shared_kv,
    norm_gain,
    kv_gain,
    ffn_gain,
    query_weight,
    key_weight,
    value_weight,
    out_weight,
    gate_weight,
    up_weight,
    down_weight,
    span_order,
    grad_output,
):
    z, x, y, c = (lax.axis_index(name) for name in ALL)
    size_x = lax.axis_size("x")
    sides = 2 * size_x
    rows_local, width_model = states.shape
    weight_rows = query_weight.shape[0]
    units_local = gate_weight.shape[1]
    own_width = width_model // 8

    side = jnp.arange(sides, dtype=jnp.int32)
    side_owner = jnp.mod(x - side // 2, size_x) * 2 + jnp.bitwise_xor(y, side % 2)
    back = jnp.mod(jnp.arange(4, dtype=jnp.int32) + 1, 4)
    back_owner = jnp.mod(z - back, 4)

    ticks = Ticks()

    block = jnp.arange(8 * sides, dtype=jnp.int32)
    block_half, block_side = block // (4 * sides), block // 4 % sides
    block_back = 2 * block_half + block // 2 % 2
    block_place = (
        (jnp.mod(z - block_back, 4) * size_x + jnp.mod(x - block_side // 2, size_x)) * 2
        + jnp.bitwise_xor(y, block_side % 2)
    ) * 2 + jnp.bitwise_xor(c, block % 2)

    state_rows = states.astype(HIGH)
    shared_rows = shared_kv.astype(HIGH)
    plain_kv, factor_kv, normed_kv = normalize(shared_rows, kv_gain)
    plain_one, factor_one, normed_one = normalize(state_rows, norm_gain)
    shared_low = normed_kv.astype(LOW)
    normed_low = normed_one.astype(LOW)

    with jax.named_scope("weight_columns"):
        pair = 2 * own_width
        projections = (key_weight, value_weight, query_weight)

        def cut(start, size, arrays):
            return jnp.concatenate(
                [lax.dynamic_slice_in_dim(v, start, size, 1) for v in arrays], axis=1
            )

        parts = [cut(jnp.mod(z + step, 4) * pair, pair, projections) for step in range(4)]
        over = ticks.tick((parts[1], 1), (parts[2], 2), (parts[3], 3), lock=False)
        columns = []
        for part in [parts[0]] + over:
            arrays = [part[:, i * pair : (i + 1) * pair] for i in range(3)]
            columns.append(cut(c * own_width, own_width, arrays))
            columns.append(hop(cut((1 - c) * own_width, own_width, arrays), "c"))
        columns = jnp.stack(columns)
    with jax.named_scope("shared_rows"):
        out_weight = after(out_weight, over)
        out_task = ticks.add(
            gather_task(out_weight[: weight_rows // 2], out_weight[weight_rows // 2 :]),
            urgent=True,
        )
        weight_task = ticks.add(gather_task(columns[:4], columns[4:]), urgent=True)
        shared_blocks = [shared_low]
        for _ in range(3):
            shared_blocks += ticks.tick((shared_blocks[-1], 1), room=1.2, lock=False)
        group_shared = ticks.join_cores(shared_blocks)
    with jax.named_scope("weight_columns"):
        first, second = ticks.finish(weight_task)[0]
        weight_kv, weight_query = place_blocks(
            first + second, block_place, (2 * own_width, own_width)
        )
    with jax.named_scope("out_weight"):
        whole = jnp.arange(sides, dtype=jnp.int32)
        whole_side = jnp.mod(x - whole // 2, size_x) * 2 + jnp.bitwise_xor(y, whole % 2)
        out_pieces = ticks.finish(out_task)[0]
        out_pieces = jnp.stack([part for pair in zip(*out_pieces) for part in pair])
        out_pieces = jnp.take(
            out_pieces.reshape(sides, weight_rows, width_model), whole_side, axis=0
        ).reshape(2, size_x // 2, 2, weight_rows, width_model)
        out_keep = lax.dynamic_index_in_dim(out_pieces, c, 0, keepdims=False)
        out_give = lax.dynamic_index_in_dim(out_pieces, 1 - c, 0, keepdims=False)
        out_got = hop(out_give, "c")
        weight_out = jnp.where(
            c == 0, jnp.stack([out_keep, out_got], axis=2), jnp.stack([out_got, out_keep], axis=2)
        ).reshape(own_width, width_model)

    with jax.named_scope("keys_values"):
        group_shared = after(group_shared, weight_out)
        keys_own = matmul(group_shared, weight_kv[:, :own_width]).astype(LOW)
        values_own = matmul(group_shared, weight_kv[:, own_width:]).astype(LOW)
        keys_task = ticks.add(gather_task(keys_own, values_own), urgent=True)
    with jax.named_scope("normed_rows"):
        normed_blocks = [normed_low]
        for _ in range(3):
            normed_blocks += ticks.tick((normed_blocks[-1], 1), lock=False)
    with jax.named_scope("normed_rows"):
        group_normed = ticks.join_cores(normed_blocks)
    with jax.named_scope("grad_output_rows"):
        grad_blocks = [grad_output] + ticks.tick((grad_output, 1))
    with jax.named_scope("keys_values"):
        key_pieces, value_pieces = ticks.finish(keys_task)[0]
        keys_all, values_all = jnp.concatenate(key_pieces), jnp.concatenate(value_pieces)
    with jax.named_scope("queries"):
        late_normed = after(group_normed, key_pieces[-1], value_pieces[-1])
        queries = matmul(late_normed, weight_query).astype(LOW)

    span_of = (back_owner[None, :] * sides + side_owner[:, None]).reshape(-1)
    ranks = jnp.take(span_order, span_of)
    spans = span_order.shape[0]
    listed = jnp.arange(spans, dtype=jnp.int32)
    place = jnp.sum(jnp.where(ranks[None, :] == listed[:, None], listed[None, :], 0), axis=1)
    scalars = (place, ranks[:4], c.reshape(1).astype(jnp.int32))

    with jax.named_scope("unit_weights"):
        late = (keys_all, values_all)
        unit_rows = jnp.concatenate(
            [
                pad_units(jnp.transpose(after(gate_weight, *late))),
                pad_units(jnp.transpose(after(up_weight, *late))),
                pad_units(after(down_weight, *late)),
            ],
            axis=0,
        )
        cuts = quarters(unit_rows.shape[0])
        chunks = [unit_rows[cuts[i] : cuts[i + 1]] for i in range(4)]
        unit_tasks = [ticks.add(gather_task(chunks[i], chunks[i + 1])) for i in (0, 2)]
    with jax.named_scope("grad_output_rows"):
        grad_blocks += ticks.tick((grad_blocks[-1], 1), (grad_output, -1))
    mixed, lse = attention_forward(scalars, queries, keys_all, values_all)
    with jax.named_scope("grad_output_rows"):
        group_grad = ticks.join_cores(grad_blocks)
    with jax.named_scope("attention_sum"):
        attention_sum = RowSum(ticks, lambda v: matmul(v, weight_out), [mixed], rows_local)
        residual = state_rows + attention_sum.finish()
    plain_two, factor_two, normed_two = normalize(residual, ffn_gain)
    with jax.named_scope("normed_two_rows"):
        group_in = ticks.gather_rows(normed_two.astype(LOW))
    with jax.named_scope("unit_weights"):
        gathered = [pieces for result in ticks.finish(*unit_tasks) for pieces in result]
        units_padded = unit_rows.shape[0] // 3

        def units_of(which):
            low, high = which * units_padded, (which + 1) * units_padded
            rows = []
            for s in range(sides):
                for i in range(4):
                    start, stop = max(low, cuts[i]), min(high, cuts[i + 1])
                    if start < stop:
                        rows.append(gathered[i][s][start - cuts[i] : stop - cuts[i]])
            return jnp.concatenate(rows, axis=0)

        weight_gate, weight_up, weight_down = (units_of(which) for which in range(3))

    gate_act = matmul_right_t(group_in, weight_gate)
    up_act = matmul_right_t(group_in, weight_up)
    grad_hidden = matmul_right_t(group_grad, weight_down)
    sigmoid = jax.nn.sigmoid(gate_act)
    silu_act = gate_act * sigmoid
    hidden = (silu_act * up_act).astype(LOW)
    grad_gate_act = (
        grad_hidden * up_act * sigmoid * (1.0 + gate_act * (1.0 - sigmoid))
    ).astype(LOW)
    grad_up_act = (grad_hidden * silu_act).astype(LOW)

    def unit_parts(values):
        step = values.shape[0] // sides
        return [values[s * step : (s + 1) * step] for s in range(sides)]

    with jax.named_scope("ffn_grad_sum"):
        ffn_grad_sum = RowSum(
            ticks,
            lambda g, u: matmul(g, weight_gate) + matmul(u, weight_up),
            [grad_gate_act, grad_up_act],
            rows_local,
        )
        unit_terms = []

        def unit_window(left, right, room=1):
            ffn_grad_sum.step(room)
            terms = matmul_left_t(after(left, ffn_grad_sum.sent), right).astype(LOW)
            unit_terms.append(unit_parts(terms))

        def chunk_parts(i):
            parts = []
            for s in range(sides):
                rows = []
                for which in range(3):
                    low = which * units_padded
                    start, stop = max(low, cuts[i]), min(low + units_padded, cuts[i + 1])
                    if start < stop:
                        rows.append(unit_terms[which][s][start - low : stop - low])
                parts.append(jnp.concatenate(rows, axis=0) if rows[1:] else rows[0])
            return parts

        unit_window(grad_gate_act, group_in)
        unit_window(grad_up_act, group_in)
        unit_sum_tasks = [ticks.add(sum_task(chunk_parts(0), chunk_parts(1)))]
        unit_window(hidden, group_grad, room=2)
        unit_sum_tasks.append(ticks.add(sum_task(chunk_parts(2), chunk_parts(3))))
        grad_ffn = ffn_grad_sum.finish()

    gain_two, grad_norm_two = norm_backward(grad_ffn, plain_two, factor_two, ffn_gain)
    grad_residual = grad_output.astype(HIGH) + grad_norm_two
    with jax.named_scope("branch_rows"):
        branch_moves = ticks.gather_parts(grad_residual.astype(LOW))
        sent = next(branch_moves)
        lined = jnp.arange(8, dtype=jnp.int32)
        order = jnp.bitwise_xor(c, lined % 2) * 4 + jnp.mod(z - lined // 2 - 1, 4)
        late_hidden = after(hidden, sent).reshape(8, rows_local, -1)
        late_hidden = jnp.take(late_hidden, order, axis=0).reshape(8 * rows_local, -1)
        terms = matmul(after(late_hidden, next(branch_moves)), weight_down).astype(LOW)
        next(branch_moves)
        branch_both = next(branch_moves)
    with jax.named_scope("ffn_sum"):
        branch = lax.psum_scatter(
            after(terms, ticks.over_z), ("z", "c"), scatter_dimension=0, tiled=True
        )
        output = (residual + branch.astype(HIGH)).astype(LOW)
    with jax.named_scope("unit_weight_sums"):
        ticks.tick(room=2, lock=False)
    grad_queries, key_terms, value_terms = attention_backward(
        scalars, queries, mixed, lse, keys_all, values_all, weight_out, branch_both
    )

    def side_parts(values, k):
        count = values.shape[0] // (2 * sides)
        return [
            lax.dynamic_slice_in_dim(
                values,
                (2 * jnp.bitwise_xor(jnp.bitwise_xor(side_owner[s], z), 2 * k) + k) * count,
                count,
                0,
            )
            for s in range(sides)
        ]

    def chunk_sums(values):
        return sum_task(side_parts(values, 0), side_parts(values, 1))

    to_layout = [
        [
            (
                ((za * size_x + xa) * 2 + ya) * 2 + ca,
                (2 * ((2 * xa + ya) ^ za ^ (2 * (ca ^ flip))) + (ca ^ flip)) * 4 + za,
            )
            for za in range(4)
            for xa in range(size_x)
            for ya in range(2)
            for ca in range(2)
        ]
        for flip in range(2)
    ]

    def layout(summed):
        sent = jnp.where(c == 0, summed[0], summed[1]), jnp.where(c == 0, summed[1], summed[0])
        got = [lax.ppermute(sent[flip], ALL, to_layout[flip]) for flip in range(2)]
        even = x % 2 == 0
        first = jnp.where(even, got[0], got[1]).astype(HIGH)
        second = jnp.where(even, got[1], got[0]).astype(HIGH)
        return [
            jnp.concatenate([part[:, at : at + own_width] for part in (first, second)], axis=1)
            for at in range(0, first.shape[1], own_width)
        ]

    with jax.named_scope("grad_keys_values"):
        keys_task = ticks.add(
            sum_task(unit_parts(key_terms), unit_parts(value_terms)), urgent=True
        )
    with jax.named_scope("normed_sum"):
        normed_sum = RowSum(
            ticks, lambda v: matmul_right_t(v, weight_query), [grad_queries], rows_local
        )
        normed_sum.step()
        sent = normed_sum.sent
    with jax.named_scope("query_weight_sum"):
        query_terms = matmul_left_t(after(group_normed, sent), grad_queries).astype(LOW)
    with jax.named_scope("out_weight_sum"):
        group_branch = jnp.concatenate(after(branch_both, sent), axis=0)
        out_terms = matmul_left_t(group_branch, mixed).astype(LOW)
    with jax.named_scope("normed_sum"):
        grad_normed = normed_sum.finish()
    with jax.named_scope("grad_keys_values"):
        grad_keys, grad_values = ticks.finish(keys_task)[0]
    with jax.named_scope("query_out_weight_sum"):
        query_out_task = ticks.add(
            chunk_sums(jnp.concatenate([query_terms, out_terms], axis=1))
        )
    with jax.named_scope("shared_sum"):
        weight_key, weight_value = weight_kv[:, :own_width], weight_kv[:, own_width:]
        shared_sum = RowSum(
            ticks,
            lambda k, v: matmul_right_t(k, weight_key) + matmul_right_t(v, weight_value),
            [grad_keys, grad_values],
            rows_local,
        )
        shared_sum.total = after(shared_sum.total, branch)
        shared_sum.step()
        sent = shared_sum.sent
    with jax.named_scope("key_value_weight_sum"):
        grad_kv = jnp.concatenate(after((grad_keys, grad_values), sent), axis=1)
        kv_terms = matmul_left_t(group_shared, grad_kv).astype(LOW)
        kv_task = ticks.add(chunk_sums(kv_terms))
    with jax.named_scope("shared_sum"):
        grad_shared_normed = shared_sum.finish()
    with jax.named_scope("weight_layout"):
        (query_out_sum,) = ticks.finish(query_out_task)
        grad_query, grad_out = layout(after(query_out_sum, grad_shared_normed))
        (kv_sum,) = ticks.finish(kv_task)
        grad_key, grad_value = layout(kv_sum)
        grad_out = jnp.transpose(grad_out)
    with jax.named_scope("unit_weight_sums"):
        sums = [part for result in ticks.finish(*unit_sum_tasks) for part in result]
        whole = jnp.concatenate(sums, axis=0).astype(HIGH)
        grad_gate, grad_up, grad_down = (
            whole[w * units_padded : w * units_padded + units_local] for w in range(3)
        )
        grad_gate, grad_up = jnp.transpose(grad_gate), jnp.transpose(grad_up)

    grad_normed = after(grad_normed, sent)
    gain_one, grad_in_one = norm_backward(grad_normed, plain_one, factor_one, norm_gain)
    gain_kv, grad_in_kv = norm_backward(grad_shared_normed, plain_kv, factor_kv, kv_gain)
    grad_states = (grad_residual + grad_in_one).astype(LOW)
    grad_shared = grad_in_kv.astype(LOW)

    devices = 8 * sides
    gain_terms = jnp.stack([g.reshape(devices, -1) for g in (gain_one, gain_kv, gain_two)], axis=1)
    gain_terms = lax.all_to_all(
        gain_terms.reshape(devices, -1), ALL, split_axis=0, concat_axis=0, tiled=True
    )
    gain_sums = jnp.sum(gain_terms, axis=0).reshape(3, -1)
    return (
        output,
        grad_states,
        grad_shared,
        gain_sums[0],
        gain_sums[1],
        gain_sums[2],
        grad_query,
        grad_key,
        grad_value,
        grad_out,
        grad_gate,
        grad_up,
        grad_down,
    )


def solution(mesh):
    size_ctx, size_head = mesh.shape["ctx"], mesh.shape["head"]
    fine = Mesh(mesh.devices.reshape(4, size_ctx // 4, 2, size_head // 2), ALL)
    rows = P(ALL, None)
    ctx, head = ("z", "x"), ("y", "c")
    in_specs = (
        rows,
        rows,
        P(),
        P(),
        P(),
        rows,
        rows,
        rows,
        rows,
        P(None, ALL),
        P(None, ALL),
        rows,
        P(),
        rows,
    )
    out_specs = (
        rows,
        rows,
        rows,
        P(ALL),
        P(ALL),
        P(ALL),
        P(ctx, head),
        P(ctx, head),
        P(ctx, head),
        P(head, ctx),
        P(None, ALL),
        P(None, ALL),
        rows,
    )
    return jax.shard_map(
        per_device, mesh=fine, in_specs=in_specs, out_specs=out_specs, check_vma=False
    )
```

```python
import math

import jax
import jax.numpy as jnp
from jax import lax
from jax.experimental import pallas as pl
from jax.experimental.pallas import tpu as pltpu
from jax.sharding import Mesh, PartitionSpec as P

HD = 128
EPSILON = 1e-06
LOW = jnp.bfloat16
HIGH = jnp.float32
LOG2E = math.log2(math.e)
SCORE_SCALE = HD ** (-0.5)
ALL = ("z", "x", "y", "c")
RUNS = (8, 4, 2, 1)


def add_low(first, second):
    return (first.astype(HIGH) + second.astype(HIGH)).astype(LOW)


def after(values, *earlier):
    return lax.optimization_barrier((values, earlier))[0]


def hop(values, axis, steps=1):
    size = lax.axis_size(axis)
    return lax.ppermute(values, axis, [(i, (i + steps) % size) for i in range(size)])


def both_cores(blocks):
    blocks = blocks[1:] + blocks[:1]
    return blocks + [hop(block, "c") for block in blocks]


def gather_task(first, second):
    size = lax.axis_size("x")
    firsts, seconds, first_over, second_over = [first], [second], [], []
    for stage in range(size):
        wanted = [("y", firsts[stage], first_over)]
        if stage == 0:
            wanted.append(("y", second, second_over))
        if stage < size - 1:
            wanted += [("x", firsts[stage], firsts), ("x", seconds[stage], seconds)]
        if stage:
            wanted.append(("x", second_over[stage - 1], second_over))
        yield wanted
    return (
        [piece for pair in zip(firsts, first_over) for piece in pair],
        [piece for pair in zip(seconds, second_over) for piece in pair],
    )


def sum_task(first, second):
    size = lax.axis_size("x")
    got, far, near = [], [], []
    over = [[] for _ in range(size)]
    far_total, near_total = second[3], second[2]
    for step in range(1, size):
        wanted = [("x", far_total, far), ("x", near_total, near)]
        if step == 1:
            wanted += [("y", first[2 * s + 1], over[s]) for s in range(1, size)]
            wanted.append(("y", first[1], over[0]))
        yield wanted
        at = 2 * ((step + 1) % size)
        far_total, near_total = add_low(second[at + 1], far[-1]), add_low(second[at], near[-1])
    merged = [add_low(first[2 * s], over[s][0]) for s in range(size)]
    total = merged[1]
    for step in range(1, size):
        wanted = [("x", total, got)]
        if step == 1:
            wanted.append(("y", far_total, far))
        yield wanted
        total = add_low(merged[(step + 1) % size], got[-1])
    return total, add_low(near_total, far[-1])


def sum_joined_task(first, second):
    if lax.axis_size("x") > 2:
        return (yield from sum_task(first, second))
    rows = first[0].shape[0]
    over_x, over_y, got, far = [], [], [], []
    yield [
        ("x", jnp.concatenate([second[3], second[2]]), over_x),
        ("y", jnp.concatenate([first[3], first[1]]), over_y),
    ]
    far_total = add_low(second[1], over_x[-1][:rows])
    near_total = add_low(second[0], over_x[-1][rows:])
    merged = add_low(first[2], over_y[-1][:rows])
    own = add_low(first[0], over_y[-1][rows:])
    yield [("x", merged, got), ("y", far_total, far)]
    return add_low(own, got[-1]), add_low(near_total, far[-1])


class Ticks:
    BYTES = 9 * 2**16

    def __init__(self):
        self.tasks = []
        self.over_z = ()
        self.sides = [(), ()]
        self.sent = None
        self.held = []
        self.places = []

    def add(self, task, urgent=False):
        entry = {"task": task, "wanted": None, "open": 0, "result": None, "urgent": urgent}
        self.tasks.insert(0 if urgent else len(self.tasks), entry)
        self.advance(entry)
        return entry

    def advance(self, entry):
        try:
            entry["wanted"] = list(next(entry["task"]))
            entry["open"] = len(entry["wanted"])
        except StopIteration as stop:
            entry["result"] = stop.value
            self.tasks.remove(entry)

    def tick(self, *moves, room=1, lock=True):
        got = []
        for values, steps in moves:
            self.sent = after(values, self.over_z, self.sides[-2])
            got.append(hop(self.sent, "z", steps))
        self.release(*([self.sent] if moves else []))
        left = {"x": room * self.BYTES, "y": room * self.BYTES}
        before = self.over_z if lock else ()
        arrived = []
        finished = []
        for entry in self.tasks:
            later = []
            for axis, values, into in entry["wanted"]:
                if left[axis] >= min(values.nbytes, self.BYTES):
                    left[axis] -= values.nbytes
                    into.append(hop(after(values, self.sides[-1], before), axis))
                    if not entry["urgent"]:
                        self.places.append((into, len(into) - 1))
                    arrived.append(into[-1])
                    entry["open"] -= 1
                else:
                    later.append((axis, values, into))
            entry["wanted"] = later
            if not entry["open"]:
                finished.append(entry)
        self.over_z = tuple(got) or self.over_z
        self.sides = self.sides[-1:] + [tuple(arrived)]
        for entry in finished:
            if entry["urgent"]:
                self.advance(entry)
            else:
                self.held.append(entry)
        return got

    def release(self, *earlier):
        if earlier:
            for into, at in self.places:
                into[at] = after(into[at], earlier)
        held, self.held, self.places = self.held, [], []
        for entry in held:
            self.tasks.remove(entry)
            self.tasks.append(entry)
            self.advance(entry)

    def finish(self, *entries):
        self.release()
        while any(entry["result"] is None for entry in entries):
            self.tick()
            self.release()
        return [entry["result"] for entry in entries]

    def gather_parts(self, rows):
        blocks = [rows]
        for _ in range(1, lax.axis_size("z")):
            blocks += self.tick((blocks[-1], 1))
            yield self.sent
        yield both_cores(blocks)

    def gather_rows(self, rows):
        *_, blocks = self.gather_parts(rows)
        return jnp.concatenate(blocks, axis=0)

    def join_cores(self, blocks):
        return jnp.concatenate(both_cores(blocks), axis=0)


class RowSum:
    def __init__(self, ticks, terms_of, inputs, rows_local):
        self.ticks = ticks
        self.rows = rows_local
        self.half = inputs[0].shape[0] // 2
        self.terms_of = terms_of
        self.inputs = tuple(inputs)
        self.count = 0
        self.total = self.terms(self.inputs, 0).astype(LOW)

    def terms(self, inputs, block):
        near, far = block * self.rows, self.half + block * self.rows
        far_terms = self.terms_of(*(v[far : far + self.rows] for v in inputs))
        got = hop(far_terms.astype(LOW), "c")
        return self.terms_of(*(v[near : near + self.rows] for v in inputs)) + got.astype(HIGH)

    def step(self, room=1):
        (got,) = self.ticks.tick((self.total, 1), room=room)
        self.sent = self.ticks.sent
        self.count += 1
        terms = lax.optimization_barrier(self.terms(after(self.inputs, self.sent), self.count))
        self.total = terms + got.astype(HIGH)
        if self.count < 3:
            self.total = self.total.astype(LOW)

    def finish(self, room=1):
        while self.count < 3:
            self.step(room)
        return self.total


def place_blocks(pieces, places, widths):
    count, rows, width = pieces[0].shape
    total = len(pieces) * count

    def kernel(place_ref, *refs):
        ins, outs = refs[: len(pieces)], refs[len(pieces) :]
        for at in range(total):
            start = 0
            for out, size in zip(outs, widths):
                out[place_ref[at]] = ins[at // count][at % count, :, start : start + size]
                start += size

    shapes = [(total, rows, size) for size in widths]
    placed = pl.pallas_call(
        kernel,
        out_shape=[jax.ShapeDtypeStruct(shape, pieces[0].dtype) for shape in shapes],
        grid_spec=pltpu.PrefetchScalarGridSpec(
            num_scalar_prefetch=1,
            grid=(1,),
            in_specs=[pl.BlockSpec((count, rows, width), lambda i, *_: (0, 0, 0))] * len(pieces),
            out_specs=[pl.BlockSpec(shape, lambda i, *_: (0, 0, 0)) for shape in shapes],
        ),
        compiler_params=pltpu.CompilerParams(vmem_limit_bytes=48 * 2**20),
        cost_estimate=pl.CostEstimate(
            flops=0, bytes_accessed=4 * total * rows * width, transcendentals=0
        ),
        name="place_blocks",
    )(places, *pieces)
    return [out.reshape(total * rows, -1) for out in placed]


def normalize(values, gain_vec):
    factor = lax.rsqrt(jnp.mean(values * values, axis=-1, keepdims=True) + EPSILON)
    plain_rows = values * factor
    return (plain_rows, factor, plain_rows * gain_vec)


def norm_backward(grad_normed, plain_rows, factor, gain_vec):
    scaled = grad_normed * gain_vec
    gain_part = jnp.sum(grad_normed * plain_rows, axis=0)
    grad_input = factor * (
        scaled - plain_rows * jnp.mean(scaled * plain_rows, axis=-1, keepdims=True)
    )
    return (gain_part, grad_input)


def matmul(left_side, right_side):
    return jnp.dot(left_side, right_side, preferred_element_type=HIGH)


def matmul_right_t(left_side, right_side):
    return lax.dot_general(
        left_side, right_side, (((1,), (1,)), ((), ())), preferred_element_type=HIGH
    )


def matmul_left_t(left_side, right_side):
    return lax.dot_general(
        left_side, right_side, (((0,), (0,)), ((), ())), preferred_element_type=HIGH
    )


def pad_units(rows):
    extra = -rows.shape[0] % 16
    return jnp.pad(rows, ((0, extra), (0, 0)))


def quarters(count):
    tiles = count // 16
    return [16 * (tiles * i // 4) for i in range(5)]


def diagonal_visible(core, span_rows, key_axis):
    half = span_rows // 2

    def place(axis):
        index = lax.broadcasted_iota(jnp.int32, (span_rows, span_rows), axis)
        flipped = jnp.where(index < half, index + half, index - half)
        return jnp.where(core == 0, index, flipped)

    return place(key_axis) <= place(1 - key_axis)


def in_runs(count, step, carry):
    done = 0
    for run in RUNS:
        stop = count // run * run
        first = done

        def body(at, carry, run=run, first=first):
            return step(first + run * at, carry, run)

        carry = lax.fori_loop(0, (stop - done) // run, body, carry)
        done = stop
    return carry


def forward_kernel(
    place_ref, rank_ref, core_ref, query_ref, key_ref, value_ref, mixed_ref, lse_ref, score_ref
):
    half_rows = query_ref.shape[1]
    span_rows = 2 * half_rows
    heads = query_ref.shape[2] // HD
    rank = rank_ref[pl.program_id(1)]
    columns = [slice(h * HD, (h + 1) * HD) for h in range(heads)]

    def span(ref, step, h):
        side = place_ref[step] // 4
        start = pl.multiple_of((place_ref[step] % 4) * half_rows, half_rows)
        return ref[side, :, pl.ds(start, half_rows), columns[h]].reshape(span_rows, HD)

    def block_scores(step, h):
        query = query_ref[:, :, columns[h]].reshape(span_rows, HD)
        return matmul_right_t(query, span(key_ref, step, h)) * (SCORE_SCALE * LOG2E)

    def fold(values, operation):
        folded = values[:, :HD]
        for at in range(HD, span_rows, HD):
            folded = operation(folded, values[:, at : at + HD])
        return folded

    def score_step(step, maxima, count):
        new = []
        for h in range(heads):
            top = maxima[h]
            for at in range(count):
                scores = block_scores(step + at, h)
                score_ref[h, step + at] = scores
                top = jnp.maximum(top, fold(scores, jnp.maximum))
            new.append(top)
        return tuple(new)

    maxima = tuple(jnp.full((span_rows, HD), -jnp.inf, HIGH) for _ in range(heads))
    maxima = in_runs(rank, score_step, maxima)
    visible = diagonal_visible(core_ref[0], span_rows, 1)
    tops = []
    for h in range(heads):
        scores = jnp.where(visible, block_scores(rank, h), -jnp.inf)
        score_ref[h, rank] = scores
        top = jnp.maximum(maxima[h], fold(scores, jnp.maximum))
        tops.append(jnp.max(top, axis=1, keepdims=True))

    def mix_step(step, running, count):
        new = []
        for h in range(heads):
            total, mixed = running[h]
            for at in range(count):
                weights = jnp.exp2(score_ref[h, step + at] - tops[h])
                total = total + fold(weights, jnp.add)
                mixed = mixed + matmul(weights.astype(LOW), span(value_ref, step + at, h))
            new.append((total, mixed))
        return tuple(new)

    zero = jnp.zeros((span_rows, HD), HIGH)
    sums = tuple((zero, zero) for _ in range(heads))
    blocks = rank + 1
    sums = in_runs(blocks, mix_step, sums)
    for h in range(heads):
        total = jnp.sum(sums[h][0], axis=1, keepdims=True)
        mixed = (sums[h][1] / total).astype(LOW)
        mixed_ref[:, :, columns[h]] = mixed.reshape(2, half_rows, HD)
        lse = jnp.broadcast_to(tops[h] + jnp.log2(total), (span_rows, HD))
        lse_ref[h] = jnp.transpose(lse)[:8, :]


def backward_kernel(
    place_ref,
    rank_ref,
    core_ref,
    query_ref,
    mixed_ref,
    lse_ref,
    key_ref,
    value_ref,
    weight_ref,
    *refs,
):
    *branch_refs, grad_query_ref, grad_key_ref, grad_value_ref = refs[:-4]
    grad_ref, turned_ref, key_sum_ref, value_sum_ref = refs[-4:]
    heads = query_ref.shape[2] // HD
    half_rows = query_ref.shape[1] // rank_ref.shape[0]
    span_rows = 2 * half_rows
    columns = [slice(h * HD, (h + 1) * HD) for h in range(heads)]
    count = len(branch_refs) // 2
    for core in range(2):
        rows = [ref[...] for ref in branch_refs[core * count : (core + 1) * count]]
        rows = jnp.concatenate(rows, axis=0)
        grad_ref[core] = matmul_right_t(rows, weight_ref[...]).astype(LOW)
    for h in range(heads):
        for at in range(turned_ref.shape[1]):
            rows = slice(at % 4 * half_rows, (at % 4 + 1) * half_rows)
            keys = key_ref[at // 4, :, rows, columns[h]].reshape(span_rows, HD)
            turned_ref[h, at] = jnp.transpose(keys)
    key_sum_ref[...] = jnp.zeros_like(key_sum_ref)
    value_sum_ref[...] = jnp.zeros_like(value_sum_ref)

    def query_span(at, carry):
        here = pl.ds(pl.multiple_of(at * half_rows, half_rows), half_rows)
        lanes = pl.ds(pl.multiple_of(at * span_rows, span_rows), span_rows)
        rank = rank_ref[at]

        def own(ref, h):
            return ref[:, here, columns[h]].reshape(span_rows, HD)

        delta = []
        lse = []
        for h in range(heads):
            product = own(grad_ref, h).astype(HIGH) * own(mixed_ref, h).astype(HIGH)
            delta.append(jnp.sum(jnp.transpose(product), axis=0, keepdims=True))
            lse.append(lse_ref[h, :1, lanes])

        def block(step, grad_query, visible):
            side = place_ref[step] // 4
            start = pl.multiple_of((place_ref[step] % 4) * half_rows, half_rows)
            there = pl.ds(start, half_rows)
            new = []
            for h in range(heads):
                query = own(query_ref, h)
                grad = own(grad_ref, h)
                keys = key_ref[side, :, there, columns[h]].reshape(span_rows, HD)
                values = value_ref[side, :, there, columns[h]].reshape(span_rows, HD)
                scores = matmul_right_t(keys, query) * (SCORE_SCALE * LOG2E)
                weights = jnp.exp2(scores - lse[h])
                if visible is not None:
                    weights = jnp.where(visible, weights, 0.0)
                grad_weights = matmul_right_t(values, grad)
                grad_scores = (weights * (grad_weights - delta[h])).astype(LOW)
                value_term = matmul(weights.astype(LOW), grad)
                key_term = matmul(grad_scores, query)
                value_sum_ref[side, :, there, columns[h]] += value_term.reshape(2, half_rows, HD)
                key_sum_ref[side, :, there, columns[h]] += key_term.reshape(2, half_rows, HD)
                new.append(grad_query[h] + matmul(turned_ref[h, place_ref[step]], grad_scores))
            return tuple(new)

        start = tuple(jnp.zeros((HD, span_rows), HIGH) for _ in range(heads))
        def blocks(first, grad_query, count):
            for more in range(count):
                grad_query = block(first + more, grad_query, None)
            return grad_query

        grad_query = in_runs(rank, blocks, start)
        visible = diagonal_visible(core_ref[0], span_rows, 0)
        grad_query = block(rank, grad_query, visible)
        for h in range(heads):
            result = (jnp.transpose(grad_query[h]) * SCORE_SCALE).astype(LOW)
            grad_query_ref[:, here, columns[h]] = result.reshape(2, half_rows, HD)
        return carry

    lax.fori_loop(0, rank_ref.shape[0], query_span, 0)
    grad_key_ref[...] = (key_sum_ref[...] * SCORE_SCALE).astype(LOW)
    grad_value_ref[...] = value_sum_ref[...].astype(LOW)


def heads_at_once(key_rows, features):
    return features // HD if key_rows <= 4096 else 1


def attention_forward(scalars, queries, keys, values):
    rows, features = queries.shape
    key_rows = keys.shape[0]
    own_spans = scalars[1].shape[0]
    half_rows = rows // own_spans // 2
    span_rows = 2 * half_rows
    heads = heads_at_once(key_rows, features)
    width = heads * HD
    pairs = rows * key_rows * features
    sides = key_rows // rows
    own = pl.BlockSpec((2, half_rows, width), lambda h, i, *_: (0, i, h))
    other = pl.BlockSpec((sides, 2, rows // 2, width), lambda h, i, *_: (0, 0, 0, h))
    mixed, lse = pl.pallas_call(
        forward_kernel,
        out_shape=(
            jax.ShapeDtypeStruct((2, rows // 2, features), LOW),
            jax.ShapeDtypeStruct((features // HD, 8, rows), HIGH),
        ),
        grid_spec=pltpu.PrefetchScalarGridSpec(
            num_scalar_prefetch=3,
            grid=(features // width, own_spans),
            in_specs=[own, other, other],
            out_specs=[own, pl.BlockSpec((heads, 8, span_rows), lambda h, i, *_: (h, 0, i))],
            scratch_shapes=[
                pltpu.VMEM((heads, key_rows // span_rows, span_rows, span_rows), HIGH)
            ],
        ),
        compiler_params=pltpu.CompilerParams(vmem_limit_bytes=56 * 2**20),
        cost_estimate=pl.CostEstimate(
            flops=20 * pairs, bytes_accessed=4 * key_rows * features, transcendentals=pairs // 256
        ),
        name="attention_forward",
    )(
        *scalars,
        queries.reshape(2, rows // 2, features),
        keys.reshape(sides, 2, rows // 2, features),
        values.reshape(sides, 2, rows // 2, features),
    )
    return mixed.reshape(rows, features), lse


def attention_backward(scalars, queries, mixed, lse, keys, values, weight_out, branch_blocks):
    rows, features = queries.shape
    key_rows = keys.shape[0]
    heads = heads_at_once(key_rows, features)
    width = heads * HD
    pairs = rows * key_rows * features
    sides = key_rows // rows
    own_shape = (2, rows // 2, features)
    key_shape = (sides, 2, rows // 2, features)
    once = pl.Buffered(1)
    own_part, key_part = own_shape[:2] + (width,), key_shape[:3] + (width,)
    own = pl.BlockSpec(own_part, lambda h, *_: (0, 0, h))
    other = pl.BlockSpec(key_part, lambda h, *_: (0, 0, 0, h))
    other_in = pl.BlockSpec(key_part, lambda h, *_: (0, 0, 0, h), pipeline_mode=once)
    block = pl.BlockSpec(branch_blocks[0].shape, lambda h, *_: (0, 0), pipeline_mode=once)
    grad_queries, grad_keys, grad_values = pl.pallas_call(
        backward_kernel,
        out_shape=(
            jax.ShapeDtypeStruct(own_shape, LOW),
            jax.ShapeDtypeStruct(key_shape, LOW),
            jax.ShapeDtypeStruct(key_shape, LOW),
        ),
        grid_spec=pltpu.PrefetchScalarGridSpec(
            num_scalar_prefetch=3,
            grid=(features // width,),
            in_specs=[
                own,
                own,
                pl.BlockSpec((heads, 8, rows), lambda h, *_: (h, 0, 0)),
                other_in,
                other_in,
                pl.BlockSpec((width, weight_out.shape[1]), lambda h, *_: (h, 0)),
            ]
            + [block] * len(branch_blocks),
            out_specs=[own, other, other],
            scratch_shapes=[
                pltpu.VMEM(own_part, LOW),
                pltpu.VMEM((heads, 4 * sides, HD, key_rows // (4 * sides)), LOW),
            ]
            + [pltpu.VMEM(key_part, HIGH)] * 2,
        ),
        compiler_params=pltpu.CompilerParams(vmem_limit_bytes=56 * 2**20),
        cost_estimate=pl.CostEstimate(
            flops=120 * pairs, bytes_accessed=8 * key_rows * features, transcendentals=pairs // 256
        ),
        name="attention_backward",
    )(
        *scalars,
        queries.reshape(own_shape),
        mixed.reshape(own_shape),
        lse,
        keys.reshape(key_shape),
        values.reshape(key_shape),
        weight_out,
        *branch_blocks,
    )
    return (
        grad_queries.reshape(rows, features),
        grad_keys.reshape(key_rows, features),
        grad_values.reshape(key_rows, features),
    )


def per_device(
    states,
    shared_kv,
    norm_gain,
    kv_gain,
    ffn_gain,
    query_weight,
    key_weight,
    value_weight,
    out_weight,
    gate_weight,
    up_weight,
    down_weight,
    span_order,
    grad_output,
):
    z, x, y, c = (lax.axis_index(name) for name in ALL)
    size_x = lax.axis_size("x")
    sides = 2 * size_x
    rows_local, width_model = states.shape
    weight_rows = query_weight.shape[0]
    units_local = gate_weight.shape[1]
    own_width = width_model // 8

    side = jnp.arange(sides, dtype=jnp.int32)
    side_owner = jnp.mod(x - side // 2, size_x) * 2 + jnp.bitwise_xor(y, side % 2)
    back = jnp.mod(jnp.arange(4, dtype=jnp.int32) + 1, 4)
    back_owner = jnp.mod(z - back, 4)

    ticks = Ticks()

    block = jnp.arange(8 * sides, dtype=jnp.int32)
    block_half, block_side = block // (4 * sides), block // 4 % sides
    block_back = 2 * block_half + block // 2 % 2
    block_place = (
        (jnp.mod(z - block_back, 4) * size_x + jnp.mod(x - block_side // 2, size_x)) * 2
        + jnp.bitwise_xor(y, block_side % 2)
    ) * 2 + jnp.bitwise_xor(c, block % 2)

    state_rows = states.astype(HIGH)
    shared_rows = shared_kv.astype(HIGH)
    plain_kv, factor_kv, normed_kv = normalize(shared_rows, kv_gain)
    plain_one, factor_one, normed_one = normalize(state_rows, norm_gain)
    shared_low = normed_kv.astype(LOW)
    normed_low = normed_one.astype(LOW)

    with jax.named_scope("weight_columns"):
        pair = 2 * own_width
        projections = (key_weight, value_weight, query_weight)

        def cut(start, size, arrays):
            return jnp.concatenate(
                [lax.dynamic_slice_in_dim(v, start, size, 1) for v in arrays], axis=1
            )

        parts = [cut(jnp.mod(z + step, 4) * pair, pair, projections) for step in range(4)]
        over = ticks.tick((parts[1], 1), (parts[2], 2), (parts[3], 3), lock=False)
        columns = []
        for part in [parts[0]] + over:
            arrays = [part[:, i * pair : (i + 1) * pair] for i in range(3)]
            columns.append(cut(c * own_width, own_width, arrays))
            columns.append(hop(cut((1 - c) * own_width, own_width, arrays), "c"))
        columns = jnp.stack(columns)
    with jax.named_scope("shared_rows"):
        out_weight = after(out_weight, over)
        out_task = ticks.add(
            gather_task(out_weight[: weight_rows // 2], out_weight[weight_rows // 2 :]),
            urgent=True,
        )
        weight_task = ticks.add(gather_task(columns[:4], columns[4:]), urgent=True)
        shared_blocks = [shared_low]
        for _ in range(3):
            shared_blocks += ticks.tick((shared_blocks[-1], 1), room=1.2, lock=False)
        group_shared = ticks.join_cores(shared_blocks)
    with jax.named_scope("weight_columns"):
        first, second = ticks.finish(weight_task)[0]
        weight_kv, weight_query = place_blocks(
            first + second, block_place, (2 * own_width, own_width)
        )
    with jax.named_scope("out_weight"):
        whole = jnp.arange(sides, dtype=jnp.int32)
        whole_side = jnp.mod(x - whole // 2, size_x) * 2 + jnp.bitwise_xor(y, whole % 2)
        out_pieces = ticks.finish(out_task)[0]
        out_pieces = jnp.stack([part for pair in zip(*out_pieces) for part in pair])
        out_pieces = jnp.take(
            out_pieces.reshape(sides, weight_rows, width_model), whole_side, axis=0
        ).reshape(2, size_x // 2, 2, weight_rows, width_model)
        out_keep = lax.dynamic_index_in_dim(out_pieces, c, 0, keepdims=False)
        out_give = lax.dynamic_index_in_dim(out_pieces, 1 - c, 0, keepdims=False)
        out_got = hop(out_give, "c")
        weight_out = jnp.where(
            c == 0, jnp.stack([out_keep, out_got], axis=2), jnp.stack([out_got, out_keep], axis=2)
        ).reshape(own_width, width_model)

    with jax.named_scope("keys_values"):
        group_shared = after(group_shared, weight_out)
        keys_own = matmul(group_shared, weight_kv[:, :own_width]).astype(LOW)
        values_own = matmul(group_shared, weight_kv[:, own_width:]).astype(LOW)
        keys_task = ticks.add(gather_task(keys_own, values_own), urgent=True)
    with jax.named_scope("normed_rows"):
        normed_blocks = [normed_low]
        for _ in range(3):
            normed_blocks += ticks.tick((normed_blocks[-1], 1), lock=False)
    with jax.named_scope("normed_rows"):
        group_normed = ticks.join_cores(normed_blocks)
    with jax.named_scope("grad_output_rows"):
        grad_blocks = [grad_output] + ticks.tick((grad_output, 1))
    with jax.named_scope("keys_values"):
        key_pieces, value_pieces = ticks.finish(keys_task)[0]
        keys_all, values_all = jnp.concatenate(key_pieces), jnp.concatenate(value_pieces)
    with jax.named_scope("queries"):
        late_normed = after(group_normed, key_pieces[-1], value_pieces[-1])
        queries = matmul(late_normed, weight_query).astype(LOW)

    span_of = (back_owner[None, :] * sides + side_owner[:, None]).reshape(-1)
    ranks = jnp.take(span_order, span_of)
    spans = span_order.shape[0]
    listed = jnp.arange(spans, dtype=jnp.int32)
    place = jnp.sum(jnp.where(ranks[None, :] == listed[:, None], listed[None, :], 0), axis=1)
    scalars = (place, ranks[:4], c.reshape(1).astype(jnp.int32))

    with jax.named_scope("unit_weights"):
        late = (keys_all, values_all)
        unit_rows = jnp.concatenate(
            [
                pad_units(jnp.transpose(after(gate_weight, *late))),
                pad_units(jnp.transpose(after(up_weight, *late))),
                pad_units(after(down_weight, *late)),
            ],
            axis=0,
        )
        cuts = quarters(unit_rows.shape[0])
        chunks = [unit_rows[cuts[i] : cuts[i + 1]] for i in range(4)]
        unit_tasks = [ticks.add(gather_task(chunks[i], chunks[i + 1])) for i in (0, 2)]
    with jax.named_scope("grad_output_rows"):
        grad_blocks += ticks.tick((grad_blocks[-1], 1), (grad_output, -1))
    mixed, lse = attention_forward(scalars, queries, keys_all, values_all)
    with jax.named_scope("grad_output_rows"):
        group_grad = ticks.join_cores(grad_blocks)
    with jax.named_scope("attention_sum"):
        attention_sum = RowSum(ticks, lambda v: matmul(v, weight_out), [mixed], rows_local)
        residual = state_rows + attention_sum.finish()
    plain_two, factor_two, normed_two = normalize(residual, ffn_gain)
    with jax.named_scope("normed_two_rows"):
        group_in = ticks.gather_rows(normed_two.astype(LOW))
    with jax.named_scope("unit_weights"):
        gathered = [pieces for result in ticks.finish(*unit_tasks) for pieces in result]
        units_padded = unit_rows.shape[0] // 3

        def units_of(which):
            low, high = which * units_padded, (which + 1) * units_padded
            rows = []
            for s in range(sides):
                for i in range(4):
                    start, stop = max(low, cuts[i]), min(high, cuts[i + 1])
                    if start < stop:
                        rows.append(gathered[i][s][start - cuts[i] : stop - cuts[i]])
            return jnp.concatenate(rows, axis=0)

        weight_gate, weight_up, weight_down = (units_of(which) for which in range(3))

    gate_act = matmul_right_t(group_in, weight_gate)
    up_act = matmul_right_t(group_in, weight_up)
    grad_hidden = matmul_right_t(group_grad, weight_down)
    sigmoid = jax.nn.sigmoid(gate_act)
    silu_act = gate_act * sigmoid
    hidden = (silu_act * up_act).astype(LOW)
    grad_gate_act = (
        grad_hidden * up_act * sigmoid * (1.0 + gate_act * (1.0 - sigmoid))
    ).astype(LOW)
    grad_up_act = (grad_hidden * silu_act).astype(LOW)

    def unit_parts(values):
        step = values.shape[0] // sides
        return [values[s * step : (s + 1) * step] for s in range(sides)]

    with jax.named_scope("ffn_grad_sum"):
        ffn_grad_sum = RowSum(
            ticks,
            lambda g, u: matmul(g, weight_gate) + matmul(u, weight_up),
            [grad_gate_act, grad_up_act],
            rows_local,
        )
        unit_terms = []

        def unit_window(left, right, room=1):
            ffn_grad_sum.step(room)
            terms = matmul_left_t(after(left, ffn_grad_sum.sent), right).astype(LOW)
            unit_terms.append(unit_parts(terms))

        def chunk_parts(i):
            parts = []
            for s in range(sides):
                rows = []
                for which in range(3):
                    low = which * units_padded
                    start, stop = max(low, cuts[i]), min(low + units_padded, cuts[i + 1])
                    if start < stop:
                        rows.append(unit_terms[which][s][start - low : stop - low])
                parts.append(jnp.concatenate(rows, axis=0) if rows[1:] else rows[0])
            return parts

        unit_window(grad_gate_act, group_in)
        unit_window(grad_up_act, group_in)
        unit_sum_tasks = [ticks.add(sum_task(chunk_parts(0), chunk_parts(1)))]
        unit_window(hidden, group_grad)
        unit_sum_tasks.append(ticks.add(sum_task(chunk_parts(2), chunk_parts(3))))
        grad_ffn = ffn_grad_sum.finish()

    gain_two, grad_norm_two = norm_backward(grad_ffn, plain_two, factor_two, ffn_gain)
    grad_residual = grad_output.astype(HIGH) + grad_norm_two
    with jax.named_scope("branch_rows"):
        branch_moves = ticks.gather_parts(grad_residual.astype(LOW))
        sent = next(branch_moves)
        lined = jnp.arange(8, dtype=jnp.int32)
        order = jnp.bitwise_xor(c, lined % 2) * 4 + jnp.mod(z - lined // 2 - 1, 4)
        late_hidden = after(hidden, sent).reshape(8, rows_local, -1)
        late_hidden = jnp.take(late_hidden, order, axis=0).reshape(8 * rows_local, -1)
        terms = matmul(after(late_hidden, next(branch_moves)), weight_down).astype(LOW)
        next(branch_moves)
        branch_both = next(branch_moves)
    with jax.named_scope("ffn_sum"):
        branch = lax.psum_scatter(
            after(terms, ticks.over_z), ("z", "c"), scatter_dimension=0, tiled=True
        )
        output = (residual + branch.astype(HIGH)).astype(LOW)
    with jax.named_scope("unit_weight_sums"):
        ticks.tick(room=2, lock=False)
    grad_queries, key_terms, value_terms = attention_backward(
        scalars, queries, mixed, lse, keys_all, values_all, weight_out, branch_both
    )

    def side_parts(values, k):
        count = values.shape[0] // (2 * sides)
        return [
            lax.dynamic_slice_in_dim(
                values,
                (2 * jnp.bitwise_xor(jnp.bitwise_xor(side_owner[s], z), 2 * k) + k) * count,
                count,
                0,
            )
            for s in range(sides)
        ]

    def chunk_sums(values):
        return sum_joined_task(side_parts(values, 0), side_parts(values, 1))

    to_layout = [
        [
            (
                ((za * size_x + xa) * 2 + ya) * 2 + ca,
                (2 * ((2 * xa + ya) ^ za ^ (2 * (ca ^ flip))) + (ca ^ flip)) * 4 + za,
            )
            for za in range(4)
            for xa in range(size_x)
            for ya in range(2)
            for ca in range(2)
        ]
        for flip in range(2)
    ]

    def layout(summed):
        sent = jnp.where(c == 0, summed[0], summed[1]), jnp.where(c == 0, summed[1], summed[0])
        got = [lax.ppermute(sent[flip], ALL, to_layout[flip]) for flip in range(2)]
        even = x % 2 == 0
        first = jnp.where(even, got[0], got[1]).astype(HIGH)
        second = jnp.where(even, got[1], got[0]).astype(HIGH)
        return [
            jnp.concatenate([part[:, at : at + own_width] for part in (first, second)], axis=1)
            for at in range(0, first.shape[1], own_width)
        ]

    with jax.named_scope("grad_keys_values"):
        keys_task = ticks.add(
            sum_joined_task(unit_parts(key_terms), unit_parts(value_terms)), urgent=True
        )
    with jax.named_scope("normed_sum"):
        normed_sum = RowSum(
            ticks, lambda v: matmul_right_t(v, weight_query), [grad_queries], rows_local
        )
        normed_sum.step()
        sent = normed_sum.sent
    with jax.named_scope("query_weight_sum"):
        query_terms = matmul_left_t(after(group_normed, sent), grad_queries).astype(LOW)
    with jax.named_scope("normed_sum"):
        normed_sum.step()
        sent = normed_sum.sent
    with jax.named_scope("out_weight_sum"):
        group_branch = jnp.concatenate(after(branch_both, sent), axis=0)
        out_terms = matmul_left_t(group_branch, mixed).astype(LOW)
    with jax.named_scope("normed_sum"):
        grad_normed = normed_sum.finish()
    with jax.named_scope("grad_keys_values"):
        grad_keys, grad_values = ticks.finish(keys_task)[0]
    with jax.named_scope("query_out_weight_sum"):
        query_out_task = ticks.add(
            chunk_sums(jnp.concatenate([query_terms, out_terms], axis=1))
        )
    with jax.named_scope("shared_sum"):
        weight_key, weight_value = weight_kv[:, :own_width], weight_kv[:, own_width:]
        shared_sum = RowSum(
            ticks,
            lambda k, v: matmul_right_t(k, weight_key) + matmul_right_t(v, weight_value),
            [grad_keys, grad_values],
            rows_local,
        )
        shared_sum.total = after(shared_sum.total, branch)
        shared_sum.step()
        sent = shared_sum.sent
    with jax.named_scope("key_value_weight_sum"):
        grad_kv = jnp.concatenate(after((grad_keys, grad_values), sent), axis=1)
        kv_terms = matmul_left_t(group_shared, grad_kv).astype(LOW)
        kv_task = ticks.add(chunk_sums(kv_terms))
    with jax.named_scope("shared_sum"):
        grad_shared_normed = shared_sum.finish()
    with jax.named_scope("weight_layout"):
        (query_out_sum,) = ticks.finish(query_out_task)
        grad_query, grad_out = layout(after(query_out_sum, grad_shared_normed))
        (kv_sum,) = ticks.finish(kv_task)
        grad_key, grad_value = layout(kv_sum)
        grad_out = jnp.transpose(grad_out)
    with jax.named_scope("unit_weight_sums"):
        sums = [part for result in ticks.finish(*unit_sum_tasks) for part in result]
        whole = jnp.concatenate(sums, axis=0).astype(HIGH)
        grad_gate, grad_up, grad_down = (
            whole[w * units_padded : w * units_padded + units_local] for w in range(3)
        )
        grad_gate, grad_up = jnp.transpose(grad_gate), jnp.transpose(grad_up)

    grad_normed = after(grad_normed, sent)
    gain_one, grad_in_one = norm_backward(grad_normed, plain_one, factor_one, norm_gain)
    gain_kv, grad_in_kv = norm_backward(grad_shared_normed, plain_kv, factor_kv, kv_gain)
    grad_states = (grad_residual + grad_in_one).astype(LOW)
    grad_shared = grad_in_kv.astype(LOW)

    devices = 8 * sides
    gain_terms = jnp.stack([g.reshape(devices, -1) for g in (gain_one, gain_kv, gain_two)], axis=1)
    gain_terms = lax.all_to_all(
        gain_terms.reshape(devices, -1), ALL, split_axis=0, concat_axis=0, tiled=True
    )
    gain_sums = jnp.sum(gain_terms, axis=0).reshape(3, -1)
    return (
        output,
        grad_states,
        grad_shared,
        gain_sums[0],
        gain_sums[1],
        gain_sums[2],
        grad_query,
        grad_key,
        grad_value,
        grad_out,
        grad_gate,
        grad_up,
        grad_down,
    )


def solution(mesh):
    size_ctx, size_head = mesh.shape["ctx"], mesh.shape["head"]
    fine = Mesh(mesh.devices.reshape(4, size_ctx // 4, 2, size_head // 2), ALL)
    rows = P(ALL, None)
    ctx, head = ("z", "x"), ("y", "c")
    in_specs = (
        rows,
        rows,
        P(),
        P(),
        P(),
        rows,
        rows,
        rows,
        rows,
        P(None, ALL),
        P(None, ALL),
        rows,
        P(),
        rows,
    )
    out_specs = (
        rows,
        rows,
        rows,
        P(ALL),
        P(ALL),
        P(ALL),
        P(ctx, head),
        P(ctx, head),
        P(ctx, head),
        P(head, ctx),
        P(None, ALL),
        P(None, ALL),
        rows,
    )
    return jax.shard_map(
        per_device, mesh=fine, in_specs=in_specs, out_specs=out_specs, check_vma=False
    )
```

```python
import math

import jax
import jax.numpy as jnp
from jax import lax
from jax.experimental import pallas as pl
from jax.experimental.pallas import tpu as pltpu
from jax.sharding import Mesh, PartitionSpec as P

HD = 128
EPSILON = 1e-06
LOW = jnp.bfloat16
HIGH = jnp.float32
LOG2E = math.log2(math.e)
SCORE_SCALE = HD ** (-0.5)
ALL = ("z", "x", "y", "c")
RUNS = (8, 4, 2, 1)


def add_low(first, second):
    return (first.astype(HIGH) + second.astype(HIGH)).astype(LOW)


def after(values, *earlier):
    return lax.optimization_barrier((values, earlier))[0]


def hop(values, axis, steps=1):
    size = lax.axis_size(axis)
    return lax.ppermute(values, axis, [(i, (i + steps) % size) for i in range(size)])


def both_cores(blocks):
    blocks = blocks[1:] + blocks[:1]
    return blocks + [hop(block, "c") for block in blocks]


def gather_task(first, second):
    size = lax.axis_size("x")
    firsts, seconds, first_over, second_over = [first], [second], [], []
    for stage in range(size):
        wanted = [("y", firsts[stage], first_over)]
        if stage == 0:
            wanted.append(("y", second, second_over))
        if stage < size - 1:
            wanted += [("x", firsts[stage], firsts), ("x", seconds[stage], seconds)]
        if stage:
            wanted.append(("x", second_over[stage - 1], second_over))
        yield wanted
    return (
        [piece for pair in zip(firsts, first_over) for piece in pair],
        [piece for pair in zip(seconds, second_over) for piece in pair],
    )


def sum_task(first, second):
    size = lax.axis_size("x")
    got, far, near = [], [], []
    over = [[] for _ in range(size)]
    far_total, near_total = second[3], second[2]
    for step in range(1, size):
        wanted = [("x", far_total, far), ("x", near_total, near)]
        if step == 1:
            wanted += [("y", first[2 * s + 1], over[s]) for s in range(1, size)]
            wanted.append(("y", first[1], over[0]))
        yield wanted
        at = 2 * ((step + 1) % size)
        far_total, near_total = add_low(second[at + 1], far[-1]), add_low(second[at], near[-1])
    merged = [add_low(first[2 * s], over[s][0]) for s in range(size)]
    total = merged[1]
    for step in range(1, size):
        wanted = [("x", total, got)]
        if step == 1:
            wanted.append(("y", far_total, far))
        yield wanted
        total = add_low(merged[(step + 1) % size], got[-1])
    return total, add_low(near_total, far[-1])


def sum_joined_task(first, second):
    if lax.axis_size("x") > 2:
        return (yield from sum_task(first, second))
    rows = first[0].shape[0]
    over_x, over_y, got, far = [], [], [], []
    yield [
        ("x", jnp.concatenate([second[3], second[2]]), over_x),
        ("y", jnp.concatenate([first[3], first[1]]), over_y),
    ]
    far_total = add_low(second[1], over_x[-1][:rows])
    near_total = add_low(second[0], over_x[-1][rows:])
    merged = add_low(first[2], over_y[-1][:rows])
    own = add_low(first[0], over_y[-1][rows:])
    yield [("x", merged, got), ("y", far_total, far)]
    return add_low(own, got[-1]), add_low(near_total, far[-1])


class Ticks:
    BYTES = 9 * 2**16

    def __init__(self):
        self.tasks = []
        self.over_z = ()
        self.sides = [(), ()]
        self.sent = None
        self.held = []
        self.places = []

    def add(self, task, urgent=False):
        entry = {"task": task, "wanted": None, "open": 0, "result": None, "urgent": urgent}
        self.tasks.insert(0 if urgent else len(self.tasks), entry)
        self.advance(entry)
        return entry

    def advance(self, entry):
        try:
            entry["wanted"] = list(next(entry["task"]))
            entry["open"] = len(entry["wanted"])
        except StopIteration as stop:
            entry["result"] = stop.value
            self.tasks.remove(entry)

    def tick(self, *moves, room=1, lock=True):
        got = []
        for values, steps in moves:
            self.sent = after(values, self.over_z, self.sides[-2])
            got.append(hop(self.sent, "z", steps))
        self.release(*([self.sent] if moves else []))
        left = {"x": room * self.BYTES, "y": room * self.BYTES}
        before = self.over_z if lock else ()
        arrived = []
        finished = []
        for entry in self.tasks:
            later = []
            for axis, values, into in entry["wanted"]:
                if left[axis] >= min(values.nbytes, self.BYTES):
                    left[axis] -= values.nbytes
                    into.append(hop(after(values, self.sides[-1], before), axis))
                    if not entry["urgent"]:
                        self.places.append((into, len(into) - 1))
                    arrived.append(into[-1])
                    entry["open"] -= 1
                else:
                    later.append((axis, values, into))
            entry["wanted"] = later
            if not entry["open"]:
                finished.append(entry)
        self.over_z = tuple(got) or self.over_z
        self.sides = self.sides[-1:] + [tuple(arrived)]
        for entry in finished:
            if entry["urgent"]:
                self.advance(entry)
            else:
                self.held.append(entry)
        return got

    def release(self, *earlier):
        if earlier:
            for into, at in self.places:
                into[at] = after(into[at], earlier)
        held, self.held, self.places = self.held, [], []
        for entry in held:
            self.tasks.remove(entry)
            self.tasks.append(entry)
            self.advance(entry)

    def finish(self, *entries):
        self.release()
        while any(entry["result"] is None for entry in entries):
            self.tick()
            self.release()
        return [entry["result"] for entry in entries]

    def gather_parts(self, rows):
        blocks = [rows]
        for _ in range(1, lax.axis_size("z")):
            blocks += self.tick((blocks[-1], 1))
            yield self.sent
        yield both_cores(blocks)

    def gather_rows(self, rows):
        *_, blocks = self.gather_parts(rows)
        return jnp.concatenate(blocks, axis=0)

    def join_cores(self, blocks):
        return jnp.concatenate(both_cores(blocks), axis=0)


class RowSum:
    def __init__(self, ticks, terms_of, inputs, rows_local):
        self.ticks = ticks
        self.rows = rows_local
        self.half = inputs[0].shape[0] // 2
        self.terms_of = terms_of
        self.inputs = tuple(inputs)
        self.count = 0
        self.total = self.terms(self.inputs, 0).astype(LOW)

    def terms(self, inputs, block):
        near, far = block * self.rows, self.half + block * self.rows
        far_terms = self.terms_of(*(v[far : far + self.rows] for v in inputs))
        got = hop(far_terms.astype(LOW), "c")
        return self.terms_of(*(v[near : near + self.rows] for v in inputs)) + got.astype(HIGH)

    def step(self, room=1):
        (got,) = self.ticks.tick((self.total, 1), room=room)
        self.sent = self.ticks.sent
        self.count += 1
        terms = lax.optimization_barrier(self.terms(after(self.inputs, self.sent), self.count))
        self.total = terms + got.astype(HIGH)
        if self.count < 3:
            self.total = self.total.astype(LOW)

    def finish(self, room=1):
        while self.count < 3:
            self.step(room)
        return self.total


def place_blocks(pieces, places, widths):
    count, rows, width = pieces[0].shape
    total = len(pieces) * count

    def kernel(place_ref, *refs):
        ins, outs = refs[: len(pieces)], refs[len(pieces) :]
        for at in range(total):
            start = 0
            for out, size in zip(outs, widths):
                out[place_ref[at]] = ins[at // count][at % count, :, start : start + size]
                start += size

    shapes = [(total, rows, size) for size in widths]
    placed = pl.pallas_call(
        kernel,
        out_shape=[jax.ShapeDtypeStruct(shape, pieces[0].dtype) for shape in shapes],
        grid_spec=pltpu.PrefetchScalarGridSpec(
            num_scalar_prefetch=1,
            grid=(1,),
            in_specs=[pl.BlockSpec((count, rows, width), lambda i, *_: (0, 0, 0))] * len(pieces),
            out_specs=[pl.BlockSpec(shape, lambda i, *_: (0, 0, 0)) for shape in shapes],
        ),
        compiler_params=pltpu.CompilerParams(vmem_limit_bytes=48 * 2**20),
        cost_estimate=pl.CostEstimate(
            flops=0, bytes_accessed=4 * total * rows * width, transcendentals=0
        ),
        name="place_blocks",
    )(places, *pieces)
    return [out.reshape(total * rows, -1) for out in placed]


def normalize(values, gain_vec):
    factor = lax.rsqrt(jnp.mean(values * values, axis=-1, keepdims=True) + EPSILON)
    plain_rows = values * factor
    return (plain_rows, factor, plain_rows * gain_vec)


def norm_backward(grad_normed, plain_rows, factor, gain_vec):
    scaled = grad_normed * gain_vec
    gain_part = jnp.sum(grad_normed * plain_rows, axis=0)
    grad_input = factor * (
        scaled - plain_rows * jnp.mean(scaled * plain_rows, axis=-1, keepdims=True)
    )
    return (gain_part, grad_input)


def matmul(left_side, right_side):
    return jnp.dot(left_side, right_side, preferred_element_type=HIGH)


def matmul_right_t(left_side, right_side):
    return lax.dot_general(
        left_side, right_side, (((1,), (1,)), ((), ())), preferred_element_type=HIGH
    )


def matmul_left_t(left_side, right_side):
    return lax.dot_general(
        left_side, right_side, (((0,), (0,)), ((), ())), preferred_element_type=HIGH
    )


def pad_units(rows):
    extra = -rows.shape[0] % 16
    return jnp.pad(rows, ((0, extra), (0, 0)))


def quarters(count):
    tiles = count // 16
    return [16 * (tiles * i // 4) for i in range(5)]


def diagonal_visible(core, span_rows, key_axis):
    half = span_rows // 2

    def place(axis):
        index = lax.broadcasted_iota(jnp.int32, (span_rows, span_rows), axis)
        flipped = jnp.where(index < half, index + half, index - half)
        return jnp.where(core == 0, index, flipped)

    return place(key_axis) <= place(1 - key_axis)


def in_runs(count, step, carry):
    done = 0
    for run in RUNS:
        stop = count // run * run
        first = done

        def body(at, carry, run=run, first=first):
            return step(first + run * at, carry, run)

        carry = lax.fori_loop(0, (stop - done) // run, body, carry)
        done = stop
    return carry


def forward_kernel(
    place_ref, rank_ref, core_ref, query_ref, key_ref, value_ref, mixed_ref, lse_ref, score_ref
):
    half_rows = query_ref.shape[1]
    span_rows = 2 * half_rows
    heads = query_ref.shape[2] // HD
    rank = rank_ref[pl.program_id(1)]
    columns = [slice(h * HD, (h + 1) * HD) for h in range(heads)]

    def span(ref, step, h):
        side = place_ref[step] // 4
        start = pl.multiple_of((place_ref[step] % 4) * half_rows, half_rows)
        return ref[side, :, pl.ds(start, half_rows), columns[h]].reshape(span_rows, HD)

    def block_scores(step, h):
        query = query_ref[:, :, columns[h]].reshape(span_rows, HD)
        return matmul_right_t(query, span(key_ref, step, h)) * (SCORE_SCALE * LOG2E)

    def fold(values, operation):
        folded = values[:, :HD]
        for at in range(HD, span_rows, HD):
            folded = operation(folded, values[:, at : at + HD])
        return folded

    def score_step(step, maxima, count):
        new = []
        for h in range(heads):
            top = maxima[h]
            for at in range(count):
                scores = block_scores(step + at, h)
                score_ref[h, step + at] = scores
                top = jnp.maximum(top, fold(scores, jnp.maximum))
            new.append(top)
        return tuple(new)

    maxima = tuple(jnp.full((span_rows, HD), -jnp.inf, HIGH) for _ in range(heads))
    maxima = in_runs(rank, score_step, maxima)
    visible = diagonal_visible(core_ref[0], span_rows, 1)
    tops = []
    for h in range(heads):
        scores = jnp.where(visible, block_scores(rank, h), -jnp.inf)
        score_ref[h, rank] = scores
        top = jnp.maximum(maxima[h], fold(scores, jnp.maximum))
        tops.append(jnp.max(top, axis=1, keepdims=True))

    def mix_step(step, running, count):
        new = []
        for h in range(heads):
            total, mixed = running[h]
            for at in range(count):
                weights = jnp.exp2(score_ref[h, step + at] - tops[h])
                total = total + fold(weights, jnp.add)
                mixed = mixed + matmul(weights.astype(LOW), span(value_ref, step + at, h))
            new.append((total, mixed))
        return tuple(new)

    zero = jnp.zeros((span_rows, HD), HIGH)
    sums = tuple((zero, zero) for _ in range(heads))
    blocks = rank + 1
    sums = in_runs(blocks, mix_step, sums)
    for h in range(heads):
        total = jnp.sum(sums[h][0], axis=1, keepdims=True)
        mixed = (sums[h][1] / total).astype(LOW)
        mixed_ref[:, :, columns[h]] = mixed.reshape(2, half_rows, HD)
        lse = jnp.broadcast_to(tops[h] + jnp.log2(total), (span_rows, HD))
        lse_ref[h] = jnp.transpose(lse)[:8, :]


def backward_kernel(
    place_ref,
    rank_ref,
    core_ref,
    query_ref,
    mixed_ref,
    lse_ref,
    key_ref,
    value_ref,
    weight_ref,
    *refs,
):
    *branch_refs, grad_query_ref, grad_key_ref, grad_value_ref = refs[:-4]
    grad_ref, turned_ref, key_sum_ref, value_sum_ref = refs[-4:]
    heads = query_ref.shape[2] // HD
    half_rows = query_ref.shape[1] // rank_ref.shape[0]
    span_rows = 2 * half_rows
    columns = [slice(h * HD, (h + 1) * HD) for h in range(heads)]
    count = len(branch_refs) // 2
    for core in range(2):
        rows = [ref[...] for ref in branch_refs[core * count : (core + 1) * count]]
        rows = jnp.concatenate(rows, axis=0)
        grad_ref[core] = matmul_right_t(rows, weight_ref[...]).astype(LOW)
    for h in range(heads):
        for at in range(turned_ref.shape[1]):
            rows = slice(at % 4 * half_rows, (at % 4 + 1) * half_rows)
            keys = key_ref[at // 4, :, rows, columns[h]].reshape(span_rows, HD)
            turned_ref[h, at] = jnp.transpose(keys)
    key_sum_ref[...] = jnp.zeros_like(key_sum_ref)
    value_sum_ref[...] = jnp.zeros_like(value_sum_ref)

    def query_span(at, carry):
        here = pl.ds(pl.multiple_of(at * half_rows, half_rows), half_rows)
        lanes = pl.ds(pl.multiple_of(at * span_rows, span_rows), span_rows)
        rank = rank_ref[at]

        def own(ref, h):
            return ref[:, here, columns[h]].reshape(span_rows, HD)

        delta = []
        lse = []
        for h in range(heads):
            product = own(grad_ref, h).astype(HIGH) * own(mixed_ref, h).astype(HIGH)
            delta.append(jnp.sum(jnp.transpose(product), axis=0, keepdims=True))
            lse.append(lse_ref[h, :1, lanes])

        def block(step, grad_query, visible):
            side = place_ref[step] // 4
            start = pl.multiple_of((place_ref[step] % 4) * half_rows, half_rows)
            there = pl.ds(start, half_rows)
            new = []
            for h in range(heads):
                query = own(query_ref, h)
                grad = own(grad_ref, h)
                keys = key_ref[side, :, there, columns[h]].reshape(span_rows, HD)
                values = value_ref[side, :, there, columns[h]].reshape(span_rows, HD)
                scores = matmul_right_t(keys, query) * (SCORE_SCALE * LOG2E)
                weights = jnp.exp2(scores - lse[h])
                if visible is not None:
                    weights = jnp.where(visible, weights, 0.0)
                grad_weights = matmul_right_t(values, grad)
                grad_scores = (weights * (grad_weights - delta[h])).astype(LOW)
                value_term = matmul(weights.astype(LOW), grad)
                key_term = matmul(grad_scores, query)
                value_sum_ref[side, :, there, columns[h]] += value_term.reshape(2, half_rows, HD)
                key_sum_ref[side, :, there, columns[h]] += key_term.reshape(2, half_rows, HD)
                new.append(grad_query[h] + matmul(turned_ref[h, place_ref[step]], grad_scores))
            return tuple(new)

        start = tuple(jnp.zeros((HD, span_rows), HIGH) for _ in range(heads))
        def blocks(first, grad_query, count):
            for more in range(count):
                grad_query = block(first + more, grad_query, None)
            return grad_query

        grad_query = in_runs(rank, blocks, start)
        visible = diagonal_visible(core_ref[0], span_rows, 0)
        grad_query = block(rank, grad_query, visible)
        for h in range(heads):
            result = (jnp.transpose(grad_query[h]) * SCORE_SCALE).astype(LOW)
            grad_query_ref[:, here, columns[h]] = result.reshape(2, half_rows, HD)
        return carry

    lax.fori_loop(0, rank_ref.shape[0], query_span, 0)
    grad_key_ref[...] = (key_sum_ref[...] * SCORE_SCALE).astype(LOW)
    grad_value_ref[...] = value_sum_ref[...].astype(LOW)


def heads_at_once(key_rows, features):
    return features // HD if key_rows <= 4096 else 1


def attention_forward(scalars, queries, keys, values):
    rows, features = queries.shape
    key_rows = keys.shape[0]
    own_spans = scalars[1].shape[0]
    half_rows = rows // own_spans // 2
    span_rows = 2 * half_rows
    heads = heads_at_once(key_rows, features)
    width = heads * HD
    pairs = rows * key_rows * features
    sides = key_rows // rows
    own = pl.BlockSpec((2, half_rows, width), lambda h, i, *_: (0, i, h))
    other = pl.BlockSpec((sides, 2, rows // 2, width), lambda h, i, *_: (0, 0, 0, h))
    mixed, lse = pl.pallas_call(
        forward_kernel,
        out_shape=(
            jax.ShapeDtypeStruct((2, rows // 2, features), LOW),
            jax.ShapeDtypeStruct((features // HD, 8, rows), HIGH),
        ),
        grid_spec=pltpu.PrefetchScalarGridSpec(
            num_scalar_prefetch=3,
            grid=(features // width, own_spans),
            in_specs=[own, other, other],
            out_specs=[own, pl.BlockSpec((heads, 8, span_rows), lambda h, i, *_: (h, 0, i))],
            scratch_shapes=[
                pltpu.VMEM((heads, key_rows // span_rows, span_rows, span_rows), HIGH)
            ],
        ),
        compiler_params=pltpu.CompilerParams(vmem_limit_bytes=56 * 2**20),
        cost_estimate=pl.CostEstimate(
            flops=20 * pairs, bytes_accessed=4 * key_rows * features, transcendentals=pairs // 256
        ),
        name="attention_forward",
    )(
        *scalars,
        queries.reshape(2, rows // 2, features),
        keys.reshape(sides, 2, rows // 2, features),
        values.reshape(sides, 2, rows // 2, features),
    )
    return mixed.reshape(rows, features), lse


def attention_backward(scalars, queries, mixed, lse, keys, values, weight_out, branch_blocks):
    rows, features = queries.shape
    key_rows = keys.shape[0]
    heads = heads_at_once(key_rows, features)
    width = heads * HD
    pairs = rows * key_rows * features
    sides = key_rows // rows
    own_shape = (2, rows // 2, features)
    key_shape = (sides, 2, rows // 2, features)
    once = pl.Buffered(1)
    own_part, key_part = own_shape[:2] + (width,), key_shape[:3] + (width,)
    own = pl.BlockSpec(own_part, lambda h, *_: (0, 0, h))
    other = pl.BlockSpec(key_part, lambda h, *_: (0, 0, 0, h))
    other_in = pl.BlockSpec(key_part, lambda h, *_: (0, 0, 0, h), pipeline_mode=once)
    block = pl.BlockSpec(branch_blocks[0].shape, lambda h, *_: (0, 0), pipeline_mode=once)
    grad_queries, grad_keys, grad_values = pl.pallas_call(
        backward_kernel,
        out_shape=(
            jax.ShapeDtypeStruct(own_shape, LOW),
            jax.ShapeDtypeStruct(key_shape, LOW),
            jax.ShapeDtypeStruct(key_shape, LOW),
        ),
        grid_spec=pltpu.PrefetchScalarGridSpec(
            num_scalar_prefetch=3,
            grid=(features // width,),
            in_specs=[
                own,
                own,
                pl.BlockSpec((heads, 8, rows), lambda h, *_: (h, 0, 0)),
                other_in,
                other_in,
                pl.BlockSpec((width, weight_out.shape[1]), lambda h, *_: (h, 0)),
            ]
            + [block] * len(branch_blocks),
            out_specs=[own, other, other],
            scratch_shapes=[
                pltpu.VMEM(own_part, LOW),
                pltpu.VMEM((heads, 4 * sides, HD, key_rows // (4 * sides)), LOW),
            ]
            + [pltpu.VMEM(key_part, HIGH)] * 2,
        ),
        compiler_params=pltpu.CompilerParams(vmem_limit_bytes=56 * 2**20),
        cost_estimate=pl.CostEstimate(
            flops=120 * pairs, bytes_accessed=8 * key_rows * features, transcendentals=pairs // 256
        ),
        name="attention_backward",
    )(
        *scalars,
        queries.reshape(own_shape),
        mixed.reshape(own_shape),
        lse,
        keys.reshape(key_shape),
        values.reshape(key_shape),
        weight_out,
        *branch_blocks,
    )
    return (
        grad_queries.reshape(rows, features),
        grad_keys.reshape(key_rows, features),
        grad_values.reshape(key_rows, features),
    )


def per_device(
    states,
    shared_kv,
    norm_gain,
    kv_gain,
    ffn_gain,
    query_weight,
    key_weight,
    value_weight,
    out_weight,
    gate_weight,
    up_weight,
    down_weight,
    span_order,
    grad_output,
):
    z, x, y, c = (lax.axis_index(name) for name in ALL)
    size_x = lax.axis_size("x")
    sides = 2 * size_x
    rows_local, width_model = states.shape
    weight_rows = query_weight.shape[0]
    units_local = gate_weight.shape[1]
    own_width = width_model // 8

    side = jnp.arange(sides, dtype=jnp.int32)
    side_owner = jnp.mod(x - side // 2, size_x) * 2 + jnp.bitwise_xor(y, side % 2)
    back = jnp.mod(jnp.arange(4, dtype=jnp.int32) + 1, 4)
    back_owner = jnp.mod(z - back, 4)

    ticks = Ticks()

    block = jnp.arange(8 * sides, dtype=jnp.int32)
    block_half, block_side = block // (4 * sides), block // 4 % sides
    block_back = 2 * block_half + block // 2 % 2
    block_place = (
        (jnp.mod(z - block_back, 4) * size_x + jnp.mod(x - block_side // 2, size_x)) * 2
        + jnp.bitwise_xor(y, block_side % 2)
    ) * 2 + jnp.bitwise_xor(c, block % 2)

    state_rows = states.astype(HIGH)
    shared_rows = shared_kv.astype(HIGH)
    plain_kv, factor_kv, normed_kv = normalize(shared_rows, kv_gain)
    plain_one, factor_one, normed_one = normalize(state_rows, norm_gain)
    shared_low = normed_kv.astype(LOW)
    normed_low = normed_one.astype(LOW)

    with jax.named_scope("weight_columns"):
        pair = 2 * own_width
        projections = (key_weight, value_weight, query_weight)

        def cut(start, size, arrays):
            return jnp.concatenate(
                [lax.dynamic_slice_in_dim(v, start, size, 1) for v in arrays], axis=1
            )

        parts = [cut(jnp.mod(z + step, 4) * pair, pair, projections) for step in range(4)]
        over = ticks.tick((parts[1], 1), (parts[2], 2), (parts[3], 3), lock=False)
        columns = []
        for part in [parts[0]] + over:
            arrays = [part[:, i * pair : (i + 1) * pair] for i in range(3)]
            columns.append(cut(c * own_width, own_width, arrays))
            columns.append(hop(cut((1 - c) * own_width, own_width, arrays), "c"))
        columns = jnp.stack(columns)
    with jax.named_scope("shared_rows"):
        out_weight = after(out_weight, over)
        out_task = ticks.add(
            gather_task(out_weight[: weight_rows // 2], out_weight[weight_rows // 2 :]),
            urgent=True,
        )
        weight_task = ticks.add(gather_task(columns[:4], columns[4:]), urgent=True)
        shared_blocks = [shared_low]
        for _ in range(3):
            shared_blocks += ticks.tick((shared_blocks[-1], 1), room=1.2, lock=False)
        group_shared = ticks.join_cores(shared_blocks)
    with jax.named_scope("weight_columns"):
        first, second = ticks.finish(weight_task)[0]
        weight_kv, weight_query = place_blocks(
            first + second, block_place, (2 * own_width, own_width)
        )
    with jax.named_scope("out_weight"):
        whole = jnp.arange(sides, dtype=jnp.int32)
        whole_side = jnp.mod(x - whole // 2, size_x) * 2 + jnp.bitwise_xor(y, whole % 2)
        out_pieces = ticks.finish(out_task)[0]
        out_pieces = jnp.stack([part for pair in zip(*out_pieces) for part in pair])
        out_pieces = jnp.take(
            out_pieces.reshape(sides, weight_rows, width_model), whole_side, axis=0
        ).reshape(2, size_x // 2, 2, weight_rows, width_model)
        out_keep = lax.dynamic_index_in_dim(out_pieces, c, 0, keepdims=False)
        out_give = lax.dynamic_index_in_dim(out_pieces, 1 - c, 0, keepdims=False)
        out_got = hop(out_give, "c")
        weight_out = jnp.where(
            c == 0, jnp.stack([out_keep, out_got], axis=2), jnp.stack([out_got, out_keep], axis=2)
        ).reshape(own_width, width_model)

    with jax.named_scope("keys_values"):
        group_shared = after(group_shared, weight_out)
        keys_own = matmul(group_shared, weight_kv[:, :own_width]).astype(LOW)
        values_own = matmul(group_shared, weight_kv[:, own_width:]).astype(LOW)
        keys_task = ticks.add(gather_task(keys_own, values_own), urgent=True)
    with jax.named_scope("normed_rows"):
        normed_blocks = [normed_low]
        for _ in range(3):
            normed_blocks += ticks.tick((normed_blocks[-1], 1), lock=False)
    with jax.named_scope("normed_rows"):
        group_normed = ticks.join_cores(normed_blocks)
    with jax.named_scope("grad_output_rows"):
        grad_blocks = [grad_output] + ticks.tick((grad_output, 1))
    with jax.named_scope("keys_values"):
        key_pieces, value_pieces = ticks.finish(keys_task)[0]
        keys_all, values_all = jnp.concatenate(key_pieces), jnp.concatenate(value_pieces)
    with jax.named_scope("queries"):
        late_normed = after(group_normed, key_pieces[-1], value_pieces[-1])
        queries = matmul(late_normed, weight_query).astype(LOW)

    span_of = (back_owner[None, :] * sides + side_owner[:, None]).reshape(-1)
    ranks = jnp.take(span_order, span_of)
    spans = span_order.shape[0]
    listed = jnp.arange(spans, dtype=jnp.int32)
    place = jnp.sum(jnp.where(ranks[None, :] == listed[:, None], listed[None, :], 0), axis=1)
    scalars = (place, ranks[:4], c.reshape(1).astype(jnp.int32))

    with jax.named_scope("unit_weights"):
        late = (keys_all, values_all)
        unit_rows = jnp.concatenate(
            [
                pad_units(jnp.transpose(after(gate_weight, *late))),
                pad_units(jnp.transpose(after(up_weight, *late))),
                pad_units(after(down_weight, *late)),
            ],
            axis=0,
        )
        cuts = quarters(unit_rows.shape[0])
        chunks = [unit_rows[cuts[i] : cuts[i + 1]] for i in range(4)]
        unit_tasks = [ticks.add(gather_task(chunks[i], chunks[i + 1])) for i in (0, 2)]
    with jax.named_scope("grad_output_rows"):
        grad_blocks += ticks.tick((grad_blocks[-1], 1), (grad_output, -1))
    mixed, lse = attention_forward(scalars, queries, keys_all, values_all)
    with jax.named_scope("attention_sum"):
        attention_sum = RowSum(ticks, lambda v: matmul(v, weight_out), [mixed], rows_local)
        residual = state_rows + attention_sum.finish()
    with jax.named_scope("grad_output_rows"):
        group_grad = ticks.join_cores(list(after(tuple(grad_blocks), attention_sum.sent)))
    plain_two, factor_two, normed_two = normalize(residual, ffn_gain)
    with jax.named_scope("normed_two_rows"):
        group_in = ticks.gather_rows(normed_two.astype(LOW))
    with jax.named_scope("unit_weights"):
        gathered = [pieces for result in ticks.finish(*unit_tasks) for pieces in result]
        units_padded = unit_rows.shape[0] // 3

        def units_of(which):
            low, high = which * units_padded, (which + 1) * units_padded
            rows = []
            for s in range(sides):
                for i in range(4):
                    start, stop = max(low, cuts[i]), min(high, cuts[i + 1])
                    if start < stop:
                        rows.append(gathered[i][s][start - cuts[i] : stop - cuts[i]])
            return jnp.concatenate(rows, axis=0)

        weight_gate, weight_up, weight_down = (units_of(which) for which in range(3))

    gate_act = matmul_right_t(group_in, weight_gate)
    up_act = matmul_right_t(group_in, weight_up)
    grad_hidden = matmul_right_t(group_grad, weight_down)
    sigmoid = jax.nn.sigmoid(gate_act)
    silu_act = gate_act * sigmoid
    hidden = (silu_act * up_act).astype(LOW)
    grad_gate_act = (
        grad_hidden * up_act * sigmoid * (1.0 + gate_act * (1.0 - sigmoid))
    ).astype(LOW)
    grad_up_act = (grad_hidden * silu_act).astype(LOW)

    def unit_parts(values):
        step = values.shape[0] // sides
        return [values[s * step : (s + 1) * step] for s in range(sides)]

    with jax.named_scope("ffn_grad_sum"):
        ffn_grad_sum = RowSum(
            ticks,
            lambda g, u: matmul(g, weight_gate) + matmul(u, weight_up),
            [grad_gate_act, grad_up_act],
            rows_local,
        )
        unit_terms = []

        def unit_window(left, right, room=1):
            ffn_grad_sum.step(room)
            terms = matmul_left_t(after(left, ffn_grad_sum.sent), right).astype(LOW)
            unit_terms.append(unit_parts(terms))

        def chunk_parts(i):
            parts = []
            for s in range(sides):
                rows = []
                for which in range(3):
                    low = which * units_padded
                    start, stop = max(low, cuts[i]), min(low + units_padded, cuts[i + 1])
                    if start < stop:
                        rows.append(unit_terms[which][s][start - low : stop - low])
                parts.append(jnp.concatenate(rows, axis=0) if rows[1:] else rows[0])
            return parts

        unit_window(grad_gate_act, group_in)
        unit_window(grad_up_act, group_in)
        unit_sum_tasks = [ticks.add(sum_task(chunk_parts(0), chunk_parts(1)))]
        unit_window(hidden, group_grad)
        unit_sum_tasks.append(ticks.add(sum_task(chunk_parts(2), chunk_parts(3))))
        grad_ffn = ffn_grad_sum.finish()

    gain_two, grad_norm_two = norm_backward(grad_ffn, plain_two, factor_two, ffn_gain)
    grad_residual = grad_output.astype(HIGH) + grad_norm_two
    with jax.named_scope("branch_rows"):
        branch_moves = ticks.gather_parts(grad_residual.astype(LOW))
        sent = next(branch_moves)
        lined = jnp.arange(8, dtype=jnp.int32)
        order = jnp.bitwise_xor(c, lined % 2) * 4 + jnp.mod(z - lined // 2 - 1, 4)
        late_hidden = after(hidden, sent).reshape(8, rows_local, -1)
        late_hidden = jnp.take(late_hidden, order, axis=0).reshape(8 * rows_local, -1)
        terms = matmul(after(late_hidden, next(branch_moves)), weight_down).astype(LOW)
        next(branch_moves)
        branch_both = next(branch_moves)
    with jax.named_scope("ffn_sum"):
        branch = lax.psum_scatter(
            after(terms, ticks.over_z), ("z", "c"), scatter_dimension=0, tiled=True
        )
        output = (residual + branch.astype(HIGH)).astype(LOW)
    with jax.named_scope("unit_weight_sums"):
        ticks.tick(room=2, lock=False)
    grad_queries, key_terms, value_terms = attention_backward(
        scalars, queries, mixed, lse, keys_all, values_all, weight_out, branch_both
    )

    def side_parts(values, k):
        count = values.shape[0] // (2 * sides)
        return [
            lax.dynamic_slice_in_dim(
                values,
                (2 * jnp.bitwise_xor(jnp.bitwise_xor(side_owner[s], z), 2 * k) + k) * count,
                count,
                0,
            )
            for s in range(sides)
        ]

    def chunk_sums(values):
        return sum_joined_task(side_parts(values, 0), side_parts(values, 1))

    to_layout = [
        [
            (
                ((za * size_x + xa) * 2 + ya) * 2 + ca,
                (2 * ((2 * xa + ya) ^ za ^ (2 * (ca ^ flip))) + (ca ^ flip)) * 4 + za,
            )
            for za in range(4)
            for xa in range(size_x)
            for ya in range(2)
            for ca in range(2)
        ]
        for flip in range(2)
    ]

    def layout(summed):
        sent = jnp.where(c == 0, summed[0], summed[1]), jnp.where(c == 0, summed[1], summed[0])
        got = [lax.ppermute(sent[flip], ALL, to_layout[flip]) for flip in range(2)]
        even = x % 2 == 0
        first = jnp.where(even, got[0], got[1]).astype(HIGH)
        second = jnp.where(even, got[1], got[0]).astype(HIGH)
        return [
            jnp.concatenate([part[:, at : at + own_width] for part in (first, second)], axis=1)
            for at in range(0, first.shape[1], own_width)
        ]

    with jax.named_scope("grad_keys_values"):
        keys_task = ticks.add(
            sum_joined_task(unit_parts(key_terms), unit_parts(value_terms)), urgent=True
        )
    with jax.named_scope("normed_sum"):
        normed_sum = RowSum(
            ticks, lambda v: matmul_right_t(v, weight_query), [grad_queries], rows_local
        )
        normed_sum.step()
        sent = normed_sum.sent
    with jax.named_scope("query_weight_sum"):
        query_terms = matmul_left_t(after(group_normed, sent), grad_queries).astype(LOW)
    with jax.named_scope("normed_sum"):
        normed_sum.step()
        sent = normed_sum.sent
    with jax.named_scope("out_weight_sum"):
        group_branch = jnp.concatenate(after(branch_both, sent), axis=0)
        out_terms = matmul_left_t(group_branch, mixed).astype(LOW)
    with jax.named_scope("normed_sum"):
        grad_normed = normed_sum.finish()
    with jax.named_scope("grad_keys_values"):
        grad_keys, grad_values = ticks.finish(keys_task)[0]
    with jax.named_scope("query_out_weight_sum"):
        query_out_task = ticks.add(
            chunk_sums(jnp.concatenate([query_terms, out_terms], axis=1))
        )
    with jax.named_scope("shared_sum"):
        weight_key, weight_value = weight_kv[:, :own_width], weight_kv[:, own_width:]
        shared_sum = RowSum(
            ticks,
            lambda k, v: matmul_right_t(k, weight_key) + matmul_right_t(v, weight_value),
            [grad_keys, grad_values],
            rows_local,
        )
        shared_sum.total = after(shared_sum.total, branch)
        shared_sum.step()
        sent = shared_sum.sent
    with jax.named_scope("key_value_weight_sum"):
        grad_kv = jnp.concatenate(after((grad_keys, grad_values), sent), axis=1)
        kv_terms = matmul_left_t(group_shared, grad_kv).astype(LOW)
        kv_task = ticks.add(chunk_sums(kv_terms))
    with jax.named_scope("shared_sum"):
        grad_shared_normed = shared_sum.finish()
    with jax.named_scope("weight_layout"):
        (query_out_sum,) = ticks.finish(query_out_task)
        grad_query, grad_out = layout(after(query_out_sum, grad_shared_normed))
        (kv_sum,) = ticks.finish(kv_task)
        grad_key, grad_value = layout(kv_sum)
        grad_out = jnp.transpose(grad_out)
    with jax.named_scope("unit_weight_sums"):
        sums = [part for result in ticks.finish(*unit_sum_tasks) for part in result]
        whole = jnp.concatenate(sums, axis=0).astype(HIGH)
        grad_gate, grad_up, grad_down = (
            whole[w * units_padded : w * units_padded + units_local] for w in range(3)
        )
        grad_gate, grad_up = jnp.transpose(grad_gate), jnp.transpose(grad_up)

    grad_normed = after(grad_normed, sent)
    gain_one, grad_in_one = norm_backward(grad_normed, plain_one, factor_one, norm_gain)
    gain_kv, grad_in_kv = norm_backward(grad_shared_normed, plain_kv, factor_kv, kv_gain)
    grad_states = (grad_residual + grad_in_one).astype(LOW)
    grad_shared = grad_in_kv.astype(LOW)

    devices = 8 * sides
    gain_terms = jnp.stack([g.reshape(devices, -1) for g in (gain_one, gain_kv, gain_two)], axis=1)
    gain_terms = lax.all_to_all(
        gain_terms.reshape(devices, -1), ALL, split_axis=0, concat_axis=0, tiled=True
    )
    gain_sums = jnp.sum(gain_terms, axis=0).reshape(3, -1)
    return (
        output,
        grad_states,
        grad_shared,
        gain_sums[0],
        gain_sums[1],
        gain_sums[2],
        grad_query,
        grad_key,
        grad_value,
        grad_out,
        grad_gate,
        grad_up,
        grad_down,
    )


def solution(mesh):
    size_ctx, size_head = mesh.shape["ctx"], mesh.shape["head"]
    fine = Mesh(mesh.devices.reshape(4, size_ctx // 4, 2, size_head // 2), ALL)
    rows = P(ALL, None)
    ctx, head = ("z", "x"), ("y", "c")
    in_specs = (
        rows,
        rows,
        P(),
        P(),
        P(),
        rows,
        rows,
        rows,
        rows,
        P(None, ALL),
        P(None, ALL),
        rows,
        P(),
        rows,
    )
    out_specs = (
        rows,
        rows,
        rows,
        P(ALL),
        P(ALL),
        P(ALL),
        P(ctx, head),
        P(ctx, head),
        P(ctx, head),
        P(head, ctx),
        P(None, ALL),
        P(None, ALL),
        rows,
    )
    return jax.shard_map(
        per_device, mesh=fine, in_specs=in_specs, out_specs=out_specs, check_vma=False
    )
```
